32 devices in a mesh: dp: 4 (over y, core), rows: 4 (over z), cols: 2 (over x).
Axes of the slice: x: 2, y: 2, z: 4, core: 2. Of those that a mesh axis runs over, the one named last changes fastest.
Arguments:
- image_in: bfloat16 [8, 64, 64, 1280], P('dp', 'rows', 'cols'), may hold values from -6 to 6
- ln1_gain: bfloat16 [1280], P(('dp', 'rows', 'cols')), may hold values from 0.5 to 1.5
- ln1_bias: bfloat16 [1280], P(('dp', 'rows', 'cols')), may hold values from -1.1953125 to 1.1953125
- w_qkv: bfloat16 [1280, 3840], P(('dp', 'rows', 'cols')), may hold values from -0.15625 to 0.15625
- qv_bias: bfloat16 [1280, 2], P(('dp', 'rows', 'cols')), may hold values from -1.1953125 to 1.1953125
- rel_rows: bfloat16 [27, 80], replicated, may hold values from -0.59765625 to 0.59765625
- rel_cols: bfloat16 [27, 80], replicated, may hold values from -0.59765625 to 0.59765625
- w_proj: bfloat16 [1280, 1280], P(('dp', 'rows', 'cols')), may hold values from -0.625 to 0.625
- proj_bias: bfloat16 [1280], P(('dp', 'rows', 'cols')), may hold values from -1.1953125 to 1.1953125
- ln2_gain: bfloat16 [1280], P(('dp', 'rows', 'cols')), may hold values from 0.5 to 1.5
- ln2_bias: bfloat16 [1280], P(('dp', 'rows', 'cols')), may hold values from -1.1953125 to 1.1953125
- w_fc1: bfloat16 [1280, 5120], P(('dp', 'rows', 'cols')), may hold values from -0.15625 to 0.15625
- fc1_bias: bfloat16 [5120], P(('dp', 'rows', 'cols')), may hold values from -1.1953125 to 1.1953125
- w_fc2: bfloat16 [5120, 1280], P(('dp', 'rows', 'cols')), may hold values from -0.078125 to 0.078125
- fc2_bias: bfloat16 [1280], P(('dp', 'rows', 'cols')), may hold values from -1.1953125 to 1.1953125
- cotangent: bfloat16 [8, 64, 64, 1280], P('dp', 'rows', 'cols'), may hold values from -6 to 6
Outputs:
- block_out: bfloat16 [8, 64, 64, 1280], P('dp', 'rows', 'cols')
- grad_in: float32 [8, 64, 64, 1280], P('dp', 'rows', 'cols')
- grad_ln1_gain: float32 [1280], P(('dp', 'rows', 'cols'))
- grad_ln1_bias: float32 [1280], P(('dp', 'rows', 'cols'))
- grad_w_qkv: float32 [1280, 3840], P(('dp', 'rows', 'cols'))
- grad_qv_bias: float32 [1280, 2], P(('dp', 'rows', 'cols'))
- grad_rel_rows: float32 [27, 80], replicated
- grad_rel_cols: float32 [27, 80], replicated
- grad_w_proj: float32 [1280, 1280], P(('dp', 'rows', 'cols'))
- grad_proj_bias: float32 [1280], P(('dp', 'rows', 'cols'))
- grad_ln2_gain: float32 [1280], P(('dp', 'rows', 'cols'))
- grad_ln2_bias: float32 [1280], P(('dp', 'rows', 'cols'))
- grad_w_fc1: float32 [1280, 5120], P(('dp', 'rows', 'cols'))
- grad_fc1_bias: float32 [5120], P(('dp', 'rows', 'cols'))
- grad_w_fc2: float32 [5120, 1280], P(('dp', 'rows', 'cols'))
- grad_fc2_bias: float32 [1280], P(('dp', 'rows', 'cols'))
The draws below stay inside these ranges and needn't reach their ends.
All inputs are finite; a program needn't handle non-finite values.
Results may differ from the reference program's by a relative error of at most 0.013.
Values may be sent and summed in bfloat16 or wider, within the bound.
No kernel may reach another device: no remote copies, remote signals or barrier semaphores. Data moves between devices by JAX's collectives and lax.ppermute only.
A program may use at most 488 MiB of HBM per device.

```python
import jax
import jax.numpy as jnp
from jax import lax

D = 1280
HEADS = 16
HD = 80
FF = 5120
IMG = 64
WIN = 14
IMAGES = 8
NWIN = 5
REL = 27


def levels(stream_key, shape, pieces, smallest, top_value):
    level = 1.0
    for position, shards_of in pieces:
        heights = jax.random.uniform(jax.random.fold_in(jax.random.fold_in(stream_key, 6), position), (shards_of,), jnp.float32, smallest / len(pieces), top_value / len(pieces))
        level = level * jnp.repeat(jnp.exp(heights), shape[position] // shards_of).reshape((-1,) + (1,) * (len(shape) - 1 - position))
    return level


def bell_draw(key, extent, spread, bound, split=(), kind=jnp.bfloat16):
    array = spread * jax.random.normal(key, extent, jnp.float32)
    if split:
        array = array * levels(key, extent, split, -0.22, 0.18)
    return jnp.clip(array, -bound, bound).astype(kind)


def setup_inputs(seed: int = 0) -> dict:
    arg_keys = jax.random.split(jax.random.key(seed), 17)
    image_in = bell_draw(arg_keys[0], (IMAGES, IMG, IMG, D), 1.0, 6.0, ((0, 4), (1, 4), (2, 2)))
    ln1_gain = jnp.clip(1.0 + 0.1 * jax.random.normal(arg_keys[1], (D,), jnp.float32), 0.5, 1.5).astype(jnp.bfloat16)
    ln1_bias = bell_draw(arg_keys[2], (D,), 0.2, 1.1953125, ((0, 32),))
    w_qkv = bell_draw(arg_keys[3], (D, 3 * D), D ** -0.5, 0.15625, ((0, 32),))
    qv_bias = bell_draw(arg_keys[4], (D, 2), 0.2, 1.1953125, ((0, 32),))
    rel_rows = bell_draw(arg_keys[5], (REL, HD), 0.1, 0.59765625)
    rel_cols = bell_draw(arg_keys[6], (REL, HD), 0.1, 0.59765625)
    w_proj = bell_draw(arg_keys[7], (D, D), (D // 16) ** -0.5, 0.625, ((0, 32),))
    proj_bias = bell_draw(arg_keys[8], (D,), 0.2, 1.1953125, ((0, 32),))
    ln2_gain = jnp.clip(1.0 + 0.1 * jax.random.normal(arg_keys[9], (D,), jnp.float32), 0.5, 1.5).astype(jnp.bfloat16)
    ln2_bias = bell_draw(arg_keys[10], (D,), 0.2, 1.1953125, ((0, 32),))
    w_fc1 = bell_draw(arg_keys[11], (D, FF), D ** -0.5, 0.15625, ((0, 32),))
    fc1_bias = bell_draw(arg_keys[12], (FF,), 0.2, 1.1953125, ((0, 32),))
    w_fc2 = bell_draw(arg_keys[13], (FF, D), FF ** -0.5, 0.078125, ((0, 32),))
    fc2_bias = bell_draw(arg_keys[14], (D,), 0.2, 1.1953125, ((0, 32),))
    cotangent = bell_draw(arg_keys[15], (IMAGES, IMG, IMG, D), 1.0, 6.0, ((0, 4), (1, 4), (2, 2)))
    return dict(image_in=image_in, ln1_gain=ln1_gain, ln1_bias=ln1_bias, w_qkv=w_qkv, qv_bias=qv_bias, rel_rows=rel_rows, rel_cols=rel_cols, w_proj=w_proj, proj_bias=proj_bias, ln2_gain=ln2_gain, ln2_bias=ln2_bias, w_fc1=w_fc1, fc1_bias=fc1_bias, w_fc2=w_fc2, fc2_bias=fc2_bias, cotangent=cotangent)


@jax.custom_vjp
def low(v):
    return lax.optimization_barrier(v.astype(jnp.bfloat16)).astype(jnp.float32)

@jax.custom_vjp
def low_back(v):
    return v

def low_keep(v):
    return (low(v), None)

def low_pass(kept, grad):
    return (grad,)

def back_keep(v):
    return (v, None)

def back_low(kept, grad):
    return (low(grad),)
low.defvjp(low_keep, low_pass)
low_back.defvjp(back_keep, back_low)
eps = 1e-06
highest = lax.Precision.HIGHEST

def layer_norm(values, gain, shift):
    average = lax.optimization_barrier(jnp.mean(values, axis=-1, keepdims=True))
    centered = values - average
    variance = lax.optimization_barrier(jnp.mean(centered * centered, axis=-1, keepdims=True))
    return centered * lax.rsqrt(variance + eps) * gain + shift

def rel_table(table):
    query_pos = jnp.arange(WIN, dtype=jnp.int32)[:, None, None]
    key_pos = jnp.arange(WIN, dtype=jnp.int32)[None, :, None]
    offset = jnp.arange(2 * WIN - 1, dtype=jnp.int32)[None, None, :]
    onehot = (offset == query_pos - key_pos + WIN - 1).astype(jnp.float32)
    return jnp.einsum('ijr,rc->ijc', onehot, table, precision=highest)

def window_attention(window, w_qkv, qv_bias, table_rows, table_cols):
    count = WIN * WIN
    tokens = window.reshape(count, D)
    bias_row = jnp.concatenate([qv_bias[:, 0], jnp.zeros((D,), jnp.float32), qv_bias[:, 1]])
    project = low_back(low(jnp.dot(tokens, w_qkv, precision=highest) + bias_row))
    query = project[:, :D].reshape(WIN, WIN, HEADS, HD)
    key = project[:, D:2 * D].reshape(WIN, WIN, HEADS, HD)
    value = project[:, 2 * D:].reshape(count, HEADS, HD)
    scores = jnp.einsum('abhc,ijhc->habij', query * HD ** (-0.5), key, precision=highest)
    along_rows = jnp.einsum('abhc,aic->habi', query, table_rows, precision=highest)
    along_cols = jnp.einsum('abhc,bjc->habj', query, table_cols, precision=highest)
    scores = scores + along_rows[:, :, :, :, None] + along_cols[:, :, :, None, :]
    scores = low_back(scores.reshape(HEADS, count, count))
    maxima = lax.optimization_barrier(jnp.max(scores, axis=-1, keepdims=True))
    weights = jnp.exp(scores - maxima)
    probs = low(weights / lax.optimization_barrier(jnp.sum(weights, axis=-1, keepdims=True)))
    attended = jnp.einsum('hqk,khc->qhc', probs, value, precision=highest)
    return low_back(low(attended.reshape(count, D)))

def image_forward(image, params):
    ln1_gain, ln1_bias, w_qkv, qv_bias, rel_rows, rel_cols, w_proj, proj_bias, ln2_gain, ln2_bias, w_fc1, fc1_bias, w_fc2, fc2_bias = params
    extra = NWIN * WIN - IMG
    normed = low(layer_norm(image, ln1_gain, ln1_bias))
    padded = jnp.pad(normed, ((0, extra), (0, extra), (0, 0)))
    windows = padded.reshape(NWIN, WIN, NWIN, WIN, D).transpose(0, 2, 1, 3, 4).reshape(NWIN * NWIN, WIN, WIN, D)
    table_rows = rel_table(rel_rows)
    table_cols = rel_table(rel_cols)
    attend = jax.checkpoint(lambda window: window_attention(window, w_qkv, qv_bias, table_rows, table_cols))
    results = lax.map(attend, windows)
    results = results.reshape(NWIN, NWIN, WIN, WIN, D).transpose(0, 2, 1, 3, 4).reshape(NWIN * WIN, NWIN * WIN, D)
    attended = results[:IMG, :IMG].reshape(IMG * IMG, D)
    branch = low_back(jnp.dot(attended, w_proj, precision=highest) + proj_bias)
    middle = image.reshape(IMG * IMG, D) + branch
    normed2 = low(layer_norm(middle, ln2_gain, ln2_bias))
    hidden = low_back(jnp.dot(normed2, w_fc1, precision=highest) + fc1_bias)
    active = low(jax.nn.gelu(hidden, approximate=False))
    mixed = low_back(jnp.dot(active, w_fc2, precision=highest) + fc2_bias)
    return (middle + mixed).reshape(IMG, IMG, D)

def reference(image_in, ln1_gain, ln1_bias, w_qkv, qv_bias, rel_rows, rel_cols, w_proj, proj_bias, ln2_gain, ln2_bias, w_fc1, fc1_bias, w_fc2, fc2_bias, cotangent):
    params = tuple((weight.astype(jnp.float32) for weight in (ln1_gain, ln1_bias, w_qkv, qv_bias, rel_rows, rel_cols, w_proj, proj_bias, ln2_gain, ln2_bias, w_fc1, fc1_bias, w_fc2, fc2_bias)))

    def one_image(totals, pair):
        image, grad_out = pair
        result, pullback = jax.vjp(image_forward, image.astype(jnp.float32), params)
        grad_image, grad_params = pullback(grad_out.astype(jnp.float32))
        totals = jax.tree.map(lambda left, right: left + right, totals, grad_params)
        return (totals, (result.astype(jnp.bfloat16), grad_image))
    zeros = jax.tree.map(jnp.zeros_like, params)
    totals, (outputs, grad_images) = lax.scan(one_image, zeros, (image_in, cotangent))
    return (outputs, grad_images, totals[0], totals[1], totals[2], totals[3], totals[4], totals[5], totals[6], totals[7], totals[8], totals[9], totals[10], totals[11], totals[12], totals[13])
```

```python
import functools

import jax
import jax.numpy as jnp
import numpy as np
from jax import lax
from jax.experimental import pallas as pl
from jax.experimental.pallas import tpu as pltpu
from jax.sharding import PartitionSpec as P

HEADS = 16
WIN = 14
NWIN = 5
SIDE = 16
HD = 80
KEYS = WIN * SIDE
TOK = SIDE * SIDE
LANES = 128
DEPTH = 128
REL = 2 * WIN - 1
NEG = -1e30
ALL = ("dp", "rows", "cols")
MIB = 1024 * 1024

eps = 1e-06


def dot(a, b):
    return jnp.dot(a, b, preferred_element_type=jnp.float32)


def dot_nt(a, b):
    return lax.dot_general(a, b, (((1,), (1,)), ((), ())), preferred_element_type=jnp.float32)


def dot_tn(a, b):
    return lax.dot_general(a, b, (((0,), (0,)), ((), ())), preferred_element_type=jnp.float32)


def offset_onehot(dtype):
    a = jnp.arange(WIN)[:, None]
    i = jnp.arange(SIDE)[None, :]
    offset = jnp.where(i < WIN, a - i + WIN - 1, -1)
    return (offset[:, :, None] == jnp.arange(REL)).astype(dtype).reshape(KEYS, REL)


def wide_tables(rel_rows, rel_cols):
    onehot = offset_onehot(jnp.bfloat16)
    return jnp.concatenate(
        [dot(onehot, table).astype(jnp.bfloat16) for table in (rel_rows, rel_cols)], axis=0
    )


def narrow_tables(grad):
    onehot = offset_onehot(jnp.float32)
    return [
        lax.dot_general(
            onehot,
            grad[n * KEYS : (n + 1) * KEYS],
            (((0,), (0,)), ((), ())),
            precision=lax.Precision.HIGHEST,
        )
        for n in (0, 1)
    ]


def key_indicator():
    row = lax.broadcasted_iota(jnp.int32, (DEPTH - HD, TOK), 0)
    key = lax.broadcasted_iota(jnp.int32, (DEPTH - HD, TOK), 1)
    return ((row == key // SIDE) | (row - SIDE == key % SIDE)).astype(jnp.bfloat16)


def query_offsets(query, tab_ref, lane):
    halves = []
    for half in range(2):
        low = half * 8
        count = min(8, WIN - low)
        part = dot(
            tab_ref[low * SIDE : (low + count) * SIDE], query[:, half * LANES : (half + 1) * LANES]
        )
        rows = part[:SIDE]
        for a in range(1, count):
            rows = jnp.where(
                lane[:, :LANES] // SIDE == a, part[a * SIDE : (a + 1) * SIDE], rows
            )
        halves.append(rows)
    part = dot(tab_ref[KEYS:], query)
    cols = part[:SIDE]
    for b in range(1, WIN):
        cols = jnp.where(lane % SIDE == b, part[b * SIDE : (b + 1) * SIDE], cols)
    return jnp.concatenate(halves, axis=1), cols


def attention_forward_kernel(
    project_ref, tab_ref, ind_ref, attended_ref, weights_ref, inverse_ref, turned_ref
):
    model = turned_ref.shape[0]
    lane = lax.broadcasted_iota(jnp.int32, (SIDE, TOK), 1)
    sub = lax.broadcasted_iota(jnp.int32, (SIDE, TOK), 0)
    ind = ind_ref[...]
    scale = HD**-0.5
    zeros = jnp.zeros((DEPTH - HD - 2 * SIDE, TOK), jnp.bfloat16)
    for head in range(HEADS):
        low = head * HD
        query = project_ref[low : low + HD]
        key = project_ref[model + low : model + low + HD]
        value = project_ref[2 * model + low : 2 * model + low + HD]
        rows, cols = query_offsets(query, tab_ref, lane)
        rows = (rows * HD**0.5).astype(jnp.bfloat16)
        cols = jnp.where(sub < WIN, cols * HD**0.5, NEG).astype(jnp.bfloat16)
        query_wide = jnp.concatenate([query, rows, cols, zeros], axis=0)
        key_wide = jnp.concatenate([key, ind], axis=0)
        scores = dot_tn(key_wide, query_wide)[:KEYS]
        maxima = jnp.max(scores, axis=0, keepdims=True)
        weights = jnp.exp((scores - maxima) * scale)
        inverse = 1.0 / jnp.sum(weights, axis=0, keepdims=True)
        weights = weights.astype(jnp.bfloat16)
        weights_ref[0, head] = weights
        inverse_ref[0, head : head + 1] = inverse
        attended = dot(value[:, :KEYS], weights)
        turned_ref[low : low + HD] = (attended * inverse).astype(jnp.bfloat16)
    attended_ref[...] = turned_ref[...].T


def attention_forward(project, tab, ind):
    model = project.shape[0] // 3
    slots = project.shape[1] // TOK
    return pl.pallas_call(
        attention_forward_kernel,
        grid=(slots,),
        in_specs=[
            pl.BlockSpec((3 * model, TOK), lambda i: (0, i)),
            pl.BlockSpec((2 * KEYS, HD), lambda i: (0, 0)),
            pl.BlockSpec((DEPTH - HD, TOK), lambda i: (0, 0)),
        ],
        out_specs=[
            pl.BlockSpec((TOK, model), lambda i: (i, 0)),
            pl.BlockSpec((1, HEADS, KEYS, TOK), lambda i: (i, 0, 0, 0)),
            pl.BlockSpec((1, HEADS, TOK), lambda i: (i, 0, 0)),
        ],
        out_shape=[
            jax.ShapeDtypeStruct((slots * TOK, model), jnp.bfloat16),
            jax.ShapeDtypeStruct((slots, HEADS, KEYS, TOK), jnp.bfloat16),
            jax.ShapeDtypeStruct((slots, HEADS, TOK), jnp.float32),
        ],
        scratch_shapes=[pltpu.VMEM((model, TOK), jnp.bfloat16)],
        compiler_params=pltpu.CompilerParams(vmem_limit_bytes=48 * MIB),
        cost_estimate=pl.CostEstimate(
            flops=slots * HEADS * 800 * 2 * TOK * LANES,
            bytes_accessed=slots * 6 * MIB,
            transcendentals=slots * HEADS * KEYS * TOK,
        ),
    )(project, tab, ind)


def attention_backward_kernel(
    project_ref, weights_ref, inverse_ref, grad_ref, tab_ref, ind_ref, out_ref, dtab_ref, turned_ref
):
    model = turned_ref.shape[0]
    lane = lax.broadcasted_iota(jnp.int32, (SIDE, TOK), 1)
    ind = ind_ref[...]
    tab = tab_ref[...]
    scale = HD**-0.5

    @pl.when(pl.program_id(0) == 0)
    def _():
        dtab_ref[...] = jnp.zeros_like(dtab_ref)

    turned_ref[...] = grad_ref[...].T
    total = jnp.zeros(dtab_ref.shape, jnp.float32)
    for head in range(HEADS):
        low = head * HD
        query = project_ref[low : low + HD]
        key = project_ref[model + low : model + low + HD]
        value = project_ref[2 * model + low : 2 * model + low + HD]
        inverse = inverse_ref[0, head : head + 1]
        grad = (turned_ref[low : low + HD] * inverse).astype(jnp.bfloat16)
        weights = weights_ref[0, head]
        weights_float = weights.astype(jnp.float32)
        terms = weights_float * dot_tn(value, grad)[:KEYS]
        inner = jnp.sum(terms, axis=0, keepdims=True) * inverse
        grad_scores = (terms - weights_float * inner).astype(jnp.bfloat16)
        grad_value = dot_nt(grad, weights)
        grad_key = dot_nt(query, grad_scores) * scale
        key_wide = jnp.concatenate([key, ind], axis=0)
        grad_wide = dot(key_wide[:, :KEYS], grad_scores)
        rows = grad_wide[HD : HD + SIDE]
        cols = grad_wide[HD + SIDE : HD + 2 * SIDE]
        spread = jnp.concatenate(
            [jnp.where(lane // SIDE == a, rows, 0.0) for a in range(WIN)]
            + [jnp.where(lane % SIDE == b, cols, 0.0) for b in range(WIN)],
            axis=0,
        ).astype(jnp.bfloat16)
        grad_query = grad_wide[:HD] * scale + dot_tn(tab, spread)
        total = total + dot_nt(spread, query)
        out_ref[low : low + HD] = grad_query.astype(jnp.bfloat16)
        out_ref[model + low : model + low + HD, :KEYS] = grad_key.astype(jnp.bfloat16)
        out_ref[2 * model + low : 2 * model + low + HD, :KEYS] = grad_value.astype(jnp.bfloat16)
    out_ref[model:, KEYS:] = jnp.zeros((2 * model, TOK - KEYS), jnp.bfloat16)
    dtab_ref[...] += total


def attention_backward(project, weights, inverse, grad, tab, ind):
    model = project.shape[0] // 3
    slots = project.shape[1] // TOK
    return pl.pallas_call(
        attention_backward_kernel,
        grid=(slots,),
        in_specs=[
            pl.BlockSpec((3 * model, TOK), lambda i: (0, i)),
            pl.BlockSpec((1, HEADS, KEYS, TOK), lambda i: (i, 0, 0, 0)),
            pl.BlockSpec((1, HEADS, TOK), lambda i: (i, 0, 0)),
            pl.BlockSpec((TOK, model), lambda i: (i, 0)),
            pl.BlockSpec((2 * KEYS, HD), lambda i: (0, 0)),
            pl.BlockSpec((DEPTH - HD, TOK), lambda i: (0, 0)),
        ],
        out_specs=[
            pl.BlockSpec((3 * model, TOK), lambda i: (0, i)),
            pl.BlockSpec((2 * KEYS, HD), lambda i: (0, 0)),
        ],
        out_shape=[
            jax.ShapeDtypeStruct((3 * model, slots * TOK), jnp.bfloat16),
            jax.ShapeDtypeStruct((2 * KEYS, HD), jnp.float32),
        ],
        scratch_shapes=[pltpu.VMEM((model, TOK), jnp.bfloat16)],
        compiler_params=pltpu.CompilerParams(vmem_limit_bytes=48 * MIB),
        cost_estimate=pl.CostEstimate(
            flops=slots * HEADS * 1600 * 2 * TOK * LANES,
            bytes_accessed=slots * 7 * MIB,
            transcendentals=0,
        ),
    )(project, weights, inverse, grad, tab, ind)


def mlp_kernel(
    rows,
    normed_ref,
    turned_ref,
    cot_ref,
    up_ref,
    down_ref,
    shift_ref,
    mixed0_ref,
    grad0_ref,
    mixed_ref,
    grad_ref,
    dup_ref,
    ddown_ref,
    dshift_ref,
    active_ref,
    hidden_ref,
):
    tokens = normed_ref.shape[0]

    @pl.when(pl.program_id(0) == 0)
    def _():
        mixed_ref[...] = mixed0_ref[...]
        grad_ref[...] = grad0_ref[...]

    up = up_ref[...]
    down = down_ref[...]
    shift = shift_ref[...]
    total = jnp.zeros(shift.shape, jnp.float32)
    for step in range(tokens // rows):
        part = slice(step * rows, (step + 1) * rows)
        hidden = dot(normed_ref[part], up) + shift
        grad_active = dot_nt(cot_ref[part], down)
        half = 0.5 + 0.5 * lax.erf(hidden * 0.5**0.5)
        active = (hidden * half).astype(jnp.bfloat16)
        slope = half + hidden * jnp.exp(hidden * hidden * -0.5) * (2 * np.pi) ** -0.5
        grad_hidden = (grad_active * slope).astype(jnp.bfloat16)
        active_ref[part] = active
        hidden_ref[part] = grad_hidden
        total = total + jnp.sum(grad_hidden.astype(jnp.float32), axis=0, keepdims=True)
        mixed_ref[part] += dot(active, down)
        grad_ref[part] += dot_nt(grad_hidden, up)
    dshift_ref[...] = total
    ddown_ref[...] = dot_tn(active_ref[...], cot_ref[...]).astype(jnp.bfloat16)
    dup_ref[...] = dot(turned_ref[...], hidden_ref[...]).astype(jnp.bfloat16)


def mlp(normed, turned, cot, up, down, shift, mixed0, grad0):
    tokens, model = normed.shape
    hidden = up.shape[1]
    block = 512 if hidden % 512 == 0 else 256
    rows = min(512, tokens)
    once = pl.Buffered(1)
    whole = pl.BlockSpec((tokens, model), lambda i: (0, 0), pipeline_mode=once)
    return pl.pallas_call(
        functools.partial(mlp_kernel, rows),
        grid=(hidden // block,),
        in_specs=[
            whole,
            pl.BlockSpec((model, tokens), lambda i: (0, 0), pipeline_mode=once),
            whole,
            pl.BlockSpec((model, block), lambda i: (0, i)),
            pl.BlockSpec((block, model), lambda i: (i, 0)),
            pl.BlockSpec((1, block), lambda i: (0, i)),
            whole,
            whole,
        ],
        out_specs=[
            pl.BlockSpec((tokens, model), lambda i: (0, 0)),
            pl.BlockSpec((tokens, model), lambda i: (0, 0)),
            pl.BlockSpec((model, block), lambda i: (0, i)),
            pl.BlockSpec((block, model), lambda i: (i, 0)),
            pl.BlockSpec((1, block), lambda i: (0, i)),
        ],
        out_shape=[
            jax.ShapeDtypeStruct((tokens, model), jnp.float32),
            jax.ShapeDtypeStruct((tokens, model), jnp.float32),
            jax.ShapeDtypeStruct((model, hidden), jnp.bfloat16),
            jax.ShapeDtypeStruct((hidden, model), jnp.bfloat16),
            jax.ShapeDtypeStruct((1, hidden), jnp.float32),
        ],
        scratch_shapes=[pltpu.VMEM((tokens, block), jnp.bfloat16)] * 2,
        compiler_params=pltpu.CompilerParams(vmem_limit_bytes=56 * MIB),
        cost_estimate=pl.CostEstimate(
            flops=12 * tokens * model * hidden,
            bytes_accessed=8 * model * hidden + 24 * tokens * model,
            transcendentals=2 * tokens * hidden,
        ),
    )(normed, turned, cot, up, down, shift, mixed0, grad0)


def normalised(values):
    average = jnp.mean(values, axis=-1, keepdims=True)
    centered = values - average
    variance = jnp.mean(centered * centered, axis=-1, keepdims=True)
    inverse = lax.rsqrt(variance + eps)
    return centered * inverse, inverse


def norm_backward(unit, inverse, gain, grad):
    scaled = grad * gain
    grad_values = inverse * (
        scaled
        - jnp.mean(scaled, axis=-1, keepdims=True)
        - unit * jnp.mean(scaled * unit, axis=-1, keepdims=True)
    )
    return grad_values, jnp.sum(grad * unit, axis=0), jnp.sum(grad, axis=0)


def axis_bits(axis):
    count = lax.axis_size(axis)
    return [(axis, 1 << bit) for bit in range(count.bit_length() - 1)]


def flipped(value, bit):
    axis, mask = bit
    return lax.ppermute(value, axis, [(i, i ^ mask) for i in range(lax.axis_size(axis))])


def bit_of(bit):
    axis, mask = bit
    return (lax.axis_index(axis) // mask) % 2


def device_bits():
    return [bit for axis in ALL for bit in reversed(axis_bits(axis))]


def scatter_sum(value, order):
    left = device_bits()
    block = value.shape[0] >> len(left)
    value = value.reshape((2,) * len(left) + (block,) + value.shape[1:])
    for bit in order:
        place = left.index(bit)
        mine = bit_of(bit)
        sent = lax.dynamic_index_in_dim(value, 1 - mine, place, keepdims=False)
        kept = lax.dynamic_index_in_dim(value, mine, place, keepdims=False)
        value = kept.astype(jnp.float32) + flipped(sent, bit).astype(jnp.float32)
        left.remove(bit)
        if left:
            value = value.astype(jnp.bfloat16)
    return value


def all_sum(value):
    for bit in reversed(device_bits()):
        value = value + flipped(value, bit)
    return value


def small_gather(value):
    for bit in reversed(device_bits()):
        arrived = flipped(value, bit)
        value = jnp.where(
            bit_of(bit) == 0,
            jnp.concatenate([value, arrived], axis=0),
            jnp.concatenate([arrived, value], axis=0),
        )
    return value


def halves_to_image(tiles):
    col = lax.axis_index("cols")
    kept = lax.dynamic_index_in_dim(tiles, col, 0, keepdims=False)
    sent = lax.dynamic_index_in_dim(tiles, 1 - col, 0, keepdims=False)
    arrived = lax.ppermute(sent, "cols", [(0, 1), (1, 0)])
    return jnp.where(
        col == 0,
        jnp.concatenate([kept, arrived], axis=1),
        jnp.concatenate([arrived, kept], axis=1),
    )


def image_to_halves(image):
    col = lax.axis_index("cols")
    width = image.shape[1] // 2
    kept = lax.dynamic_slice_in_dim(image, col * width, width, 1)
    sent = lax.dynamic_slice_in_dim(image, (1 - col) * width, width, 1)
    arrived = lax.ppermute(sent, "cols", [(0, 1), (1, 0)])
    return jnp.where(col == 0, jnp.stack([kept, arrived]), jnp.stack([arrived, kept]))


def column_windows(tile):
    height, width, model = tile.shape
    wide = jnp.pad(tile, ((0, 0), (0, NWIN * WIN - width), (0, 0)))
    wide = wide.reshape(height, NWIN, WIN, model).transpose(1, 0, 2, 3)
    return jnp.pad(wide, ((0, 0), (0, 0), (0, SIDE - WIN), (0, 0)))


def column_rows(windows, width):
    _, height, _, model = windows.shape
    wide = windows[:, :, :WIN].transpose(1, 0, 2, 3).reshape(height, NWIN * WIN, model)
    return wide[:, :width]


def pad_rows(value, top, bottom):
    widths = [(0, 0)] * value.ndim
    widths[-3] = (top, bottom)
    return jnp.pad(value, widths)


def near_plan():
    return lax.axis_size("rows") == NWIN - 1


def spread(tile):
    height = tile.shape[0]
    count = lax.axis_size("rows")
    row = lax.axis_index("rows")
    windows = column_windows(tile)
    if not near_plan():
        windows = lax.all_gather(windows, "rows", axis=1, tiled=True)
        extra = NWIN * WIN - windows.shape[1]
        windows = jnp.pad(windows, ((0, 0), (0, extra), (0, 0), (0, 0)))
        windows = windows.reshape(NWIN, NWIN, WIN, SIDE, -1).transpose(1, 0, 2, 3, 4)
        windows = windows.reshape((NWIN * NWIN,) + windows.shape[2:])
        slots = -(-NWIN * NWIN // count)
        windows = jnp.pad(
            windows, ((0, slots * count - NWIN * NWIN), (0, SIDE - WIN), (0, 0), (0, 0))
        )
        return lax.dynamic_slice_in_dim(windows, row * slots, slots, 0)
    step = height - WIN
    last = count - 1
    halo = step * last
    rest = height * count - WIN * count
    down = lax.ppermute(windows[:, height - halo :], "rows", [(i, i + 1) for i in range(last)])
    main = lax.dynamic_slice_in_dim(
        jnp.concatenate([down, windows], axis=1), halo - step * row, WIN, 1
    )
    tail = windows[:, height - rest :]
    extra = tail[last]
    for target in range(last):
        arrived = lax.ppermute(tail[target], "rows", [(last, target)])
        extra = jnp.where(row == target, arrived, extra)
    more = jnp.where(row == last, tail[last + 1 :], jnp.zeros_like(tail[last + 1 :]))
    ends = jnp.concatenate([extra[None], more], axis=0)
    return jnp.concatenate([pad_rows(main, 0, SIDE - WIN), pad_rows(ends, 0, SIDE - rest)], axis=0)


def collect(windows, height, width):
    count = lax.axis_size("rows")
    row = lax.axis_index("rows")
    if not near_plan():
        windows = lax.all_gather(windows[:, :WIN], "rows", axis=0, tiled=True)
        windows = windows[: NWIN * NWIN].reshape((NWIN, NWIN) + windows.shape[1:])
        windows = windows.transpose(1, 0, 2, 3, 4).reshape(NWIN, NWIN * WIN, SIDE, -1)
        return column_rows(lax.dynamic_slice_in_dim(windows, row * height, height, 1), width)
    step = height - WIN
    last = count - 1
    halo = step * last
    rest = height * count - WIN * count
    main = windows[:NWIN, :WIN]
    ends = windows[NWIN:, :rest]
    up = lax.ppermute(main[:, :halo], "rows", [(i + 1, i) for i in range(last)])
    tail = jnp.concatenate(
        [lax.ppermute(ends[0], "rows", [(source, last)])[None] for source in range(last)] + [ends],
        axis=0,
    )
    below = jnp.where(row == last, tail, pad_rows(up, 0, rest - halo))
    whole = jnp.concatenate([main, below], axis=1)
    return column_rows(lax.dynamic_slice_in_dim(whole, step * row, height, 1), width)


def token_mask(slots, height, width):
    count = lax.axis_size("rows")
    row = lax.axis_index("rows")
    slot = lax.broadcasted_iota(jnp.int32, (slots, SIDE, SIDE, 1), 0)
    i = lax.broadcasted_iota(jnp.int32, (slots, SIDE, SIDE, 1), 1)
    j = lax.broadcasted_iota(jnp.int32, (slots, SIDE, SIDE, 1), 2)
    if near_plan():
        window_row = jnp.where(slot < NWIN, row, NWIN - 1)
        extra = jnp.where(row == count - 1, row + slot - NWIN, row)
        window_col = jnp.where(slot < NWIN, slot, extra)
        held = (slot <= NWIN) | (row == count - 1)
    else:
        window = row * slots + slot
        window_row = window // NWIN
        window_col = window % NWIN
        held = window < NWIN * NWIN
    inside = (window_row * WIN + i < height) & (window_col * WIN + j < width)
    return (held & inside & (i < WIN) & (j < WIN)).astype(jnp.float32)


def shards(
    image_in,
    ln1_gain,
    ln1_bias,
    w_qkv,
    qv_bias,
    rel_rows,
    rel_cols,
    w_proj,
    proj_bias,
    ln2_gain,
    ln2_bias,
    w_fc1,
    fc1_bias,
    w_fc2,
    fc2_bias,
    cotangent,
):
    devices = lax.axis_size(ALL)
    me = lax.axis_index(ALL)
    images, tile_h, tile_w, model = image_in.shape
    tokens = images * tile_h * tile_w
    width = tile_w * lax.axis_size("cols")
    share = model // devices
    unit = fc1_bias.shape[0]
    part = unit // 2

    def gathered(shard):
        return lax.all_gather(shard, ALL, axis=0, tiled=True)

    vectors = [ln1_gain, ln1_bias, qv_bias[:, 0], qv_bias[:, 1], proj_bias, ln2_gain, ln2_bias]
    vectors = small_gather(jnp.concatenate(vectors + [fc2_bias, fc1_bias])[None])
    vectors = vectors.astype(jnp.float32)
    gain1, shift1, query_shift, value_shift, proj_shift, gain2, shift2, down_shift = (
        vectors[:, n * share : (n + 1) * share].reshape(model) for n in range(8)
    )
    up_shift = vectors[:, 8 * share :]
    qkv_full = gathered(w_qkv)
    proj_full = gathered(w_proj)
    up_parts = w_fc1.reshape(share, devices, 2, part)
    ups = [gathered(up_parts[:, :, n].reshape(share, devices * part)) for n in (0, 1)]
    downs = [gathered(w_fc2[n * part : (n + 1) * part]) for n in (0, 1)]

    raw = spread(halves_to_image(image_in))
    slots = raw.shape[0]
    there = token_mask(slots, tile_h * lax.axis_size("rows"), width)
    window_unit, _ = normalised(raw.astype(jnp.float32))
    window_tokens = ((window_unit * gain1 + shift1) * there).astype(jnp.bfloat16)
    window_tokens = window_tokens.reshape(slots * TOK, model)
    shift_qkv = jnp.concatenate([query_shift, jnp.zeros((model,), jnp.float32), value_shift])
    project = lax.dot_general(
        qkv_full, window_tokens, (((0,), (1,)), ((), ())), preferred_element_type=jnp.float32
    )
    project = (project + shift_qkv[:, None]).astype(jnp.bfloat16)
    tab = wide_tables(rel_rows, rel_cols)
    ind = key_indicator()
    attended_windows, weights, inverse = attention_forward(project, tab, ind)
    attended = image_to_halves(
        collect(attended_windows.reshape(slots, SIDE, SIDE, model), tile_h, width)
    ).reshape(tokens, model)

    image = image_in.astype(jnp.float32).reshape(tokens, model)
    cot = cotangent.reshape(tokens, model)
    middle = image + dot(attended, proj_full) + proj_shift
    unit2, inverse2 = normalised(middle)
    normed2 = (unit2 * gain2 + shift2).astype(jnp.bfloat16)
    turned2 = normed2.T
    mixed = jnp.zeros((tokens, model), jnp.float32)
    grad_normed2 = jnp.zeros((tokens, model), jnp.float32)
    grad_ups, grad_downs, grad_up_shifts = [], [], []
    for n in (0, 1):
        shift = up_shift[:, n * part : (n + 1) * part].reshape(1, devices * part)
        mixed, grad_normed2, grad_up, grad_down, grad_shift = mlp(
            normed2, turned2, cot, ups[n], downs[n], shift, mixed, grad_normed2
        )
        grad_ups.append(grad_up)
        grad_downs.append(grad_down)
        grad_up_shifts.append(grad_shift.reshape(devices, part))
    output = (middle + mixed + down_shift).astype(jnp.bfloat16).reshape(image_in.shape)

    dp_bits = axis_bits("dp")
    core, chips = dp_bits[:1], dp_bits[1:]
    x_first = core + axis_bits("cols") + chips + axis_bits("rows")
    y_first = core + chips + axis_bits("cols") + axis_bits("rows")
    sum_ups = [scatter_sum(grad, x_first) for grad in grad_ups]
    sum_downs = [scatter_sum(grad, y_first) for grad in grad_downs]

    grad_middle, grad_gain2, grad_shift2 = norm_backward(unit2, inverse2, gain2, grad_normed2)
    grad_middle = grad_middle + cot.astype(jnp.float32)
    grad_branch = grad_middle.astype(jnp.bfloat16)
    grad_attended = dot_nt(grad_branch, proj_full).astype(jnp.bfloat16)
    grad_proj = dot_tn(attended, grad_branch).astype(jnp.bfloat16)
    sum_proj = scatter_sum(grad_proj, x_first)

    def rows_of(vector):
        return vector.reshape(devices, -1)

    early = jnp.concatenate(
        [
            rows_of(jnp.sum(grad_branch, axis=0, dtype=jnp.float32)),
            rows_of(grad_gain2),
            rows_of(grad_shift2),
            rows_of(jnp.sum(cot, axis=0, dtype=jnp.float32)),
        ]
        + grad_up_shifts,
        axis=1,
    )
    early = lax.dynamic_index_in_dim(all_sum(early), me, 0, keepdims=False)

    grad_windows = spread(halves_to_image(grad_attended.reshape(image_in.shape)))
    grad_project, grad_tab = attention_backward(
        project, weights, inverse, grad_windows.reshape(slots * TOK, model), tab, ind
    )
    grad_qkv = lax.dot_general(
        window_tokens, grad_project, (((0,), (1,)), ((), ())), preferred_element_type=jnp.float32
    ).astype(jnp.bfloat16)
    cut = 3 * model // 2
    sum_qkv = [scatter_sum(grad_qkv[:, :cut], x_first), scatter_sum(grad_qkv[:, cut:], y_first)]
    grad_tokens = lax.dot_general(
        grad_project, qkv_full, (((0,), (1,)), ((), ())), preferred_element_type=jnp.float32
    ).astype(jnp.bfloat16)
    grad_normed = image_to_halves(
        collect(grad_tokens.reshape(slots, SIDE, SIDE, model), tile_h, width)
    )
    unit1, inverse1 = normalised(image)
    grad_image, grad_gain1, grad_shift1 = norm_backward(
        unit1, inverse1, gain1, grad_normed.reshape(tokens, model).astype(jnp.float32)
    )
    grad_in = (grad_middle + grad_image).reshape(image_in.shape)
    grad_sums = jnp.sum(grad_project, axis=1, dtype=jnp.float32)
    late = jnp.concatenate(
        [
            rows_of(grad_gain1),
            rows_of(grad_shift1),
            rows_of(grad_sums[:model]),
            rows_of(grad_sums[2 * model :]),
        ],
        axis=1,
    )
    grad_tables = jnp.stack(narrow_tables(grad_tab))
    late, grad_tables = all_sum_pair(late, grad_tables)
    late = lax.dynamic_index_in_dim(late, me, 0, keepdims=False)

    grad_fc1 = jnp.stack([grad.reshape(share, devices, part) for grad in sum_ups], axis=2)
    return (
        output,
        grad_in,
        late[:share],
        late[share : 2 * share],
        jnp.concatenate(sum_qkv, axis=1),
        jnp.stack([late[2 * share : 3 * share], late[3 * share :]], axis=1),
        grad_tables[0],
        grad_tables[1],
        sum_proj,
        early[:share],
        early[share : 2 * share],
        early[2 * share : 3 * share],
        grad_fc1.reshape(share, devices * unit),
        early[4 * share :],
        jnp.concatenate(sum_downs, axis=0),
        early[3 * share : 4 * share],
    )


def all_sum_pair(first, second):
    sizes = first.size
    joined = all_sum(jnp.concatenate([first.reshape(-1), second.reshape(-1)]))
    return joined[:sizes].reshape(first.shape), joined[sizes:].reshape(second.shape)


def solution(mesh):
    tile = P("dp", "rows", "cols", None)
    vector = P(ALL)
    matrix = P(ALL, None)
    in_specs = (
        tile, vector, vector, matrix, matrix, P(), P(), matrix, vector, vector, vector,
        matrix, vector, matrix, vector, tile,
    )
    out_specs = (
        tile, tile, vector, vector, matrix, matrix, P(), P(), matrix, vector, vector, vector,
        matrix, vector, matrix, vector,
    )
    return jax.shard_map(shards, mesh=mesh, in_specs=in_specs, out_specs=out_specs, check_vma=False)
```

```python
import functools

import jax
import jax.numpy as jnp
import numpy as np
from jax import lax
from jax.experimental import pallas as pl
from jax.experimental.pallas import tpu as pltpu
from jax.sharding import PartitionSpec as P

HEADS = 16
HALF = HEADS // 2
WIN = 14
NWIN = 5
SIDE = 16
HD = 80
KEYS = WIN * SIDE
TOK = SIDE * SIDE
LANES = 128
DEPTH = 128
REL = 2 * WIN - 1
NEG = -1e30
END = 24
ALL = ("dp", "rows", "cols")
MIB = 1024 * 1024
PARTS = 4

eps = 1e-06


def dot(a, b):
    return jnp.dot(a, b, preferred_element_type=jnp.float32)


def dot_nt(a, b):
    return lax.dot_general(a, b, (((1,), (1,)), ((), ())), preferred_element_type=jnp.float32)


def dot_tn(a, b):
    return lax.dot_general(a, b, (((0,), (0,)), ((), ())), preferred_element_type=jnp.float32)


def offset_onehot(dtype):
    a = jnp.arange(WIN)[:, None]
    i = jnp.arange(SIDE)[None, :]
    offset = jnp.where(i < WIN, a - i + WIN - 1, -1)
    return (offset[:, :, None] == jnp.arange(REL)).astype(dtype).reshape(KEYS, REL)


def wide_tables(rel_rows, rel_cols):
    onehot = offset_onehot(jnp.bfloat16)
    return jnp.concatenate(
        [dot(onehot, table).astype(jnp.bfloat16) for table in (rel_rows, rel_cols)], axis=0
    )


def narrow_tables(grad):
    onehot = offset_onehot(jnp.float32)
    return [
        lax.dot_general(
            onehot,
            grad[n * KEYS : (n + 1) * KEYS],
            (((0,), (0,)), ((), ())),
            precision=lax.Precision.HIGHEST,
        )
        for n in (0, 1)
    ]


def key_indicator():
    row = lax.broadcasted_iota(jnp.int32, (DEPTH - HD, TOK), 0)
    key = lax.broadcasted_iota(jnp.int32, (DEPTH - HD, TOK), 1)
    return ((row == key // SIDE) | (row - SIDE == key % SIDE)).astype(jnp.bfloat16)


def query_offsets(query, tab_ref, lane):
    halves = []
    for half in range(2):
        low = half * 8
        count = min(8, WIN - low)
        part = dot(
            tab_ref[low * SIDE : (low + count) * SIDE], query[:, half * LANES : (half + 1) * LANES]
        )
        rows = part[:SIDE]
        for a in range(1, count):
            rows = jnp.where(
                lane[:, :LANES] // SIDE == a, part[a * SIDE : (a + 1) * SIDE], rows
            )
        halves.append(rows)
    part = dot(tab_ref[KEYS:], query)
    cols = part[:SIDE]
    for b in range(1, WIN):
        cols = jnp.where(lane % SIDE == b, part[b * SIDE : (b + 1) * SIDE], cols)
    return jnp.concatenate(halves, axis=1), cols


def attention_forward_kernel(
    project_ref, tab_ref, ind_ref, attended_ref, weights_ref, inverse_ref, turned_ref
):
    model = turned_ref.shape[0]
    lane = lax.broadcasted_iota(jnp.int32, (SIDE, TOK), 1)
    sub = lax.broadcasted_iota(jnp.int32, (SIDE, TOK), 0)
    ind = ind_ref[...]
    scale = HD**-0.5
    zeros = jnp.zeros((DEPTH - HD - 2 * SIDE, TOK), jnp.bfloat16)
    for head in range(HEADS):
        low = head * HD
        place = head // HALF * 3 * model // 2 + head % HALF * HD
        query = project_ref[place : place + HD]
        key = project_ref[model // 2 + place : model // 2 + place + HD]
        value = project_ref[model + place : model + place + HD]
        rows, cols = query_offsets(query, tab_ref, lane)
        rows = (rows * HD**0.5).astype(jnp.bfloat16)
        cols = jnp.where(sub < WIN, cols * HD**0.5, NEG).astype(jnp.bfloat16)
        query_wide = jnp.concatenate([query, rows, cols, zeros], axis=0)
        key_wide = jnp.concatenate([key, ind], axis=0)
        scores = dot_tn(key_wide, query_wide)[:KEYS]
        maxima = jnp.max(scores, axis=0, keepdims=True)
        weights = jnp.exp((scores - maxima) * scale)
        inverse = 1.0 / jnp.sum(weights, axis=0, keepdims=True)
        weights = weights.astype(jnp.bfloat16)
        weights_ref[0, head] = weights
        inverse_ref[0, head : head + 1] = inverse
        attended = dot(value[:, :KEYS], weights)
        turned_ref[low : low + HD] = (attended * inverse).astype(jnp.bfloat16)
    attended_ref[...] = turned_ref[...].T


def attention_forward(project, tab, ind):
    model = project.shape[0] // 3
    slots = project.shape[1] // TOK
    return pl.pallas_call(
        attention_forward_kernel,
        grid=(slots,),
        in_specs=[
            pl.BlockSpec((3 * model, TOK), lambda i: (0, i)),
            pl.BlockSpec((2 * KEYS, HD), lambda i: (0, 0)),
            pl.BlockSpec((DEPTH - HD, TOK), lambda i: (0, 0)),
        ],
        out_specs=[
            pl.BlockSpec((TOK, model), lambda i: (i, 0)),
            pl.BlockSpec((1, HEADS, KEYS, TOK), lambda i: (i, 0, 0, 0)),
            pl.BlockSpec((1, HEADS, TOK), lambda i: (i, 0, 0)),
        ],
        out_shape=[
            jax.ShapeDtypeStruct((slots * TOK, model), jnp.bfloat16),
            jax.ShapeDtypeStruct((slots, HEADS, KEYS, TOK), jnp.bfloat16),
            jax.ShapeDtypeStruct((slots, HEADS, TOK), jnp.float32),
        ],
        scratch_shapes=[pltpu.VMEM((model, TOK), jnp.bfloat16)],
        compiler_params=pltpu.CompilerParams(vmem_limit_bytes=48 * MIB),
        cost_estimate=pl.CostEstimate(
            flops=slots * 7_000_000_000,
            bytes_accessed=slots * 6 * MIB,
            transcendentals=slots * HEADS * KEYS * TOK,
        ),
    )(project, tab, ind)


def attention_backward_kernel(
    project_ref, weights_ref, inverse_ref, grad_ref, tab_ref, ind_ref, out_ref, dtab_ref, turned_ref
):
    model = turned_ref.shape[0]
    lane = lax.broadcasted_iota(jnp.int32, (SIDE, TOK), 1)
    ind = ind_ref[...]
    tab = tab_ref[...]
    scale = HD**-0.5

    @pl.when(pl.program_id(0) == 0)
    def _():
        dtab_ref[...] = jnp.zeros_like(dtab_ref)

    turned_ref[...] = grad_ref[...].T
    total = jnp.zeros(dtab_ref.shape, jnp.float32)
    for head in range(HALF):
        low = head * HD
        query = project_ref[low : low + HD]
        key = project_ref[model + low : model + low + HD]
        value = project_ref[2 * model + low : 2 * model + low + HD]
        inverse = inverse_ref[0, head : head + 1]
        grad = (turned_ref[low : low + HD] * inverse).astype(jnp.bfloat16)
        weights = weights_ref[0, head]
        weights_float = weights.astype(jnp.float32)
        terms = weights_float * dot_tn(value, grad)[:KEYS]
        inner = jnp.sum(terms, axis=0, keepdims=True) * inverse
        grad_scores = (terms - weights_float * inner).astype(jnp.bfloat16)
        grad_value = dot_nt(grad, weights)
        grad_key = dot_nt(query, grad_scores) * scale
        key_wide = jnp.concatenate([key, ind], axis=0)
        grad_wide = dot(key_wide[:, :KEYS], grad_scores)
        rows = grad_wide[HD : HD + SIDE]
        cols = grad_wide[HD + SIDE : HD + 2 * SIDE]
        spread = jnp.concatenate(
            [jnp.where(lane // SIDE == a, rows, 0.0) for a in range(WIN)]
            + [jnp.where(lane % SIDE == b, cols, 0.0) for b in range(WIN)],
            axis=0,
        ).astype(jnp.bfloat16)
        grad_query = grad_wide[:HD] * scale + dot_tn(tab, spread)
        total = total + dot_nt(spread, query)
        out_ref[low : low + HD] = grad_query.astype(jnp.bfloat16)
        out_ref[model + low : model + low + HD, :KEYS] = grad_key.astype(jnp.bfloat16)
        out_ref[2 * model + low : 2 * model + low + HD, :KEYS] = grad_value.astype(jnp.bfloat16)
    out_ref[model:, KEYS:] = jnp.zeros((2 * model, TOK - KEYS), jnp.bfloat16)
    dtab_ref[...] += total


def attention_backward(project, weights, inverse, grad, tab, ind, half):
    model = project.shape[0] // 6
    slots = project.shape[1] // TOK
    return pl.pallas_call(
        attention_backward_kernel,
        grid=(slots,),
        in_specs=[
            pl.BlockSpec((3 * model, TOK), lambda i: (half, i)),
            pl.BlockSpec((1, HALF, KEYS, TOK), lambda i: (i, half, 0, 0)),
            pl.BlockSpec((1, HALF, TOK), lambda i: (i, half, 0)),
            pl.BlockSpec((TOK, model), lambda i: (i, half)),
            pl.BlockSpec((2 * KEYS, HD), lambda i: (0, 0)),
            pl.BlockSpec((DEPTH - HD, TOK), lambda i: (0, 0)),
        ],
        out_specs=[
            pl.BlockSpec((3 * model, TOK), lambda i: (0, i)),
            pl.BlockSpec((2 * KEYS, HD), lambda i: (0, 0)),
        ],
        out_shape=[
            jax.ShapeDtypeStruct((3 * model, slots * TOK), jnp.bfloat16),
            jax.ShapeDtypeStruct((2 * KEYS, HD), jnp.float32),
        ],
        scratch_shapes=[pltpu.VMEM((model, TOK), jnp.bfloat16)],
        compiler_params=pltpu.CompilerParams(vmem_limit_bytes=48 * MIB),
        cost_estimate=pl.CostEstimate(
            flops=slots * 4_000_000_000, bytes_accessed=slots * 4 * MIB, transcendentals=0
        ),
    )(project, weights, inverse, grad, tab, ind)


def write_placed(table_ref, kept_ref, sent_ref, core_stride, write):
    devices = table_ref.shape[0] - 1
    for core in (0, 1):

        @pl.when(table_ref[devices] == core)
        def _():
            def write_block(block, rows, value):
                place = table_ref[block]
                if block // core_stride % 2 == core:
                    kept_ref[place, rows] = value
                else:
                    sent_ref[place - devices // 2, rows] = value

            write(write_block)


def mlp_kernel(rows, begins, ends, placed, core_stride, *refs):
    if placed:
        table_ref, *refs = refs
    normed_ref, cot_ref, up_ref, down_ref, shift_ref, mixed0_ref, grad0_ref = refs[:7]
    last_ref, mixed_ref, grad_ref, dup_ref, ddown_ref, dshift_ref = refs[7:13]
    active_ref, hidden_ref = refs[13:15]
    sum_ref = refs[15] if ends else mixed_ref
    tokens = normed_ref.shape[0]
    step = pl.program_id(0) * pl.num_programs(1) + pl.program_id(1)

    @pl.when(step == 0)
    def _():
        sum_ref[...] = jnp.zeros_like(sum_ref)
        grad_ref[...] = jnp.zeros_like(grad_ref)

    piece = mixed0_ref.shape[0]

    @pl.when(step < tokens // piece)
    def _():
        place = pl.ds(pl.multiple_of(step * piece, piece), piece)
        sum_ref[place] += mixed0_ref[...]
        if not begins:
            grad_ref[place] += grad0_ref[...]

    up = up_ref[...]
    down = down_ref[...]
    shift = shift_ref[...]
    total = jnp.zeros(shift.shape, jnp.float32)
    for step_rows in range(tokens // rows):
        part = slice(step_rows * rows, (step_rows + 1) * rows)
        hidden = dot(normed_ref[part], up) + shift
        grad_active = dot_nt(cot_ref[part], down)
        half = 0.5 + 0.5 * lax.erf(hidden * 0.5**0.5)
        active = (hidden * half).astype(jnp.bfloat16)
        slope = half + hidden * jnp.exp(hidden * hidden * -0.5) * (2 * np.pi) ** -0.5
        grad_hidden = (grad_active * slope).astype(jnp.bfloat16)
        active_ref[part] = active
        hidden_ref[part] = grad_hidden
        total = total + jnp.sum(grad_hidden.astype(jnp.float32), axis=0, keepdims=True)
        sum_ref[part] += dot(active, down)
        grad_ref[part] += dot_nt(grad_hidden, up)
    dshift_ref[...] = total
    grad_down = dot_tn(active_ref[...], cot_ref[...]).astype(jnp.bfloat16)
    grad_up = dot_tn(normed_ref[...], hidden_ref[...]).astype(jnp.bfloat16)
    if not placed:
        ddown_ref[...] = grad_down
        dup_ref[...] = grad_up
    else:
        devices = table_ref.shape[0] - 1
        share, wide = grad_up.shape[0] // devices, grad_up.shape[1]
        steps = grad_up.shape[0] // wide
        for index in range(steps):

            @pl.when(pl.program_id(1) == index)
            def _():
                def write(write_block):
                    for block in range(devices):
                        part = grad_up[block * share : (block + 1) * share]
                        write_block(block, slice(index * share, (index + 1) * share), part)
                    for block in range(devices // steps):
                        part = grad_down[block * share : (block + 1) * share]
                        for n in range(steps):
                            low = (steps + n) * share
                            piece = part[:, n * wide : (n + 1) * wide]
                            place = index * devices // steps + block
                            write_block(place, slice(low, low + share), piece)

                write_placed(table_ref, ddown_ref, dup_ref, core_stride, write)
    if ends:

        @pl.when(step == pl.num_programs(0) * pl.num_programs(1) - 1)
        def _():
            mixed_ref[...] = (sum_ref[...] + last_ref[...]).astype(jnp.bfloat16)


def mlp(normed, cot, joint, shift, mixed0, grad0, last, first, count, table):
    tokens, model = normed.shape
    devices = table.shape[0] - 1
    share = model // devices
    steps = 2
    block = model // steps
    begins, ends = first == 0, first + count == PARTS
    placed = share % 8 == 0
    if placed:
        shape = (devices // 2, count * 2 * steps * share, block)
        shapes = [jax.ShapeDtypeStruct(shape, jnp.bfloat16)] * 2
        spec = pl.BlockSpec((devices // 2, 2 * steps * share, block), lambda p, i, *_: (0, p, 0))
        specs = [spec, spec]
    else:
        shapes = [
            jax.ShapeDtypeStruct((model, count * model), jnp.bfloat16),
            jax.ShapeDtypeStruct((count * model, model), jnp.bfloat16),
        ]
        specs = [
            pl.BlockSpec((model, block), lambda p, i, *_: (0, p * steps + i)),
            pl.BlockSpec((block, model), lambda p, i, *_: (p * steps + i, 0)),
        ]
    pieces = count * steps
    piece = pl.BlockSpec((tokens // pieces, model), lambda p, i, *_: (p * steps + i, 0))
    once = pl.Buffered(1)
    whole = pl.BlockSpec((tokens, model), lambda p, i, *_: (0, 0), pipeline_mode=once)
    core_stride = lax.axis_size("rows") * lax.axis_size("cols")
    mixed, grad, sent, kept, grad_shift = pl.pallas_call(
        functools.partial(mlp_kernel, tokens // 2, begins, ends, placed, core_stride),
        grid_spec=pltpu.PrefetchScalarGridSpec(
            num_scalar_prefetch=1 if placed else 0,
            grid=(count, steps),
            in_specs=[
                whole,
                whole,
                pl.BlockSpec((model, block), lambda p, i, *_: (0, (first + p) * steps + i)),
                pl.BlockSpec((block, model), lambda p, i, *_: (i, PARTS + first + p)),
                pl.BlockSpec((1, block), lambda p, i, *_: (0, (first + p) * steps + i)),
                piece,
                pl.BlockSpec((8, LANES), lambda p, i, *_: (0, 0)) if begins else piece,
                pl.BlockSpec((1, model), lambda p, i, *_: (0, 0)),
            ],
            out_specs=[
                whole,
                whole,
                specs[0],
                specs[1],
                pl.BlockSpec((1, block), lambda p, i, *_: (0, p * steps + i)),
            ],
            scratch_shapes=[pltpu.VMEM((tokens, block), jnp.bfloat16)] * 2
            + ([pltpu.VMEM((tokens, model), jnp.float32)] if ends else []),
        ),
        out_shape=[
            jax.ShapeDtypeStruct((tokens, model), jnp.bfloat16 if ends else jnp.float32),
            jax.ShapeDtypeStruct((tokens, model), jnp.float32),
            shapes[0],
            shapes[1],
            jax.ShapeDtypeStruct((1, count * model), jnp.float32),
        ],
        compiler_params=pltpu.CompilerParams(vmem_limit_bytes=62 * MIB),
        cost_estimate=pl.CostEstimate(
            flops=16 * tokens * model * model * count,
            bytes_accessed=8 * model * model * count + 24 * tokens * model,
            transcendentals=2 * tokens * model * count,
        ),
    )(*([table] if placed else []), normed, cot, joint, joint, shift, mixed0, grad0, last)
    if placed:
        return mixed, grad, (sent, kept), grad_shift
    down = kept.reshape(count, devices, share, model).transpose(1, 0, 2, 3)
    parts = [sent.reshape(devices, share, -1), down.reshape(devices, -1, model)]
    return mixed, grad, parts, grad_shift


def window_gradient_kernel(own, core_stride, table_ref, *refs):
    tokens_ref, grad_ref, *ready, sent_ref, kept_ref, sums_ref = refs
    devices = table_ref.shape[0] - 1
    share = tokens_ref.shape[0] // devices
    step = pl.program_id(0)

    def place(value):
        def write(write_block):
            for block in range(devices):
                part = value[block * share : (block + 1) * share]
                write_block(block, slice(0, share), part)

        write_placed(table_ref, kept_ref, sent_ref, core_stride, write)

    @pl.when(step < own)
    def _():
        grad = grad_ref[...]
        place(dot_nt(tokens_ref[...], grad).astype(jnp.bfloat16))
        sums_ref[...] = dot_nt(jnp.ones((8, grad.shape[1]), jnp.bfloat16), grad)

    for ready_ref in ready:

        @pl.when(step >= own)
        def _():
            place(ready_ref[...])


def window_gradient(turned, grad, ready, table):
    model, tokens = turned.shape
    devices = table.shape[0] - 1
    wide = model // 2
    own = grad.shape[0] // wide
    steps = own + sum(one.shape[1] // wide for one in ready)
    shape = jax.ShapeDtypeStruct((devices // 2, model // devices, steps * wide), jnp.bfloat16)
    spec = pl.BlockSpec((devices // 2, model // devices, wide), lambda n, *_: (0, 0, n))
    core_stride = lax.axis_size("rows") * lax.axis_size("cols")
    return pl.pallas_call(
        functools.partial(window_gradient_kernel, own, core_stride),
        grid_spec=pltpu.PrefetchScalarGridSpec(
            num_scalar_prefetch=1,
            grid=(steps,),
            in_specs=[
                pl.BlockSpec((model, tokens), lambda n, *_: (0, 0), pipeline_mode=pl.Buffered(1)),
                pl.BlockSpec((wide, tokens), lambda n, *_: (jnp.minimum(n, own - 1), 0)),
            ]
            + [pl.BlockSpec((model, wide), lambda n, *_: (0, jnp.maximum(n - own, 0)))] * len(ready),
            out_specs=[
                spec,
                spec,
                pl.BlockSpec((8, wide), lambda n, *_: (0, jnp.minimum(n, own - 1))),
            ],
        ),
        out_shape=[shape, shape, jax.ShapeDtypeStruct((8, own * wide), jnp.float32)],
        compiler_params=pltpu.CompilerParams(vmem_limit_bytes=56 * MIB),
        cost_estimate=pl.CostEstimate(
            flops=2 * tokens * model * own * wide,
            bytes_accessed=2 * (tokens * model + tokens * own * wide + model * steps * wide),
            transcendentals=0,
        ),
    )(table, turned, grad, *ready)


def hidden_parts(unit):
    return 5 if unit % 160 == 0 else 1


def normalised(values):
    average = jnp.mean(values, axis=-1, keepdims=True)
    centered = values - average
    variance = jnp.mean(centered * centered, axis=-1, keepdims=True)
    inverse = lax.rsqrt(variance + eps)
    return centered * inverse, inverse


def norm_backward(unit, inverse, gain, grad):
    scaled = grad * gain
    return inverse * (
        scaled
        - jnp.mean(scaled, axis=-1, keepdims=True)
        - unit * jnp.mean(scaled * unit, axis=-1, keepdims=True)
    )


def column_sum(value):
    return jnp.sum(value, axis=0, keepdims=True)


def row_block(tokens):
    return tokens // 4


def row_norm_kernel(rows_ref, vectors_ref, out_ref):
    unit, _ = normalised(rows_ref[...].astype(jnp.float32))
    out_ref[...] = (unit * vectors_ref[0:1] + vectors_ref[1:2]).astype(jnp.bfloat16)


def row_norm(rows, vectors):
    tokens, model = rows.shape
    block = pl.BlockSpec((row_block(tokens), model), lambda i: (i, 0))
    return pl.pallas_call(
        row_norm_kernel,
        grid=(4,),
        in_specs=[block, pl.BlockSpec((8, model), lambda i: (0, 0))],
        out_specs=block,
        out_shape=jax.ShapeDtypeStruct((tokens, model), jnp.bfloat16),
        cost_estimate=pl.CostEstimate(
            flops=8 * tokens * model, bytes_accessed=4 * tokens * model, transcendentals=0
        ),
    )(rows, vectors)


def middle_kernel(attended_ref, proj_ref, image_ref, vectors_ref, middle_ref, normed_ref):
    branch = dot(attended_ref[...], proj_ref[...]) + vectors_ref[0:1]
    middle = image_ref[...].astype(jnp.float32) + branch
    unit, _ = normalised(middle)
    normed = (unit * vectors_ref[1:2] + vectors_ref[2:3]).astype(jnp.bfloat16)
    middle_ref[...] = middle
    normed_ref[...] = normed


def middle_forward(attended, proj, image, vectors):
    tokens, model = attended.shape
    rows = row_block(tokens)
    block = pl.BlockSpec((rows, model), lambda i: (i, 0))
    return pl.pallas_call(
        middle_kernel,
        grid=(tokens // rows,),
        in_specs=[
            block,
            pl.BlockSpec((model, model), lambda i: (0, 2 * PARTS)),
            block,
            pl.BlockSpec((8, model), lambda i: (0, 0)),
        ],
        out_specs=[block, block],
        out_shape=[
            jax.ShapeDtypeStruct((tokens, model), jnp.float32),
            jax.ShapeDtypeStruct((tokens, model), jnp.bfloat16),
        ],
        compiler_params=pltpu.CompilerParams(vmem_limit_bytes=40 * MIB),
        cost_estimate=pl.CostEstimate(
            flops=2 * tokens * model * model, bytes_accessed=12 * tokens * model, transcendentals=0
        ),
    )(attended, proj, image, vectors)


def middle_backward_kernel(
    grad_ref, middle_ref, cot_ref, attended_ref, proj_ref, vectors_ref,
    grad_middle_ref, grad_attended_ref, dproj_ref, sums_ref, total_ref,
):
    step = pl.program_id(0)

    @pl.when(step == 0)
    def _():
        sums_ref[...] = jnp.zeros_like(sums_ref)
        total_ref[...] = jnp.zeros_like(total_ref)

    middle = middle_ref[...]
    unit, inverse = normalised(middle)
    grad = grad_ref[...]
    cot = cot_ref[...].astype(jnp.float32)
    grad_middle = cot + norm_backward(unit, inverse, vectors_ref[1:2], grad)
    branch = grad_middle.astype(jnp.bfloat16)
    grad_middle_ref[...] = grad_middle
    grad_attended_ref[...] = dot_nt(branch, proj_ref[...]).astype(jnp.bfloat16)
    total_ref[...] += dot_tn(attended_ref[...], branch)
    sums_ref[0:1] += column_sum(branch.astype(jnp.float32))
    sums_ref[1:2] += column_sum(grad * unit)
    sums_ref[2:3] += column_sum(grad)
    sums_ref[3:4] += column_sum(cot)

    @pl.when(step == pl.num_programs(0) - 1)
    def _():
        dproj_ref[...] = total_ref[...].astype(jnp.bfloat16)


def middle_backward(grad, middle, cot, attended, proj, vectors):
    tokens, model = attended.shape
    rows = row_block(tokens)
    block = pl.BlockSpec((rows, model), lambda i: (i, 0))
    few = pl.BlockSpec((8, model), lambda i: (0, 0))
    return pl.pallas_call(
        middle_backward_kernel,
        grid=(tokens // rows,),
        in_specs=[
            block, block, block, block,
            pl.BlockSpec((model, model), lambda i: (0, 2 * PARTS)),
            few,
        ],
        out_specs=[block, block, pl.BlockSpec((model, model), lambda i: (0, 0)), few],
        out_shape=[
            jax.ShapeDtypeStruct((tokens, model), jnp.float32),
            jax.ShapeDtypeStruct((tokens, model), jnp.bfloat16),
            jax.ShapeDtypeStruct((model, model), jnp.bfloat16),
            jax.ShapeDtypeStruct((8, model), jnp.float32),
        ],
        scratch_shapes=[pltpu.VMEM((model, model), jnp.float32)],
        compiler_params=pltpu.CompilerParams(vmem_limit_bytes=56 * MIB),
        cost_estimate=pl.CostEstimate(
            flops=4 * tokens * model * model, bytes_accessed=24 * tokens * model, transcendentals=0
        ),
    )(grad, middle, cot, attended, proj, vectors)


def image_backward_kernel(
    rows_ref, first_ref, second_ref, grad_middle_ref, vectors_ref, out_ref, sums_ref
):
    @pl.when(pl.program_id(0) == 0)
    def _():
        sums_ref[...] = jnp.zeros_like(sums_ref)

    unit, inverse = normalised(rows_ref[...].astype(jnp.float32))
    grad = first_ref[...].astype(jnp.float32) + second_ref[...].astype(jnp.float32)
    total = grad_middle_ref[...] + norm_backward(unit, inverse, vectors_ref[0:1], grad)
    out_ref[...] = total.astype(jnp.bfloat16)
    sums_ref[0:1] += column_sum(grad * unit)
    sums_ref[1:2] += column_sum(grad)


def image_backward(rows, first, second, grad_middle, vectors):
    tokens, model = rows.shape
    block = pl.BlockSpec((row_block(tokens), model), lambda i: (i, 0))
    few = pl.BlockSpec((8, model), lambda i: (0, 0))
    return pl.pallas_call(
        image_backward_kernel,
        grid=(4,),
        in_specs=[block, block, block, block, few],
        out_specs=[block, few],
        out_shape=[
            jax.ShapeDtypeStruct((tokens, model), jnp.bfloat16),
            jax.ShapeDtypeStruct((8, model), jnp.float32),
        ],
        cost_estimate=pl.CostEstimate(
            flops=12 * tokens * model, bytes_accessed=10 * tokens * model, transcendentals=0
        ),
    )(rows, first, second, grad_middle, vectors)


def main_place(width):
    col = lax.broadcasted_iota(jnp.int32, (width, NWIN * SIDE), 0)
    slot = lax.broadcasted_iota(jnp.int32, (width, NWIN * SIDE), 1)
    inside = slot % SIDE < WIN
    return (inside & (col == slot // SIDE * WIN + slot % SIDE)).astype(jnp.bfloat16)


def end_starts(width, count):
    starts = [b * WIN // 8 * 8 for b in range(count - 1)]
    return starts + [width - END]


def end_place(width):
    count = lax.axis_size("rows")
    row = lax.axis_index("rows")
    start = jnp.array(end_starts(width, count))[row]
    col = start + lax.broadcasted_iota(jnp.int32, (END, 2 * SIDE), 0)
    slot = lax.broadcasted_iota(jnp.int32, (END, 2 * SIDE), 1)
    held = (slot % SIDE < WIN) & ((slot < SIDE) | (row == count - 1))
    window = row + slot // SIDE
    return (held & (col == window * WIN + slot % SIDE)).astype(jnp.bfloat16)


def to_windows_kernel(width, rest, rows_ref, main_ref, end_ref, out_ref):
    out_ref[...] = jnp.zeros_like(out_ref)
    for i in range(WIN):
        part = dot_tn(main_ref[...], rows_ref[i * width : (i + 1) * width]).astype(jnp.bfloat16)
        for b in range(NWIN):
            out_ref[b * TOK + i * SIDE : b * TOK + (i + 1) * SIDE] = part[b * SIDE : (b + 1) * SIDE]
    first = WIN * width
    for i in range(rest):
        part = rows_ref[first + i * END : first + (i + 1) * END]
        part = dot_tn(end_ref[...], part).astype(jnp.bfloat16)
        for b in range(2):
            place = (NWIN + b) * TOK + i * SIDE
            out_ref[place : place + SIDE] = part[b * SIDE : (b + 1) * SIDE]


def to_rows_kernel(width, rest, windows_ref, main_ref, end_ref, out_ref):
    for i in range(WIN):
        part = jnp.concatenate(
            [windows_ref[b * TOK + i * SIDE : b * TOK + (i + 1) * SIDE] for b in range(NWIN)],
            axis=0,
        )
        out_ref[i * width : (i + 1) * width] = dot(main_ref[...], part).astype(jnp.bfloat16)
    first = WIN * width
    for i in range(rest):
        part = jnp.concatenate(
            [
                windows_ref[b * TOK + i * SIDE : b * TOK + (i + 1) * SIDE]
                for b in range(NWIN, NWIN + 2)
            ],
            axis=0,
        )
        part = dot(end_ref[...], part).astype(jnp.bfloat16)
        out_ref[first + i * END : first + (i + 1) * END] = part


def rearranged(kernel, value, width, rest, tokens):
    model = value.shape[1]
    lanes = model // 5
    main, end = main_place(width), end_place(width)
    return pl.pallas_call(
        functools.partial(kernel, width, rest),
        grid=(5,),
        in_specs=[
            pl.BlockSpec((value.shape[0], lanes), lambda i: (0, i)),
            pl.BlockSpec(main.shape, lambda i: (0, 0)),
            pl.BlockSpec(end.shape, lambda i: (0, 0)),
        ],
        out_specs=pl.BlockSpec((tokens, lanes), lambda i: (0, i)),
        out_shape=jax.ShapeDtypeStruct((tokens, model), jnp.bfloat16),
        compiler_params=pltpu.CompilerParams(vmem_limit_bytes=32 * MIB),
        cost_estimate=pl.CostEstimate(
            flops=200 * tokens * model, bytes_accessed=6 * tokens * model, transcendentals=0
        ),
    )(value, main, end)


def axis_bits(axis):
    count = lax.axis_size(axis)
    return [(axis, 1 << bit) for bit in range(count.bit_length() - 1)]


def flipped(value, bit):
    axis, mask = bit
    return lax.ppermute(value, axis, [(i, i ^ mask) for i in range(lax.axis_size(axis))])


def bit_of(bit):
    axis, mask = bit
    return (lax.axis_index(axis) // mask) % 2


def device_bits():
    return [bit for axis in ALL for bit in reversed(axis_bits(axis))]


def after(value, others):
    return lax.optimization_barrier((value, others))[0]


def beside(flights, value, kernel):
    return sync(kernel(launch(value, flights)), flights)


class Flight:

    def __init__(self, steps):
        self.steps = steps
        self.sent = self.arrived = self.value = None
        self.flying = True

    def advance(self):
        try:
            self.sent, self.arrived = self.steps.send(self.arrived)
        except StopIteration as end:
            self.sent, self.arrived, self.flying = [], [], False
            self.value = end.value

    def finish(self):
        while self.flying:
            self.advance()
        return self.value


def launch(value, flights):
    for one in flights:
        if one.flying:
            one.advance()
    return after(value, [one.sent for one in flights])


def sync(value, flights):
    flights = [one for one in flights if one.flying]
    value, arrived = lax.optimization_barrier((value, [one.arrived for one in flights]))
    for one, pieces in zip(flights, arrived):
        one.arrived = pieces
    return value


def index_masks(bits):
    weights = {"cols": 1, "rows": lax.axis_size("cols")}
    weights["dp"] = weights["rows"] * lax.axis_size("rows")
    return [weights[axis] * mask for axis, mask in bits]


def halving_orders():
    dp, rows, cols = axis_bits("dp"), axis_bits("rows"), axis_bits("cols")
    core, chips = dp[:1], dp[1:]
    (core,) = index_masks(core)
    orders = [cols + chips + rows, chips + rows[:1] + cols + rows[1:]]
    return core, [index_masks(order) for order in orders]


def block_tables():
    core, orders = halving_orders()
    me = lax.axis_index(ALL)
    steps = len(orders[0])
    flips = []
    for order in orders:
        place = np.arange(1 << steps)
        flips.append(sum((place >> (steps - 1 - n) & 1) * mask for n, mask in enumerate(order)))
    flips = [jnp.asarray(flip, jnp.int32) for flip in flips]
    first = (me & core) == 0
    there = (me ^ core) ^ jnp.where(first, flips[1], flips[0])
    here = me ^ jnp.where(first, flips[0], flips[1])
    return there, here


def place_table():
    there, here = block_tables()
    blocks = jnp.concatenate([here, there])
    count = blocks.shape[0]
    hit = blocks[:, None] == jnp.arange(count)[None, :]
    places = jnp.sum(jnp.where(hit, jnp.arange(count)[:, None], 0), axis=0)
    core, _ = halving_orders()
    return jnp.concatenate([places, (lax.axis_index(ALL) // core % 2)[None]]).astype(jnp.int32)


def partner_permute(value, step):
    core, orders = halving_orders()
    pairs = []
    for index in range(lax.axis_size(ALL)):
        order = orders[(index & core) // core]
        pairs.append((index, index ^ (core if step == 0 else order[step - 1])))
    return lax.ppermute(value, ALL, pairs)


def packed_shape(parts):
    if len({part.shape[1] for part in parts}) == 1:
        return parts[0].shape[1], sum(part.shape[2] for part in parts)
    wide = 2 * LANES
    return sum(part.shape[1] * part.shape[2] // wide for part in parts), wide


def pack_into(refs, write):
    rows, wide = packed_shape(refs)
    side = rows == refs[0].shape[1]
    place = 0
    for ref in refs:
        height, width = ref.shape[1:]
        if side:
            write(slice(0, rows), slice(place, place + width), ref[0])
            place += width
            continue
        for low in range(0, width, wide):
            write(slice(place, place + height), slice(0, wide), ref[0, :, low : low + wide])
            place += height


def pack_kernel(table_ref, *refs):
    def write(rows, cols, value):
        refs[-1][0, rows, cols] = value

    pack_into(refs[:-1], write)


def pack(parts, table):
    count = table.shape[0]
    rows, wide = packed_shape(parts)
    return pl.pallas_call(
        pack_kernel,
        grid_spec=pltpu.PrefetchScalarGridSpec(
            num_scalar_prefetch=1,
            grid=(count,),
            in_specs=[
                pl.BlockSpec((1,) + part.shape[1:], lambda i, table: (table[i], 0, 0))
                for part in parts
            ],
            out_specs=pl.BlockSpec((1, rows, wide), lambda i, table: (i, 0, 0)),
        ),
        out_shape=jax.ShapeDtypeStruct((count, rows, wide), jnp.bfloat16),
        cost_estimate=pl.CostEstimate(
            flops=0, bytes_accessed=4 * count * rows * wide, transcendentals=0
        ),
    )(table, *parts)


def summed(sent, kept):
    held = [kept]
    size = 2 * kept.shape[0]
    step = 0
    while size > 1:
        if step:
            sent = sum(piece[size // 2 : size].astype(jnp.float32) for piece in held)
            sent = sent.astype(jnp.bfloat16)
        held = yield [sent], [partner_permute(sent, step)] + held
        size //= 2
        step += 1
    return sum(piece[0].astype(jnp.float32) for piece in held)


def summed_packed(parts):
    there, here = block_tables()
    total = yield from summed(pack(parts, there), pack(parts, here))
    shapes = [part.shape[1:] for part in parts]
    rows, wide = packed_shape(parts)
    out = []
    place = 0
    for height, width in shapes:
        if rows == height:
            out.append(total[:, place : place + width])
            place += width
        else:
            pieces = width // wide
            piece = total[place : place + pieces * height].reshape(pieces, height, wide)
            out.append(piece.transpose(1, 0, 2).reshape(height, width))
            place += pieces * height
    return out


def summed_mlp(parts, share):
    total = yield from summed(*parts)
    wide = total.shape[1]
    total = total.reshape(-1, 2, 2, share, wide)
    up = total[:, 0].transpose(2, 0, 1, 3).reshape(share, -1)
    down = total[:, 1].transpose(0, 2, 1, 3).reshape(-1, 2 * wide)
    return [up, down]


def summed_columns(sent, kept, widths):
    total = yield from summed(sent, kept)
    places = np.cumsum([0] + list(widths))
    return [total[:, low : low + width] for low, width in zip(places, widths)]


def all_sum(value):
    for bit in reversed(device_bits()):
        value = value + flipped(value, bit)
    return value


def small_gather(value):
    for bit in reversed(device_bits()):
        arrived = flipped(value, bit)
        value = jnp.where(
            bit_of(bit) == 0,
            jnp.concatenate([value, arrived], axis=0),
            jnp.concatenate([arrived, value], axis=0),
        )
    return value


SWAP = [(0, 1), (1, 0)]


def split_tiles(tiles):
    col = lax.axis_index("cols")
    kept = lax.dynamic_index_in_dim(tiles, col, 0, keepdims=False)
    sent = lax.dynamic_index_in_dim(tiles, 1 - col, 0, keepdims=False)
    return kept, sent, lax.ppermute(sent, "cols", SWAP)


def join_tiles(kept, arrived):
    return jnp.where(
        lax.axis_index("cols") == 0,
        jnp.concatenate([kept, arrived], axis=1),
        jnp.concatenate([arrived, kept], axis=1),
    )


def split_image(image):
    col = lax.axis_index("cols")
    width = image.shape[1] // 2
    kept = lax.dynamic_slice_in_dim(image, col * width, width, 1)
    sent = lax.dynamic_slice_in_dim(image, (1 - col) * width, width, 1)
    return kept, sent, lax.ppermute(sent, "cols", SWAP)


def join_image(kept, arrived):
    return jnp.where(
        lax.axis_index("cols") == 0, jnp.stack([kept, arrived]), jnp.stack([arrived, kept])
    )


def halves_to_image(tiles):
    kept, _, arrived = split_tiles(tiles)
    return join_tiles(kept, arrived)


def image_to_halves(image):
    kept, _, arrived = split_image(image)
    return join_image(kept, arrived)


def column_windows(rows):
    width = rows.shape[1]
    parts = []
    for b in range(NWIN):
        piece = rows[:, b * WIN : min((b + 1) * WIN, width)]
        parts.append(jnp.pad(piece, ((0, 0), (0, SIDE - piece.shape[1]), (0, 0))))
    return jnp.stack(parts)


def column_rows(windows, width):
    parts = [windows[b, :, : min(WIN, width - b * WIN)] for b in range(len(windows))]
    return jnp.concatenate(parts, axis=1)


def pad_rows(value, top, bottom):
    widths = [(0, 0)] * value.ndim
    widths[-3] = (top, bottom)
    return jnp.pad(value, widths)


class Layout:

    def __init__(self, tiles):
        self.tiles = tiles
        _, self.height, tile_w, self.model = tiles
        self.width = 2 * tile_w
        self.count = lax.axis_size("rows")
        self.row = lax.axis_index("rows")
        self.near = self.count == NWIN - 1
        self.step = self.height - WIN
        self.halo = self.step * (self.count - 1)
        self.rest = self.height * self.count - WIN * self.count
        if self.near:
            self.slots = NWIN + 2
            self.tokens = WIN * self.width + self.rest * END
        else:
            self.slots = -(-NWIN * NWIN // self.count)
            self.tokens = 2 * self.height * tile_w

    def enter(self, tiles):
        if not self.near:
            return tiles.reshape(self.tokens, self.model)
        last, rest, halo = self.count - 1, self.rest, self.halo
        top = self.height - rest
        kept_low, sent_low, low = split_tiles(tiles[:, top:])
        kept_up, sent_up, up = split_tiles(tiles[:, :top])
        low, up = yield [sent_low, sent_up], [low, up]
        lower = join_tiles(kept_low, low)
        upper = join_tiles(kept_up, up)
        starts = end_starts(self.width, self.count)
        sent = [lower[rest - halo :]]
        arrived = [lax.ppermute(sent[0], "rows", [(i, i + 1) for i in range(last)])]
        for target in range(last):
            sent.append(lower[:, starts[target] : starts[target] + END])
            arrived.append(lax.ppermute(sent[-1], "rows", [(last, target)]))
        down, *arrived = yield sent, arrived
        end = lower[:, starts[last] :]
        for target in range(last):
            end = jnp.where(self.row == target, arrived[target], end)
        held = jnp.sum(end_place(self.width), axis=1).astype(jnp.bfloat16)
        end = end * held[None, :, None]
        whole = jnp.concatenate([down, upper, lower], axis=0)
        main = lax.dynamic_slice_in_dim(whole, halo - self.step * self.row, WIN, 0)
        return jnp.concatenate(
            [main.reshape(-1, self.model), end.reshape(-1, self.model)], axis=0
        )

    def leave(self, tokens):
        if not self.near:
            return tokens.reshape(self.tiles)
        last, rest, halo = self.count - 1, self.rest, self.halo
        top = self.height - rest
        main = tokens[: WIN * self.width].reshape(WIN, self.width, self.model)
        end = tokens[WIN * self.width :].reshape(rest, END, self.model)
        held = jnp.sum(end_place(self.width), axis=1).astype(jnp.bfloat16)
        end = end * held[None, :, None]
        up = lax.ppermute(main[:halo], "rows", [(i + 1, i) for i in range(last)])
        pieces = [lax.ppermute(end, "rows", [(source, last)]) for source in range(last)]
        upper = lax.dynamic_slice_in_dim(main, self.step * self.row, top, 0)
        kept_up, sent_up, arrived_up = split_image(upper)
        up, arrived_up, *pieces = yield [end, sent_up], [up, arrived_up] + pieces
        tail = 0
        for start, piece in zip(end_starts(self.width, self.count), pieces + [end]):
            tail = tail + jnp.pad(piece, ((0, 0), (start, self.width - END - start), (0, 0)))
        below = jnp.where(self.row == last, tail, pad_rows(up, 0, rest - halo))
        whole = jnp.concatenate([main, below], axis=0)
        place = self.step * self.row + top
        kept_low, sent_low, arrived_low = split_image(
            lax.dynamic_slice_in_dim(whole, place, rest, 0)
        )
        (arrived_low,) = yield [sent_low], [arrived_low]
        upper = join_image(kept_up, arrived_up)
        lower = join_image(kept_low, arrived_low)
        return jnp.concatenate([upper, lower], axis=1)

    def to_windows(self, tokens):
        if self.near:
            total = self.slots * TOK
            return rearranged(to_windows_kernel, tokens, self.width, self.rest, total)
        windows = column_windows(halves_to_image(tokens.reshape(self.tiles)))
        windows = lax.all_gather(windows, "rows", axis=1, tiled=True)
        extra = NWIN * WIN - windows.shape[1]
        windows = jnp.pad(windows, ((0, 0), (0, extra), (0, 0), (0, 0)))
        windows = windows.reshape(NWIN, NWIN, WIN, SIDE, self.model).transpose(1, 0, 2, 3, 4)
        windows = windows.reshape(NWIN * NWIN, WIN, SIDE, self.model)
        extra = self.slots * self.count - NWIN * NWIN
        windows = jnp.pad(windows, ((0, extra), (0, SIDE - WIN), (0, 0), (0, 0)))
        windows = lax.dynamic_slice_in_dim(windows, self.row * self.slots, self.slots, 0)
        return windows.reshape(self.slots * TOK, self.model)

    def to_rows(self, windows):
        if self.near:
            return rearranged(to_rows_kernel, windows, self.width, self.rest, self.tokens)
        windows = windows.reshape(self.slots, SIDE, SIDE, self.model)
        windows = lax.all_gather(windows[:, :WIN], "rows", axis=0, tiled=True)
        windows = windows[: NWIN * NWIN].reshape(NWIN, NWIN, WIN, SIDE, self.model)
        windows = windows.transpose(1, 0, 2, 3, 4).reshape(NWIN, NWIN * WIN, SIDE, self.model)
        windows = lax.dynamic_slice_in_dim(windows, self.row * self.height, self.height, 1)
        return image_to_halves(column_rows(windows, self.width)).reshape(self.tokens, self.model)


def shards(
    image_in,
    ln1_gain,
    ln1_bias,
    w_qkv,
    qv_bias,
    rel_rows,
    rel_cols,
    w_proj,
    proj_bias,
    ln2_gain,
    ln2_bias,
    w_fc1,
    fc1_bias,
    w_fc2,
    fc2_bias,
    cotangent,
):
    devices = lax.axis_size(ALL)
    me = lax.axis_index(ALL)
    model = image_in.shape[3]
    layout = Layout(image_in.shape)
    tokens = layout.tokens
    share = model // devices
    unit = fc1_bias.shape[0]

    rows = Flight(layout.enter(image_in))
    cot = Flight(layout.enter(cotangent))
    rows.advance()

    def gathered(shard):
        return lax.all_gather(shard, ALL, axis=0, tiled=True)

    vectors = [ln1_gain, ln1_bias, qv_bias[:, 0], qv_bias[:, 1], proj_bias, ln2_gain, ln2_bias]
    vectors = small_gather(jnp.concatenate(vectors + [fc2_bias, fc1_bias])[None])
    vectors = vectors.astype(jnp.float32)
    gain1, shift1, query_shift, value_shift, proj_shift, gain2, shift2, down_shift = (
        vectors[:, n * share : (n + 1) * share].reshape(1, model) for n in range(8)
    )
    norm_vectors = jnp.pad(jnp.concatenate([gain1, shift1], axis=0), ((0, 6), (0, 0)))
    middle_vectors = jnp.concatenate([proj_shift, gain2, shift2, down_shift], axis=0)
    middle_vectors = jnp.pad(middle_vectors, ((0, 4), (0, 0)))
    up_shift = vectors[:, 8 * share :].reshape(devices, PARTS, share)
    up_shift = up_shift.transpose(1, 0, 2).reshape(1, devices * unit)
    half = model // 2
    thirds = [w_qkv[:, n * half : (n + 1) * half] for n in (0, 2, 4, 1, 3, 5)]
    qkv_full = gathered(jnp.concatenate(thirds, axis=1))
    up_shard = w_fc1.reshape(share, devices, PARTS, share).transpose(0, 2, 1, 3)
    down_shard = [w_fc2[n * share : (n + 1) * share] for n in range(PARTS)]
    joint = gathered(
        jnp.concatenate([up_shard.reshape(share, devices * unit)] + down_shard + [w_proj], axis=1)
    )

    norm_vectors = sync(norm_vectors, [rows])
    norm_vectors = launch(norm_vectors, [rows, cot])
    norm_vectors = sync(norm_vectors, [rows])
    rows = rows.finish()
    window_tokens = layout.to_windows(row_norm(rows, norm_vectors))
    turned_tokens = window_tokens.T
    nothing = jnp.zeros((1, half), jnp.float32)
    shift_qkv = jnp.concatenate(
        [query_shift[:, :half], nothing, value_shift[:, :half]]
        + [query_shift[:, half:], nothing, value_shift[:, half:]],
        axis=1,
    )
    project = lax.dot_general(
        qkv_full, window_tokens, (((0,), (1,)), ((), ())), preferred_element_type=jnp.float32
    )
    project = (project + shift_qkv.reshape(3 * model, 1)).astype(jnp.bfloat16)
    project = sync(project, [cot])
    project = launch(project, [cot])
    tab = wide_tables(rel_rows, rel_cols)
    ind = key_indicator()
    attended_windows, weights, inverse = attention_forward(project, tab, ind)
    attended = layout.to_rows(attended_windows)
    attended, cot, turned_tokens, joint = sync(
        (attended, cot.finish(), turned_tokens, joint), []
    )
    middle, normed2 = middle_forward(attended, joint, rows, middle_vectors)

    mixed = middle
    grad_normed2 = jnp.zeros((8, LANES), jnp.float32)
    table = place_table()
    sums = []
    shifts = []
    for first, count in ((0, 2), (2, 2)):

        def step(normed2):
            return mlp(
                normed2,
                cot,
                joint,
                up_shift,
                mixed,
                grad_normed2,
                down_shift,
                first,
                count,
                table,
            )

        mixed, grad_normed2, blocks, grad_shift = beside(sums, normed2, step)
        shifts.append(grad_shift.reshape(count, devices, share))
        if isinstance(blocks, list):
            sums.append(Flight(summed_packed(blocks)))
        else:
            sums.append(Flight(summed_mlp(blocks, share)))

    output = Flight(layout.leave(mixed))
    grad_normed2 = launch(grad_normed2, sums)
    grad_middle, grad_attended, grad_proj, middle_sums = sync(
        middle_backward(grad_normed2, middle, cot, attended, joint, middle_vectors), sums[1:]
    )

    def rows_of(vector):
        return vector.reshape(devices, -1)

    def attention_step(half):
        return attention_backward(project, weights, inverse, grad_windows, tab, ind, half)

    def project_step(grad_project, half):
        return lax.dot_general(
            grad_project,
            qkv_full[:, half * 3 * model // 2 : (half + 1) * 3 * model // 2],
            (((0,), (1,)), ((), ())),
            preferred_element_type=jnp.float32,
        ).astype(jnp.bfloat16)

    grad_windows = layout.to_windows(launch(grad_attended, sums[1:] + [output]))
    grad_project, grad_tab = sync(attention_step(0), sums[:1])
    grad_project = launch(grad_project, sums[:1])
    sent, kept, sums0 = sync(
        window_gradient(turned_tokens, grad_project, [grad_proj], table), sums[1:] + [output]
    )
    sums.append(Flight(summed_columns(sent, kept, [3 * half, model])))
    grad_project = launch(grad_project, sums[1:] + [output])
    first_rows = layout.to_rows(project_step(grad_project, 0))
    first_rows, grad_windows = sync((first_rows, grad_windows), sums[:1] + sums[-1:])
    grad_windows = launch(grad_windows, sums[:1] + sums[-1:])
    grad_project, grad_part = sync(attention_step(1), sums + [output])
    grad_project = launch(grad_project, sums + [output])
    sent, kept, sums1 = window_gradient(turned_tokens, grad_project, [], table)
    sums.append(Flight(summed_columns(sent, kept, [3 * half])))
    grad_project = launch(grad_project, sums[-1:])
    second_rows = sync(project_step(grad_project, 1), sums)
    second_rows = layout.to_rows(launch(second_rows, sums))
    grad_tab = grad_tab + grad_part
    grad_sums = [sums0[0], sums1[0]]
    grad_rows, norm_sums = image_backward(
        rows, first_rows, second_rows, grad_middle, norm_vectors
    )
    grad_rows, norm_sums = sync((grad_rows, norm_sums), sums)
    grad_in = Flight(layout.leave(grad_rows))
    norm_sums = launch(norm_sums, sums + [grad_in])

    up_shift_sums = jnp.concatenate(shifts, axis=0).transpose(1, 0, 2).reshape(devices, unit)
    small = jnp.concatenate(
        [
            rows_of(norm_sums[0]),
            rows_of(norm_sums[1]),
            rows_of(jnp.concatenate([piece[:half] for piece in grad_sums])),
            rows_of(jnp.concatenate([piece[2 * half :] for piece in grad_sums])),
        ]
        + [rows_of(middle_sums[n]) for n in range(4)]
        + [up_shift_sums],
        axis=1,
    )
    small, grad_tables = all_sum_pair(small, jnp.stack(narrow_tables(grad_tab)))
    small = lax.dynamic_index_in_dim(small, me, 0, keepdims=False)

    ups, downs = zip(*[one.finish() for one in sums[:-2]])
    (first_qkv, sum_proj), (last_qkv,) = (one.finish() for one in sums[-2:])
    grad_fc1 = jnp.concatenate([grad.reshape(share, -1, devices, share) for grad in ups], axis=1)
    thirds = [
        piece[:, n * half : (n + 1) * half] for n in range(3) for piece in (first_qkv, last_qkv)
    ]
    return (
        output.finish(),
        grad_in.finish().astype(jnp.float32),
        small[:share],
        small[share : 2 * share],
        jnp.concatenate(thirds, axis=1),
        jnp.stack([small[2 * share : 3 * share], small[3 * share : 4 * share]], axis=1),
        grad_tables[0],
        grad_tables[1],
        sum_proj,
        small[4 * share : 5 * share],
        small[5 * share : 6 * share],
        small[6 * share : 7 * share],
        grad_fc1.transpose(0, 2, 1, 3).reshape(share, devices * unit),
        small[8 * share :],
        jnp.concatenate(downs, axis=0),
        small[7 * share : 8 * share],
    )


def all_sum_pair(first, second):
    sizes = first.size
    joined = all_sum(jnp.concatenate([first.reshape(-1), second.reshape(-1)]))
    return joined[:sizes].reshape(first.shape), joined[sizes:].reshape(second.shape)


def solution(mesh):
    tile = P("dp", "rows", "cols", None)
    vector = P(ALL)
    matrix = P(ALL, None)
    in_specs = (
        tile, vector, vector, matrix, matrix, P(), P(), matrix, vector, vector, vector,
        matrix, vector, matrix, vector, tile,
    )
    out_specs = (
        tile, tile, vector, vector, matrix, matrix, P(), P(), matrix, vector, vector, vector,
        matrix, vector, matrix, vector,
    )
    return jax.shard_map(shards, mesh=mesh, in_specs=in_specs, out_specs=out_specs, check_vma=False)
```

```python
import functools

import jax
import jax.numpy as jnp
import numpy as np
from jax import lax
from jax.experimental import pallas as pl
from jax.experimental.pallas import tpu as pltpu
from jax.sharding import PartitionSpec as P

HEADS = 16
HALF = HEADS // 2
WIN = 14
NWIN = 5
SIDE = 16
HD = 80
KEYS = WIN * SIDE
TOK = SIDE * SIDE
LANES = 128
DEPTH = 128
REL = 2 * WIN - 1
NEG = -1e30
END = 24
ALL = ("dp", "rows", "cols")
MIB = 1024 * 1024
PARTS = 4

eps = 1e-06


def dot(a, b):
    return jnp.dot(a, b, preferred_element_type=jnp.float32)


def dot_nt(a, b):
    return lax.dot_general(a, b, (((1,), (1,)), ((), ())), preferred_element_type=jnp.float32)


def dot_tn(a, b):
    return lax.dot_general(a, b, (((0,), (0,)), ((), ())), preferred_element_type=jnp.float32)


def offset_onehot(dtype):
    a = jnp.arange(WIN)[:, None]
    i = jnp.arange(SIDE)[None, :]
    offset = jnp.where(i < WIN, a - i + WIN - 1, -1)
    return (offset[:, :, None] == jnp.arange(REL)).astype(dtype).reshape(KEYS, REL)


def wide_tables(rel_rows, rel_cols):
    onehot = offset_onehot(jnp.bfloat16)
    return jnp.concatenate(
        [dot(onehot, table).astype(jnp.bfloat16) for table in (rel_rows, rel_cols)], axis=0
    )


def narrow_tables(grad):
    onehot = offset_onehot(jnp.float32)
    return [
        lax.dot_general(
            onehot,
            grad[n * KEYS : (n + 1) * KEYS],
            (((0,), (0,)), ((), ())),
            precision=lax.Precision.HIGHEST,
        )
        for n in (0, 1)
    ]


def key_indicator():
    row = lax.broadcasted_iota(jnp.int32, (DEPTH - HD, TOK), 0)
    key = lax.broadcasted_iota(jnp.int32, (DEPTH - HD, TOK), 1)
    return ((row == key // SIDE) | (row - SIDE == key % SIDE)).astype(jnp.bfloat16)


def query_offsets(query, tab_ref, lane):
    halves = []
    for half in range(2):
        low = half * 8
        count = min(8, WIN - low)
        part = dot(
            tab_ref[low * SIDE : (low + count) * SIDE], query[:, half * LANES : (half + 1) * LANES]
        )
        rows = part[:SIDE]
        for a in range(1, count):
            rows = jnp.where(
                lane[:, :LANES] // SIDE == a, part[a * SIDE : (a + 1) * SIDE], rows
            )
        halves.append(rows)
    part = dot(tab_ref[KEYS:], query)
    cols = part[:SIDE]
    for b in range(1, WIN):
        cols = jnp.where(lane % SIDE == b, part[b * SIDE : (b + 1) * SIDE], cols)
    return jnp.concatenate(halves, axis=1), cols


def attention_forward_kernel(
    project_ref, tab_ref, ind_ref, attended_ref, weights_ref, inverse_ref, turned_ref
):
    model = turned_ref.shape[0]
    lane = lax.broadcasted_iota(jnp.int32, (SIDE, TOK), 1)
    sub = lax.broadcasted_iota(jnp.int32, (SIDE, TOK), 0)
    ind = ind_ref[...]
    scale = HD**-0.5
    zeros = jnp.zeros((DEPTH - HD - 2 * SIDE, TOK), jnp.bfloat16)
    for head in range(HEADS):
        low = head * HD
        place = head // HALF * 3 * model // 2 + head % HALF * HD
        query = project_ref[place : place + HD]
        key = project_ref[model // 2 + place : model // 2 + place + HD]
        value = project_ref[model + place : model + place + HD]
        rows, cols = query_offsets(query, tab_ref, lane)
        rows = (rows * HD**0.5).astype(jnp.bfloat16)
        cols = jnp.where(sub < WIN, cols * HD**0.5, NEG).astype(jnp.bfloat16)
        query_wide = jnp.concatenate([query, rows, cols, zeros], axis=0)
        key_wide = jnp.concatenate([key, ind], axis=0)
        scores = dot_tn(key_wide, query_wide)[:KEYS]
        maxima = jnp.max(scores, axis=0, keepdims=True)
        weights = jnp.exp((scores - maxima) * scale)
        inverse = 1.0 / jnp.sum(weights, axis=0, keepdims=True)
        weights = weights.astype(jnp.bfloat16)
        weights_ref[0, head] = weights
        inverse_ref[0, head : head + 1] = inverse
        attended = dot(value[:, :KEYS], weights)
        turned_ref[low : low + HD] = (attended * inverse).astype(jnp.bfloat16)
    attended_ref[...] = turned_ref[...].T


def attention_forward(project, tab, ind):
    model = project.shape[0] // 3
    slots = project.shape[1] // TOK
    return pl.pallas_call(
        attention_forward_kernel,
        grid=(slots,),
        in_specs=[
            pl.BlockSpec((3 * model, TOK), lambda i: (0, i)),
            pl.BlockSpec((2 * KEYS, HD), lambda i: (0, 0)),
            pl.BlockSpec((DEPTH - HD, TOK), lambda i: (0, 0)),
        ],
        out_specs=[
            pl.BlockSpec((TOK, model), lambda i: (i, 0)),
            pl.BlockSpec((1, HEADS, KEYS, TOK), lambda i: (i, 0, 0, 0)),
            pl.BlockSpec((1, HEADS, TOK), lambda i: (i, 0, 0)),
        ],
        out_shape=[
            jax.ShapeDtypeStruct((slots * TOK, model), jnp.bfloat16),
            jax.ShapeDtypeStruct((slots, HEADS, KEYS, TOK), jnp.bfloat16),
            jax.ShapeDtypeStruct((slots, HEADS, TOK), jnp.float32),
        ],
        scratch_shapes=[pltpu.VMEM((model, TOK), jnp.bfloat16)],
        compiler_params=pltpu.CompilerParams(vmem_limit_bytes=48 * MIB),
        cost_estimate=pl.CostEstimate(
            flops=slots * 7_000_000_000,
            bytes_accessed=slots * 6 * MIB,
            transcendentals=slots * HEADS * KEYS * TOK,
        ),
    )(project, tab, ind)


def attention_backward_kernel(
    project_ref, weights_ref, inverse_ref, grad_ref, tab_ref, ind_ref, out_ref, dtab_ref, turned_ref
):
    model = turned_ref.shape[0]
    lane = lax.broadcasted_iota(jnp.int32, (SIDE, TOK), 1)
    ind = ind_ref[...]
    tab = tab_ref[...]
    scale = HD**-0.5

    @pl.when(pl.program_id(0) == 0)
    def _():
        dtab_ref[...] = jnp.zeros_like(dtab_ref)

    turned_ref[...] = grad_ref[...].T
    total = jnp.zeros(dtab_ref.shape, jnp.float32)
    for head in range(HALF):
        low = head * HD
        query = project_ref[low : low + HD]
        key = project_ref[model + low : model + low + HD]
        value = project_ref[2 * model + low : 2 * model + low + HD]
        inverse = inverse_ref[0, head : head + 1]
        grad = (turned_ref[low : low + HD] * inverse).astype(jnp.bfloat16)
        weights = weights_ref[0, head]
        weights_float = weights.astype(jnp.float32)
        terms = weights_float * dot_tn(value, grad)[:KEYS]
        inner = jnp.sum(terms, axis=0, keepdims=True) * inverse
        grad_scores = (terms - weights_float * inner).astype(jnp.bfloat16)
        grad_value = dot_nt(grad, weights)
        grad_key = dot_nt(query, grad_scores) * scale
        key_wide = jnp.concatenate([key, ind], axis=0)
        grad_wide = dot(key_wide[:, :KEYS], grad_scores)
        rows = grad_wide[HD : HD + SIDE]
        cols = grad_wide[HD + SIDE : HD + 2 * SIDE]
        spread = jnp.concatenate(
            [jnp.where(lane // SIDE == a, rows, 0.0) for a in range(WIN)]
            + [jnp.where(lane % SIDE == b, cols, 0.0) for b in range(WIN)],
            axis=0,
        ).astype(jnp.bfloat16)
        grad_query = grad_wide[:HD] * scale + dot_tn(tab, spread)
        total = total + dot_nt(spread, query)
        out_ref[low : low + HD] = grad_query.astype(jnp.bfloat16)
        out_ref[model + low : model + low + HD, :KEYS] = grad_key.astype(jnp.bfloat16)
        out_ref[2 * model + low : 2 * model + low + HD, :KEYS] = grad_value.astype(jnp.bfloat16)
    out_ref[model:, KEYS:] = jnp.zeros((2 * model, TOK - KEYS), jnp.bfloat16)
    dtab_ref[...] += total


def attention_backward(project, weights, inverse, grad, tab, ind, half):
    model = project.shape[0] // 6
    slots = project.shape[1] // TOK
    return pl.pallas_call(
        attention_backward_kernel,
        grid=(slots,),
        in_specs=[
            pl.BlockSpec((3 * model, TOK), lambda i: (half, i)),
            pl.BlockSpec((1, HALF, KEYS, TOK), lambda i: (i, half, 0, 0)),
            pl.BlockSpec((1, HALF, TOK), lambda i: (i, half, 0)),
            pl.BlockSpec((TOK, model), lambda i: (i, half)),
            pl.BlockSpec((2 * KEYS, HD), lambda i: (0, 0)),
            pl.BlockSpec((DEPTH - HD, TOK), lambda i: (0, 0)),
        ],
        out_specs=[
            pl.BlockSpec((3 * model, TOK), lambda i: (0, i)),
            pl.BlockSpec((2 * KEYS, HD), lambda i: (0, 0)),
        ],
        out_shape=[
            jax.ShapeDtypeStruct((3 * model, slots * TOK), jnp.bfloat16),
            jax.ShapeDtypeStruct((2 * KEYS, HD), jnp.float32),
        ],
        scratch_shapes=[pltpu.VMEM((model, TOK), jnp.bfloat16)],
        compiler_params=pltpu.CompilerParams(vmem_limit_bytes=48 * MIB),
        cost_estimate=pl.CostEstimate(
            flops=slots * 4_000_000_000, bytes_accessed=slots * 4 * MIB, transcendentals=0
        ),
    )(project, weights, inverse, grad, tab, ind)


def write_placed(table_ref, kept_ref, sent_ref, core_stride, write):
    devices = table_ref.shape[0] - 1
    for core in (0, 1):

        @pl.when(table_ref[devices] == core)
        def _():
            def write_block(block, rows, value):
                place = table_ref[block]
                if block // core_stride % 2 == core:
                    kept_ref[place, rows] = value
                else:
                    sent_ref[place - devices // 2, rows] = value

            write(write_block)


def mlp_kernel(rows, begins, ends, placed, core_stride, *refs):
    if placed:
        table_ref, *refs = refs
    normed_ref, cot_ref, up_ref, down_ref, shift_ref, mixed0_ref, grad0_ref = refs[:7]
    last_ref, mixed_ref, grad_ref, dup_ref, ddown_ref, dshift_ref = refs[7:13]
    active_ref, hidden_ref = refs[13:15]
    sum_ref = refs[15] if ends else mixed_ref
    tokens = normed_ref.shape[0]
    step = pl.program_id(0) * pl.num_programs(1) + pl.program_id(1)

    @pl.when(step == 0)
    def _():
        sum_ref[...] = jnp.zeros_like(sum_ref)
        grad_ref[...] = jnp.zeros_like(grad_ref)

    piece = mixed0_ref.shape[0]

    @pl.when(step < tokens // piece)
    def _():
        place = pl.ds(pl.multiple_of(step * piece, piece), piece)
        sum_ref[place] += mixed0_ref[...]
        if not begins:
            grad_ref[place] += grad0_ref[...]

    up = up_ref[...]
    down = down_ref[...]
    shift = shift_ref[...]
    total = jnp.zeros(shift.shape, jnp.float32)
    for step_rows in range(tokens // rows):
        part = slice(step_rows * rows, (step_rows + 1) * rows)
        hidden = dot(normed_ref[part], up) + shift
        grad_active = dot_nt(cot_ref[part], down)
        half = 0.5 + 0.5 * lax.erf(hidden * 0.5**0.5)
        active = (hidden * half).astype(jnp.bfloat16)
        slope = half + hidden * jnp.exp(hidden * hidden * -0.5) * (2 * np.pi) ** -0.5
        grad_hidden = (grad_active * slope).astype(jnp.bfloat16)
        active_ref[part] = active
        hidden_ref[part] = grad_hidden
        total = total + jnp.sum(grad_hidden.astype(jnp.float32), axis=0, keepdims=True)
        sum_ref[part] += dot(active, down)
        grad_ref[part] += dot_nt(grad_hidden, up)
    dshift_ref[...] = total
    grad_down = dot_tn(active_ref[...], cot_ref[...]).astype(jnp.bfloat16)
    grad_up = dot_tn(normed_ref[...], hidden_ref[...]).astype(jnp.bfloat16)
    if not placed:
        ddown_ref[...] = grad_down
        dup_ref[...] = grad_up
    else:
        devices = table_ref.shape[0] - 1
        share, wide = grad_up.shape[0] // devices, grad_up.shape[1]
        steps = grad_up.shape[0] // wide
        for index in range(steps):

            @pl.when(pl.program_id(1) == index)
            def _():
                def write(write_block):
                    for block in range(devices):
                        part = grad_up[block * share : (block + 1) * share]
                        write_block(block, slice(index * share, (index + 1) * share), part)
                    for block in range(devices // steps):
                        part = grad_down[block * share : (block + 1) * share]
                        for n in range(steps):
                            low = (steps + n) * share
                            piece = part[:, n * wide : (n + 1) * wide]
                            place = index * devices // steps + block
                            write_block(place, slice(low, low + share), piece)

                write_placed(table_ref, ddown_ref, dup_ref, core_stride, write)
    if ends:

        @pl.when(step == pl.num_programs(0) * pl.num_programs(1) - 1)
        def _():
            mixed_ref[...] = (sum_ref[...] + last_ref[...]).astype(jnp.bfloat16)


def mlp(normed, cot, joint, shift, mixed0, grad0, last, first, count, table):
    tokens, model = normed.shape
    devices = table.shape[0] - 1
    share = model // devices
    steps = 2
    block = model // steps
    begins, ends = first == 0, first + count == PARTS
    placed = share % 8 == 0
    if placed:
        shape = (devices // 2, count * 2 * steps * share, block)
        shapes = [jax.ShapeDtypeStruct(shape, jnp.bfloat16)] * 2
        spec = pl.BlockSpec((devices // 2, 2 * steps * share, block), lambda p, i, *_: (0, p, 0))
        specs = [spec, spec]
    else:
        shapes = [
            jax.ShapeDtypeStruct((model, count * model), jnp.bfloat16),
            jax.ShapeDtypeStruct((count * model, model), jnp.bfloat16),
        ]
        specs = [
            pl.BlockSpec((model, block), lambda p, i, *_: (0, p * steps + i)),
            pl.BlockSpec((block, model), lambda p, i, *_: (p * steps + i, 0)),
        ]
    pieces = count * steps
    piece = pl.BlockSpec((tokens // pieces, model), lambda p, i, *_: (p * steps + i, 0))
    once = pl.Buffered(1)
    whole = pl.BlockSpec((tokens, model), lambda p, i, *_: (0, 0), pipeline_mode=once)
    core_stride = lax.axis_size("rows") * lax.axis_size("cols")
    mixed, grad, sent, kept, grad_shift = pl.pallas_call(
        functools.partial(mlp_kernel, tokens // 2, begins, ends, placed, core_stride),
        grid_spec=pltpu.PrefetchScalarGridSpec(
            num_scalar_prefetch=1 if placed else 0,
            grid=(count, steps),
            in_specs=[
                whole,
                whole,
                pl.BlockSpec((model, block), lambda p, i, *_: (0, p * steps + i)),
                pl.BlockSpec((block, model), lambda p, i, *_: (i, count + p)),
                pl.BlockSpec((1, block), lambda p, i, *_: (0, (first + p) * steps + i)),
                piece,
                pl.BlockSpec((8, LANES), lambda p, i, *_: (0, 0)) if begins else piece,
                pl.BlockSpec((1, model), lambda p, i, *_: (0, 0)),
            ],
            out_specs=[
                whole,
                whole,
                specs[0],
                specs[1],
                pl.BlockSpec((1, block), lambda p, i, *_: (0, p * steps + i)),
            ],
            scratch_shapes=[pltpu.VMEM((tokens, block), jnp.bfloat16)] * 2
            + ([pltpu.VMEM((tokens, model), jnp.float32)] if ends else []),
        ),
        out_shape=[
            jax.ShapeDtypeStruct((tokens, model), jnp.bfloat16 if ends else jnp.float32),
            jax.ShapeDtypeStruct((tokens, model), jnp.float32),
            shapes[0],
            shapes[1],
            jax.ShapeDtypeStruct((1, count * model), jnp.float32),
        ],
        compiler_params=pltpu.CompilerParams(vmem_limit_bytes=62 * MIB),
        cost_estimate=pl.CostEstimate(
            flops=16 * tokens * model * model * count,
            bytes_accessed=8 * model * model * count + 24 * tokens * model,
            transcendentals=2 * tokens * model * count,
        ),
    )(*([table] if placed else []), normed, cot, joint, joint, shift, mixed0, grad0, last)
    if placed:
        return mixed, grad, (sent, kept), grad_shift
    down = kept.reshape(count, devices, share, model).transpose(1, 0, 2, 3)
    parts = [sent.reshape(devices, share, -1), down.reshape(devices, -1, model)]
    return mixed, grad, parts, grad_shift


def window_gradient_kernel(own, core_stride, table_ref, *refs):
    tokens_ref, grad_ref, *ready, sent_ref, kept_ref, sums_ref = refs
    devices = table_ref.shape[0] - 1
    share = tokens_ref.shape[1] // devices
    step = pl.program_id(0)

    def place(value):
        def write(write_block):
            for block in range(devices):
                part = value[block * share : (block + 1) * share]
                write_block(block, slice(0, share), part)

        write_placed(table_ref, kept_ref, sent_ref, core_stride, write)

    @pl.when(step < own)
    def _():
        place(dot(grad_ref[...], tokens_ref[...]).astype(jnp.bfloat16).T)
        total = 0
        for low in range(0, grad_ref.shape[1], LANES):
            total = total + grad_ref[:, low : low + LANES].astype(jnp.float32)
        sums_ref[...] = total

    for ready_ref in ready:

        @pl.when(step >= own)
        def _():
            place(ready_ref[...])


def window_gradient(rows, grad, ready, table):
    tokens, model = rows.shape
    devices = table.shape[0] - 1
    wide = model // 2
    own = grad.shape[0] // wide
    steps = own + sum(one.shape[1] // wide for one in ready)
    shape = jax.ShapeDtypeStruct((devices // 2, model // devices, steps * wide), jnp.bfloat16)
    spec = pl.BlockSpec((devices // 2, model // devices, wide), lambda n, *_: (0, 0, n))
    core_stride = lax.axis_size("rows") * lax.axis_size("cols")
    return pl.pallas_call(
        functools.partial(window_gradient_kernel, own, core_stride),
        grid_spec=pltpu.PrefetchScalarGridSpec(
            num_scalar_prefetch=1,
            grid=(steps,),
            in_specs=[
                pl.BlockSpec((tokens, model), lambda n, *_: (0, 0), pipeline_mode=pl.Buffered(1)),
                pl.BlockSpec((wide, tokens), lambda n, *_: (jnp.minimum(n, own - 1), 0)),
            ]
            + [pl.BlockSpec((model, wide), lambda n, *_: (0, jnp.maximum(n - own, 0)))] * len(ready),
            out_specs=[
                spec,
                spec,
                pl.BlockSpec((wide, LANES), lambda n, *_: (jnp.minimum(n, own - 1), 0)),
            ],
        ),
        out_shape=[shape, shape, jax.ShapeDtypeStruct((own * wide, LANES), jnp.float32)],
        compiler_params=pltpu.CompilerParams(vmem_limit_bytes=56 * MIB),
        cost_estimate=pl.CostEstimate(
            flops=2 * tokens * model * own * wide,
            bytes_accessed=2 * (tokens * model + tokens * own * wide + model * steps * wide),
            transcendentals=0,
        ),
    )(table, rows, grad, *ready)


def hidden_parts(unit):
    return 5 if unit % 160 == 0 else 1


def normalised(values):
    average = jnp.mean(values, axis=-1, keepdims=True)
    centered = values - average
    variance = jnp.mean(centered * centered, axis=-1, keepdims=True)
    inverse = lax.rsqrt(variance + eps)
    return centered * inverse, inverse


def norm_backward(unit, inverse, gain, grad):
    scaled = grad * gain
    return inverse * (
        scaled
        - jnp.mean(scaled, axis=-1, keepdims=True)
        - unit * jnp.mean(scaled * unit, axis=-1, keepdims=True)
    )


def column_sum(value):
    return jnp.sum(value, axis=0, keepdims=True)


def row_block(tokens):
    return tokens // 4


def row_norm_kernel(rows_ref, vectors_ref, out_ref):
    unit, _ = normalised(rows_ref[...].astype(jnp.float32))
    out_ref[...] = (unit * vectors_ref[0:1] + vectors_ref[1:2]).astype(jnp.bfloat16)


def row_norm(rows, vectors):
    tokens, model = rows.shape
    block = pl.BlockSpec((row_block(tokens), model), lambda i: (i, 0))
    return pl.pallas_call(
        row_norm_kernel,
        grid=(4,),
        in_specs=[block, pl.BlockSpec((8, model), lambda i: (0, 0))],
        out_specs=block,
        out_shape=jax.ShapeDtypeStruct((tokens, model), jnp.bfloat16),
        cost_estimate=pl.CostEstimate(
            flops=8 * tokens * model, bytes_accessed=4 * tokens * model, transcendentals=0
        ),
    )(rows, vectors)


def middle_kernel(attended_ref, proj_ref, image_ref, vectors_ref, middle_ref, normed_ref):
    branch = dot(attended_ref[...], proj_ref[...]) + vectors_ref[0:1]
    middle = image_ref[...].astype(jnp.float32) + branch
    unit, _ = normalised(middle)
    normed = (unit * vectors_ref[1:2] + vectors_ref[2:3]).astype(jnp.bfloat16)
    middle_ref[...] = middle
    normed_ref[...] = normed


def middle_forward(attended, proj, image, vectors):
    tokens, model = attended.shape
    rows = row_block(tokens)
    block = pl.BlockSpec((rows, model), lambda i: (i, 0))
    return pl.pallas_call(
        middle_kernel,
        grid=(tokens // rows,),
        in_specs=[
            block,
            pl.BlockSpec((model, model), lambda i: (0, PARTS)),
            block,
            pl.BlockSpec((8, model), lambda i: (0, 0)),
        ],
        out_specs=[block, block],
        out_shape=[
            jax.ShapeDtypeStruct((tokens, model), jnp.float32),
            jax.ShapeDtypeStruct((tokens, model), jnp.bfloat16),
        ],
        compiler_params=pltpu.CompilerParams(vmem_limit_bytes=40 * MIB),
        cost_estimate=pl.CostEstimate(
            flops=2 * tokens * model * model, bytes_accessed=12 * tokens * model, transcendentals=0
        ),
    )(attended, proj, image, vectors)


def middle_backward_kernel(
    grad_ref, middle_ref, cot_ref, attended_ref, proj_ref, vectors_ref,
    grad_middle_ref, grad_attended_ref, dproj_ref, sums_ref, branch_ref,
):
    step = pl.program_id(0)

    @pl.when(step == 0)
    def _():
        sums_ref[...] = jnp.zeros_like(sums_ref)

    rows = middle_ref.shape[0]
    unit, inverse = normalised(middle_ref[...])
    grad = grad_ref[...]
    cot = cot_ref[...].astype(jnp.float32)
    grad_middle = cot + norm_backward(unit, inverse, vectors_ref[1:2], grad)
    branch = grad_middle.astype(jnp.bfloat16)
    grad_middle_ref[...] = grad_middle
    branch_ref[pl.ds(pl.multiple_of(step * rows, rows), rows)] = branch
    grad_attended_ref[...] = dot_nt(branch, proj_ref[...]).astype(jnp.bfloat16)
    sums_ref[0:1] += column_sum(branch.astype(jnp.float32))
    sums_ref[1:2] += column_sum(grad * unit)
    sums_ref[2:3] += column_sum(grad)
    sums_ref[3:4] += column_sum(cot)

    @pl.when(step == pl.num_programs(0) - 1)
    def _():
        dproj_ref[...] = dot_tn(attended_ref[...], branch_ref[...]).astype(jnp.bfloat16)


def middle_backward(grad, middle, cot, attended, proj, vectors):
    tokens, model = attended.shape
    rows = row_block(tokens)
    block = pl.BlockSpec((rows, model), lambda i: (i, 0))
    few = pl.BlockSpec((8, model), lambda i: (0, 0))
    return pl.pallas_call(
        middle_backward_kernel,
        grid=(tokens // rows,),
        in_specs=[
            block, block, block,
            pl.BlockSpec((tokens, model), lambda i: (0, 0), pipeline_mode=pl.Buffered(1)),
            pl.BlockSpec((model, model), lambda i: (0, PARTS), pipeline_mode=pl.Buffered(1)),
            few,
        ],
        out_specs=[block, block, pl.BlockSpec((model, model), lambda i: (0, 0)), few],
        out_shape=[
            jax.ShapeDtypeStruct((tokens, model), jnp.float32),
            jax.ShapeDtypeStruct((tokens, model), jnp.bfloat16),
            jax.ShapeDtypeStruct((model, model), jnp.bfloat16),
            jax.ShapeDtypeStruct((8, model), jnp.float32),
        ],
        scratch_shapes=[pltpu.VMEM((tokens, model), jnp.bfloat16)],
        compiler_params=pltpu.CompilerParams(vmem_limit_bytes=56 * MIB),
        cost_estimate=pl.CostEstimate(
            flops=4 * tokens * model * model, bytes_accessed=24 * tokens * model, transcendentals=0
        ),
    )(grad, middle, cot, attended, proj, vectors)


def image_backward_kernel(
    rows_ref, first_ref, second_ref, grad_middle_ref, vectors_ref, out_ref, sums_ref
):
    @pl.when(pl.program_id(0) == 0)
    def _():
        sums_ref[...] = jnp.zeros_like(sums_ref)

    unit, inverse = normalised(rows_ref[...].astype(jnp.float32))
    grad = first_ref[...].astype(jnp.float32) + second_ref[...].astype(jnp.float32)
    total = grad_middle_ref[...] + norm_backward(unit, inverse, vectors_ref[0:1], grad)
    out_ref[...] = total.astype(jnp.bfloat16)
    sums_ref[0:1] += column_sum(grad * unit)
    sums_ref[1:2] += column_sum(grad)


def image_backward(rows, first, second, grad_middle, vectors):
    tokens, model = rows.shape
    block = pl.BlockSpec((row_block(tokens), model), lambda i: (i, 0))
    few = pl.BlockSpec((8, model), lambda i: (0, 0))
    return pl.pallas_call(
        image_backward_kernel,
        grid=(4,),
        in_specs=[block, block, block, block, few],
        out_specs=[block, few],
        out_shape=[
            jax.ShapeDtypeStruct((tokens, model), jnp.bfloat16),
            jax.ShapeDtypeStruct((8, model), jnp.float32),
        ],
        cost_estimate=pl.CostEstimate(
            flops=12 * tokens * model, bytes_accessed=10 * tokens * model, transcendentals=0
        ),
    )(rows, first, second, grad_middle, vectors)


def main_place(width):
    col = lax.broadcasted_iota(jnp.int32, (width, NWIN * SIDE), 0)
    slot = lax.broadcasted_iota(jnp.int32, (width, NWIN * SIDE), 1)
    inside = slot % SIDE < WIN
    return (inside & (col == slot // SIDE * WIN + slot % SIDE)).astype(jnp.bfloat16)


def end_starts(width, count):
    return [b * WIN for b in range(count - 1)] + [width - END]


def end_place(width):
    count = lax.axis_size("rows")
    row = lax.axis_index("rows")
    start = jnp.array(end_starts(width, count))[row]
    col = start + lax.broadcasted_iota(jnp.int32, (END, 2 * SIDE), 0)
    slot = lax.broadcasted_iota(jnp.int32, (END, 2 * SIDE), 1)
    held = (slot % SIDE < WIN) & ((slot < SIDE) | (row == count - 1))
    window = row + slot // SIDE
    return (held & (col == window * WIN + slot % SIDE)).astype(jnp.bfloat16)


def to_windows_kernel(width, rest, rows_ref, main_ref, end_ref, out_ref):
    out_ref[...] = jnp.zeros_like(out_ref)
    for i in range(WIN):
        part = dot_tn(main_ref[...], rows_ref[i * width : (i + 1) * width]).astype(jnp.bfloat16)
        for b in range(NWIN):
            out_ref[b * TOK + i * SIDE : b * TOK + (i + 1) * SIDE] = part[b * SIDE : (b + 1) * SIDE]
    first = WIN * width
    for i in range(rest):
        part = rows_ref[first + i * END : first + (i + 1) * END]
        part = dot_tn(end_ref[...], part).astype(jnp.bfloat16)
        for b in range(2):
            place = (NWIN + b) * TOK + i * SIDE
            out_ref[place : place + SIDE] = part[b * SIDE : (b + 1) * SIDE]


def to_rows_kernel(width, rest, windows_ref, main_ref, end_ref, out_ref):
    for i in range(WIN):
        part = jnp.concatenate(
            [windows_ref[b * TOK + i * SIDE : b * TOK + (i + 1) * SIDE] for b in range(NWIN)],
            axis=0,
        )
        out_ref[i * width : (i + 1) * width] = dot(main_ref[...], part).astype(jnp.bfloat16)
    first = WIN * width
    for i in range(rest):
        part = jnp.concatenate(
            [
                windows_ref[b * TOK + i * SIDE : b * TOK + (i + 1) * SIDE]
                for b in range(NWIN, NWIN + 2)
            ],
            axis=0,
        )
        part = dot(end_ref[...], part).astype(jnp.bfloat16)
        out_ref[first + i * END : first + (i + 1) * END] = part


def rearranged(kernel, value, width, rest, tokens):
    model = value.shape[1]
    lanes = model // 5
    main, end = main_place(width), end_place(width)
    return pl.pallas_call(
        functools.partial(kernel, width, rest),
        grid=(5,),
        in_specs=[
            pl.BlockSpec((value.shape[0], lanes), lambda i: (0, i)),
            pl.BlockSpec(main.shape, lambda i: (0, 0)),
            pl.BlockSpec(end.shape, lambda i: (0, 0)),
        ],
        out_specs=pl.BlockSpec((tokens, lanes), lambda i: (0, i)),
        out_shape=jax.ShapeDtypeStruct((tokens, model), jnp.bfloat16),
        compiler_params=pltpu.CompilerParams(vmem_limit_bytes=32 * MIB),
        cost_estimate=pl.CostEstimate(
            flops=200 * tokens * model, bytes_accessed=6 * tokens * model, transcendentals=0
        ),
    )(value, main, end)


def axis_bits(axis):
    count = lax.axis_size(axis)
    return [(axis, 1 << bit) for bit in range(count.bit_length() - 1)]


def flipped(value, bit):
    axis, mask = bit
    return lax.ppermute(value, axis, [(i, i ^ mask) for i in range(lax.axis_size(axis))])


def bit_of(bit):
    axis, mask = bit
    return (lax.axis_index(axis) // mask) % 2


def device_bits():
    return [bit for axis in ALL for bit in reversed(axis_bits(axis))]


def after(value, others):
    return lax.optimization_barrier((value, others))[0]


def beside(flights, value, kernel):
    return sync(kernel(launch(value, flights)), flights)


class Flight:

    def __init__(self, steps):
        self.steps = steps
        self.sent = self.arrived = self.value = None
        self.flying = True

    def advance(self):
        try:
            self.sent, self.arrived = self.steps.send(self.arrived)
        except StopIteration as end:
            self.sent, self.arrived, self.flying = [], [], False
            self.value = end.value

    def finish(self):
        while self.flying:
            self.advance()
        return self.value


def launch(value, flights):
    for one in flights:
        if one.flying:
            one.advance()
    return after(value, [one.sent for one in flights])


def sync(value, flights):
    flights = [one for one in flights if one.flying]
    value, arrived = lax.optimization_barrier((value, [one.arrived for one in flights]))
    for one, pieces in zip(flights, arrived):
        one.arrived = pieces
    return value


def index_masks(bits):
    weights = {"cols": 1, "rows": lax.axis_size("cols")}
    weights["dp"] = weights["rows"] * lax.axis_size("rows")
    return [weights[axis] * mask for axis, mask in bits]


def halving_orders():
    dp, rows, cols = axis_bits("dp"), axis_bits("rows"), axis_bits("cols")
    core, chips = dp[:1], dp[1:]
    (core,) = index_masks(core)
    orders = [cols + chips + rows, chips + rows[:1] + cols + rows[1:]]
    return core, [index_masks(order) for order in orders]


def block_tables():
    core, orders = halving_orders()
    me = lax.axis_index(ALL)
    steps = len(orders[0])
    flips = []
    for order in orders:
        place = np.arange(1 << steps)
        flips.append(sum((place >> (steps - 1 - n) & 1) * mask for n, mask in enumerate(order)))
    flips = [jnp.asarray(flip, jnp.int32) for flip in flips]
    first = (me & core) == 0
    there = (me ^ core) ^ jnp.where(first, flips[1], flips[0])
    here = me ^ jnp.where(first, flips[0], flips[1])
    return there, here


def place_table():
    there, here = block_tables()
    blocks = jnp.concatenate([here, there])
    count = blocks.shape[0]
    hit = blocks[:, None] == jnp.arange(count)[None, :]
    places = jnp.sum(jnp.where(hit, jnp.arange(count)[:, None], 0), axis=0)
    core, _ = halving_orders()
    return jnp.concatenate([places, (lax.axis_index(ALL) // core % 2)[None]]).astype(jnp.int32)


def partner_permute(value, step):
    core, orders = halving_orders()
    pairs = []
    for index in range(lax.axis_size(ALL)):
        order = orders[(index & core) // core]
        pairs.append((index, index ^ (core if step == 0 else order[step - 1])))
    return lax.ppermute(value, ALL, pairs)


def packed_shape(parts):
    if len({part.shape[1] for part in parts}) == 1:
        return parts[0].shape[1], sum(part.shape[2] for part in parts)
    wide = 2 * LANES
    return sum(part.shape[1] * part.shape[2] // wide for part in parts), wide


def pack_into(refs, write):
    rows, wide = packed_shape(refs)
    side = rows == refs[0].shape[1]
    place = 0
    for ref in refs:
        height, width = ref.shape[1:]
        if side:
            write(slice(0, rows), slice(place, place + width), ref[0])
            place += width
            continue
        for low in range(0, width, wide):
            write(slice(place, place + height), slice(0, wide), ref[0, :, low : low + wide])
            place += height


def pack_kernel(table_ref, *refs):
    def write(rows, cols, value):
        refs[-1][0, rows, cols] = value

    pack_into(refs[:-1], write)


def pack(parts, table):
    count = table.shape[0]
    rows, wide = packed_shape(parts)
    return pl.pallas_call(
        pack_kernel,
        grid_spec=pltpu.PrefetchScalarGridSpec(
            num_scalar_prefetch=1,
            grid=(count,),
            in_specs=[
                pl.BlockSpec((1,) + part.shape[1:], lambda i, table: (table[i], 0, 0))
                for part in parts
            ],
            out_specs=pl.BlockSpec((1, rows, wide), lambda i, table: (i, 0, 0)),
        ),
        out_shape=jax.ShapeDtypeStruct((count, rows, wide), jnp.bfloat16),
        cost_estimate=pl.CostEstimate(
            flops=0, bytes_accessed=4 * count * rows * wide, transcendentals=0
        ),
    )(table, *parts)


def summed(sent, kept):
    held = [kept]
    size = 2 * kept.shape[0]
    step = 0
    while size > 1:
        if step:
            sent = sum(piece[size // 2 : size].astype(jnp.float32) for piece in held)
            sent = sent.astype(jnp.bfloat16)
        held = yield [sent], [partner_permute(sent, step)] + held
        size //= 2
        step += 1
    return sum(piece[0].astype(jnp.float32) for piece in held)


def summed_packed(parts):
    there, here = block_tables()
    total = yield from summed(pack(parts, there), pack(parts, here))
    shapes = [part.shape[1:] for part in parts]
    rows, wide = packed_shape(parts)
    out = []
    place = 0
    for height, width in shapes:
        if rows == height:
            out.append(total[:, place : place + width])
            place += width
        else:
            pieces = width // wide
            piece = total[place : place + pieces * height].reshape(pieces, height, wide)
            out.append(piece.transpose(1, 0, 2).reshape(height, width))
            place += pieces * height
    return out


def summed_mlp(parts, share):
    total = yield from summed(*parts)
    wide = total.shape[1]
    total = total.reshape(-1, 2, 2, share, wide)
    up = total[:, 0].transpose(2, 0, 1, 3).reshape(share, -1)
    down = total[:, 1].transpose(0, 2, 1, 3).reshape(-1, 2 * wide)
    return [up, down]


def summed_columns(sent, kept, widths):
    total = yield from summed(sent, kept)
    places = np.cumsum([0] + list(widths))
    return [total[:, low : low + width] for low, width in zip(places, widths)]


def all_sum(value):
    for bit in reversed(device_bits()):
        (arrived,) = yield [value], [flipped(value, bit)]
        value = value + arrived
    return value


def small_gather(value):
    for bit in reversed(device_bits()):
        arrived = flipped(value, bit)
        value = jnp.where(
            bit_of(bit) == 0,
            jnp.concatenate([value, arrived], axis=0),
            jnp.concatenate([arrived, value], axis=0),
        )
    return value


SWAP = [(0, 1), (1, 0)]


def split_tiles(tiles):
    col = lax.axis_index("cols")
    kept = lax.dynamic_index_in_dim(tiles, col, 0, keepdims=False)
    sent = lax.dynamic_index_in_dim(tiles, 1 - col, 0, keepdims=False)
    return kept, sent, lax.ppermute(sent, "cols", SWAP)


def join_tiles(kept, arrived):
    return jnp.where(
        lax.axis_index("cols") == 0,
        jnp.concatenate([kept, arrived], axis=1),
        jnp.concatenate([arrived, kept], axis=1),
    )


def split_image(image):
    col = lax.axis_index("cols")
    width = image.shape[1] // 2
    kept = lax.dynamic_slice_in_dim(image, col * width, width, 1)
    sent = lax.dynamic_slice_in_dim(image, (1 - col) * width, width, 1)
    return kept, sent, lax.ppermute(sent, "cols", SWAP)


def join_image(kept, arrived):
    return jnp.where(
        lax.axis_index("cols") == 0, jnp.stack([kept, arrived]), jnp.stack([arrived, kept])
    )


def halves_to_image(tiles):
    kept, _, arrived = split_tiles(tiles)
    return join_tiles(kept, arrived)


def image_to_halves(image):
    kept, _, arrived = split_image(image)
    return join_image(kept, arrived)


def column_windows(rows):
    width = rows.shape[1]
    parts = []
    for b in range(NWIN):
        piece = rows[:, b * WIN : min((b + 1) * WIN, width)]
        parts.append(jnp.pad(piece, ((0, 0), (0, SIDE - piece.shape[1]), (0, 0))))
    return jnp.stack(parts)


def column_rows(windows, width):
    parts = [windows[b, :, : min(WIN, width - b * WIN)] for b in range(len(windows))]
    return jnp.concatenate(parts, axis=1)


def pad_rows(value, top, bottom):
    widths = [(0, 0)] * value.ndim
    widths[-3] = (top, bottom)
    return jnp.pad(value, widths)


class Layout:

    def __init__(self, tiles):
        self.tiles = tiles
        _, self.height, tile_w, self.model = tiles
        self.width = 2 * tile_w
        self.count = lax.axis_size("rows")
        self.row = lax.axis_index("rows")
        self.near = self.count == NWIN - 1
        self.step = self.height - WIN
        self.halo = self.step * (self.count - 1)
        self.rest = self.height * self.count - WIN * self.count
        if self.near:
            self.slots = NWIN + 2
            self.tokens = WIN * self.width + self.rest * END
        else:
            self.slots = -(-NWIN * NWIN // self.count)
            self.tokens = 2 * self.height * tile_w

    def enter(self, tiles):
        if not self.near:
            return tiles.reshape(self.tokens, self.model)
        last, rest, halo = self.count - 1, self.rest, self.halo
        top = self.height - rest
        kept_low, sent_low, low = split_tiles(tiles[:, top:])
        (low,) = yield [sent_low], [low]
        lower = join_tiles(kept_low, low)
        kept_up, sent_up, up = split_tiles(after(tiles[:, :top], low))
        starts = end_starts(self.width, self.count)
        sent = [lower[rest - halo :]]
        arrived = [lax.ppermute(sent[0], "rows", [(i, i + 1) for i in range(last)])]
        for target in range(last):
            sent.append(lower[:, starts[target] : starts[target] + SIDE])
            arrived.append(lax.ppermute(sent[-1], "rows", [(last, target)]))
        up, down, *arrived = yield sent + [sent_up], [up] + arrived
        upper = join_tiles(kept_up, up)
        end = lower[:, starts[last] :]
        for target in range(last):
            piece = jnp.pad(arrived[target], ((0, 0), (0, END - SIDE), (0, 0)))
            end = jnp.where(self.row == target, piece, end)
        held = jnp.sum(end_place(self.width), axis=1).astype(jnp.bfloat16)
        end = end * held[None, :, None]
        whole = jnp.concatenate([down, upper, lower], axis=0)
        main = lax.dynamic_slice_in_dim(whole, halo - self.step * self.row, WIN, 0)
        return jnp.concatenate(
            [main.reshape(-1, self.model), end.reshape(-1, self.model)], axis=0
        )

    def leave(self, tokens):
        if not self.near:
            return tokens.reshape(self.tiles)
        last, rest, halo = self.count - 1, self.rest, self.halo
        top = self.height - rest
        main = tokens[: WIN * self.width].reshape(WIN, self.width, self.model)
        end = tokens[WIN * self.width :].reshape(rest, END, self.model)
        held = jnp.sum(end_place(self.width), axis=1).astype(jnp.bfloat16)
        end = end * held[None, :, None]
        up = lax.ppermute(main[:halo], "rows", [(i + 1, i) for i in range(last)])
        piece = end[:, :SIDE]
        pieces = [lax.ppermute(piece, "rows", [(source, last)]) for source in range(last)]
        upper = lax.dynamic_slice_in_dim(main, self.step * self.row, top, 0)
        kept_up, sent_up, arrived_up = split_image(upper)
        up, arrived_up, *pieces = yield [piece, sent_up], [up, arrived_up] + pieces
        tail = 0
        for start, piece in zip(end_starts(self.width, self.count), pieces + [end]):
            rest_wide = self.width - piece.shape[1] - start
            tail = tail + jnp.pad(piece, ((0, 0), (start, rest_wide), (0, 0)))
        below = jnp.where(self.row == last, tail, pad_rows(up, 0, rest - halo))
        whole = jnp.concatenate([main, below], axis=0)
        place = self.step * self.row + top
        kept_low, sent_low, arrived_low = split_image(
            lax.dynamic_slice_in_dim(whole, place, rest, 0)
        )
        (arrived_low,) = yield [sent_low], [arrived_low]
        upper = join_image(kept_up, arrived_up)
        lower = join_image(kept_low, arrived_low)
        return jnp.concatenate([upper, lower], axis=1)

    def to_windows(self, tokens):
        if self.near:
            total = self.slots * TOK
            return rearranged(to_windows_kernel, tokens, self.width, self.rest, total)
        windows = column_windows(halves_to_image(tokens.reshape(self.tiles)))
        windows = lax.all_gather(windows, "rows", axis=1, tiled=True)
        extra = NWIN * WIN - windows.shape[1]
        windows = jnp.pad(windows, ((0, 0), (0, extra), (0, 0), (0, 0)))
        windows = windows.reshape(NWIN, NWIN, WIN, SIDE, self.model).transpose(1, 0, 2, 3, 4)
        windows = windows.reshape(NWIN * NWIN, WIN, SIDE, self.model)
        extra = self.slots * self.count - NWIN * NWIN
        windows = jnp.pad(windows, ((0, extra), (0, SIDE - WIN), (0, 0), (0, 0)))
        windows = lax.dynamic_slice_in_dim(windows, self.row * self.slots, self.slots, 0)
        return windows.reshape(self.slots * TOK, self.model)

    def to_rows(self, windows):
        if self.near:
            return rearranged(to_rows_kernel, windows, self.width, self.rest, self.tokens)
        windows = windows.reshape(self.slots, SIDE, SIDE, self.model)
        windows = lax.all_gather(windows[:, :WIN], "rows", axis=0, tiled=True)
        windows = windows[: NWIN * NWIN].reshape(NWIN, NWIN, WIN, SIDE, self.model)
        windows = windows.transpose(1, 0, 2, 3, 4).reshape(NWIN, NWIN * WIN, SIDE, self.model)
        windows = lax.dynamic_slice_in_dim(windows, self.row * self.height, self.height, 1)
        return image_to_halves(column_rows(windows, self.width)).reshape(self.tokens, self.model)


def shards(
    image_in,
    ln1_gain,
    ln1_bias,
    w_qkv,
    qv_bias,
    rel_rows,
    rel_cols,
    w_proj,
    proj_bias,
    ln2_gain,
    ln2_bias,
    w_fc1,
    fc1_bias,
    w_fc2,
    fc2_bias,
    cotangent,
):
    devices = lax.axis_size(ALL)
    me = lax.axis_index(ALL)
    model = image_in.shape[3]
    layout = Layout(image_in.shape)
    tokens = layout.tokens
    share = model // devices
    unit = fc1_bias.shape[0]

    rows = Flight(layout.enter(image_in))
    cot = Flight(layout.enter(cotangent))
    rows.advance()

    def gathered(shard):
        return lax.all_gather(shard, ALL, axis=0, tiled=True)

    vectors = [ln1_gain, ln1_bias, qv_bias[:, 0], qv_bias[:, 1], proj_bias, ln2_gain, ln2_bias]
    vectors = small_gather(jnp.concatenate(vectors + [fc2_bias, fc1_bias])[None])
    vectors = launch(sync(vectors, [rows]), [rows])
    w_fc1 = after(w_fc1, rows.sent)
    vectors = vectors.astype(jnp.float32)
    gain1, shift1, query_shift, value_shift, proj_shift, gain2, shift2, down_shift = (
        vectors[:, n * share : (n + 1) * share].reshape(1, model) for n in range(8)
    )
    norm_vectors = jnp.pad(jnp.concatenate([gain1, shift1], axis=0), ((0, 6), (0, 0)))
    middle_vectors = jnp.concatenate([proj_shift, gain2, shift2, down_shift], axis=0)
    middle_vectors = jnp.pad(middle_vectors, ((0, 4), (0, 0)))
    up_shift = vectors[:, 8 * share :].reshape(devices, PARTS, share)
    up_shift = up_shift.transpose(1, 0, 2).reshape(1, devices * unit)
    half = model // 2
    thirds = [w_qkv[:, n * half : (n + 1) * half] for n in (0, 2, 4, 1, 3, 5)]
    qkv_full = gathered(jnp.concatenate(thirds, axis=1))
    up_shard = w_fc1.reshape(share, devices, PARTS, share).transpose(0, 2, 1, 3)
    down_shard = [w_fc2[n * share : (n + 1) * share] for n in range(PARTS)]
    up_shard = up_shard.reshape(share, devices * unit)
    cut = PARTS // 2
    joint = gathered(
        jnp.concatenate([up_shard[:, : cut * model]] + down_shard[:cut] + [w_proj], axis=1)
    )
    joint2 = gathered(jnp.concatenate([up_shard[:, cut * model :]] + down_shard[cut:], axis=1))

    norm_vectors = sync(norm_vectors, [rows])
    rows = rows.finish()
    window_tokens = layout.to_windows(row_norm(rows, norm_vectors))
    nothing = jnp.zeros((1, half), jnp.float32)
    shift_qkv = jnp.concatenate(
        [query_shift[:, :half], nothing, value_shift[:, :half]]
        + [query_shift[:, half:], nothing, value_shift[:, half:]],
        axis=1,
    )
    window_tokens = launch(window_tokens, [cot])
    project = lax.dot_general(
        qkv_full, window_tokens, (((0,), (1,)), ((), ())), preferred_element_type=jnp.float32
    )
    project = (project + shift_qkv.reshape(3 * model, 1)).astype(jnp.bfloat16)
    project = sync(project, [cot])
    project = launch(project, [cot])
    tab = wide_tables(rel_rows, rel_cols)
    ind = key_indicator()
    attended_windows, weights, inverse = attention_forward(project, tab, ind)
    attended = layout.to_rows(attended_windows)
    attended, cot, joint = sync((attended, cot.finish(), joint), [])
    middle, normed2 = middle_forward(attended, joint, rows, middle_vectors)

    mixed = middle
    grad_normed2 = jnp.zeros((8, LANES), jnp.float32)
    table = place_table()
    sums = []
    shifts = []
    for first, count in ((0, 2), (2, 2)):

        def step(normed2):
            return mlp(
                normed2,
                cot,
                joint if first == 0 else joint2,
                up_shift,
                mixed,
                grad_normed2,
                down_shift,
                first,
                count,
                table,
            )

        if first:
            mixed, joint2 = sync((mixed, joint2), [])
        mixed, grad_normed2, blocks, grad_shift = beside(sums, normed2, step)
        shifts.append(grad_shift.reshape(count, devices, share))
        if isinstance(blocks, list):
            sums.append(Flight(summed_packed(blocks)))
        else:
            sums.append(Flight(summed_mlp(blocks, share)))

    output = Flight(layout.leave(mixed))
    grad_normed2 = launch(grad_normed2, sums)
    grad_middle, grad_attended, grad_proj, middle_sums = sync(
        middle_backward(grad_normed2, middle, cot, attended, joint, middle_vectors), sums[1:]
    )

    def rows_of(vector):
        return vector.reshape(devices, -1)

    def attention_step(half):
        return attention_backward(project, weights, inverse, grad_windows, tab, ind, half)

    def project_step(grad_project, half):
        return lax.dot_general(
            grad_project,
            qkv_full[:, half * 3 * model // 2 : (half + 1) * 3 * model // 2],
            (((0,), (1,)), ((), ())),
            preferred_element_type=jnp.float32,
        ).astype(jnp.bfloat16)

    grad_windows = layout.to_windows(launch(grad_attended, sums[1:] + [output]))
    grad_project, grad_tab = sync(attention_step(0), sums[:1])
    grad_project = launch(grad_project, sums[:1])
    sent, kept, sums0 = sync(
        window_gradient(window_tokens, grad_project, [grad_proj], table), sums[1:] + [output]
    )
    sums.append(Flight(summed_columns(sent, kept, [3 * half, model])))
    grad_project = launch(grad_project, sums[1:] + [output])
    first_rows = layout.to_rows(project_step(grad_project, 0))
    first_rows, grad_windows = sync((first_rows, grad_windows), sums[:1] + sums[-1:])
    grad_windows = launch(grad_windows, sums[:1] + sums[-1:])
    grad_project, grad_part = sync(attention_step(1), sums + [output])
    grad_project = launch(grad_project, sums + [output])
    sent, kept, sums1 = sync(
        window_gradient(window_tokens, grad_project, [], table), sums + [output]
    )
    sums.append(Flight(summed_columns(sent, kept, [3 * half])))
    grad_project = launch(grad_project, sums)
    grad_tokens = sync(project_step(grad_project, 1), sums)
    second_rows = layout.to_rows(launch(grad_tokens, sums))
    grad_rows, norm_sums = sync(
        image_backward(rows, first_rows, second_rows, grad_middle, norm_vectors), sums
    )
    grad_in = Flight(layout.leave(grad_rows))

    grad_sums = [jnp.sum(piece, axis=1) for piece in (sums0, sums1)]
    up_shift_sums = jnp.concatenate(shifts, axis=0).transpose(1, 0, 2).reshape(devices, unit)
    small = jnp.concatenate(
        [
            rows_of(norm_sums[0]),
            rows_of(norm_sums[1]),
            rows_of(jnp.concatenate([piece[:half] for piece in grad_sums])),
            rows_of(jnp.concatenate([piece[2 * half :] for piece in grad_sums])),
        ]
        + [rows_of(middle_sums[n]) for n in range(4)]
        + [up_shift_sums],
        axis=1,
    )
    shape = small.shape
    small = [small.reshape(-1)] + [
        table.reshape(-1) for table in narrow_tables(grad_tab + grad_part)
    ]
    small = Flight(all_sum(jnp.concatenate(small)))
    sums.append(small)

    def formatted(ups, downs):
        ups = [grad.reshape(share, -1, devices, share) for grad in ups]
        ups = jnp.concatenate(ups, axis=1).transpose(0, 2, 1, 3)
        return ups.reshape(share, devices * unit), jnp.concatenate(downs, axis=0)

    launch(norm_sums, [grad_in] + sums)
    done = output.finish()
    done = sync(done, sums)
    launch(done, sums)
    grad_fc1, grad_fc2 = formatted(*zip(*[one.finish() for one in sums[:-3]]))
    grad_fc1, grad_fc2 = sync((grad_fc1, grad_fc2), sums + [grad_in])
    launch(grad_fc1, [grad_in] + sums)
    first_qkv, sum_proj = sums[-3].finish()
    first_qkv, sum_proj = sync((first_qkv, sum_proj), sums + [grad_in])
    launch(first_qkv, [grad_in] + sums)
    (last_qkv,) = sums[-2].finish()
    small = small.finish()
    tables = small[shape[0] * shape[1] :].reshape(2, REL, HD)
    small = small[: shape[0] * shape[1]].reshape(shape)
    small = lax.dynamic_index_in_dim(small, me, 0, keepdims=False)
    thirds = [
        piece[:, n * half : (n + 1) * half] for n in range(3) for piece in (first_qkv, last_qkv)
    ]
    return (
        done,
        grad_in.finish().astype(jnp.float32),
        small[:share],
        small[share : 2 * share],
        jnp.concatenate(thirds, axis=1),
        jnp.stack([small[2 * share : 3 * share], small[3 * share : 4 * share]], axis=1),
        tables[0],
        tables[1],
        sum_proj,
        small[4 * share : 5 * share],
        small[5 * share : 6 * share],
        small[6 * share : 7 * share],
        grad_fc1,
        small[8 * share :],
        grad_fc2,
        small[7 * share : 8 * share],
    )


def solution(mesh):
    tile = P("dp", "rows", "cols", None)
    vector = P(ALL)
    matrix = P(ALL, None)
    in_specs = (
        tile, vector, vector, matrix, matrix, P(), P(), matrix, vector, vector, vector,
        matrix, vector, matrix, vector, tile,
    )
    out_specs = (
        tile, tile, vector, vector, matrix, matrix, P(), P(), matrix, vector, vector, vector,
        matrix, vector, matrix, vector,
    )
    return jax.shard_map(shards, mesh=mesh, in_specs=in_specs, out_specs=out_specs, check_vma=False)
```

```python
import functools

import jax
import jax.numpy as jnp
import numpy as np
from jax import lax
from jax.experimental import pallas as pl
from jax.experimental.pallas import tpu as pltpu
from jax.sharding import PartitionSpec as P

HEADS = 16
HALF = HEADS // 2
GROUP = 8
WIN = 14
NWIN = 5
SIDE = 16
HD = 80
KEYS = WIN * SIDE
TOK = SIDE * SIDE
LANES = 128
DEPTH = 128
REL = 2 * WIN - 1
NEG = -1e30
END = 24
ALL = ("dp", "rows", "cols")
MIB = 1024 * 1024
PARTS = 4

eps = 1e-06


def dot(a, b):
    return jnp.dot(a, b, preferred_element_type=jnp.float32)


def dot_nt(a, b):
    return lax.dot_general(a, b, (((1,), (1,)), ((), ())), preferred_element_type=jnp.float32)


def dot_tn(a, b):
    return lax.dot_general(a, b, (((0,), (0,)), ((), ())), preferred_element_type=jnp.float32)


def offset_onehot(dtype):
    a = jnp.arange(WIN)[:, None]
    i = jnp.arange(SIDE)[None, :]
    offset = jnp.where(i < WIN, a - i + WIN - 1, -1)
    return (offset[:, :, None] == jnp.arange(REL)).astype(dtype).reshape(KEYS, REL)


def wide_tables(rel_rows, rel_cols):
    onehot = offset_onehot(jnp.bfloat16)
    return jnp.concatenate(
        [dot(onehot, table).astype(jnp.bfloat16) for table in (rel_rows, rel_cols)], axis=0
    )


def narrow_tables(grad):
    onehot = offset_onehot(jnp.float32)
    return [
        lax.dot_general(
            onehot,
            grad[n * KEYS : (n + 1) * KEYS],
            (((0,), (0,)), ((), ())),
            precision=lax.Precision.HIGHEST,
        )
        for n in (0, 1)
    ]


def key_indicator():
    row = lax.broadcasted_iota(jnp.int32, (DEPTH - HD, TOK), 0)
    key = lax.broadcasted_iota(jnp.int32, (DEPTH - HD, TOK), 1)
    return ((row == key // SIDE) | (row - SIDE == key % SIDE)).astype(jnp.bfloat16)


def query_offsets(query, tab_ref, lane):
    halves = []
    for half in range(2):
        low = half * 8
        count = min(8, WIN - low)
        part = dot(
            tab_ref[low * SIDE : (low + count) * SIDE], query[:, half * LANES : (half + 1) * LANES]
        )
        rows = part[:SIDE]
        for a in range(1, count):
            rows = jnp.where(
                lane[:, :LANES] // SIDE == a, part[a * SIDE : (a + 1) * SIDE], rows
            )
        halves.append(rows)
    part = dot(tab_ref[KEYS:], query)
    cols = part[:SIDE]
    for b in range(1, WIN):
        cols = jnp.where(lane % SIDE == b, part[b * SIDE : (b + 1) * SIDE], cols)
    return jnp.concatenate(halves, axis=1), cols


def attention_forward_kernel(
    project_ref, tab_ref, ind_ref, attended_ref, weights_ref, inverse_ref, turned_ref
):
    model = turned_ref.shape[0]
    lane = lax.broadcasted_iota(jnp.int32, (SIDE, TOK), 1)
    sub = lax.broadcasted_iota(jnp.int32, (SIDE, TOK), 0)
    ind = ind_ref[...]
    scale = HD**-0.5
    zeros = jnp.zeros((DEPTH - HD - 2 * SIDE, TOK), jnp.bfloat16)

    def place_of(head):
        return head // HALF * 3 * model // 2 + head % HALF * HD

    def wide(head):
        place = place_of(head)
        query = project_ref[place : place + HD]
        key = project_ref[model // 2 + place : model // 2 + place + HD]
        rows, cols = query_offsets(query, tab_ref, lane)
        rows = (rows * HD**0.5).astype(jnp.bfloat16)
        cols = jnp.where(sub < WIN, cols * HD**0.5, NEG).astype(jnp.bfloat16)
        query = jnp.concatenate([query, rows, cols, zeros], axis=0)
        return jnp.concatenate([key, ind], axis=0), query

    def softmax(scores):
        maxima = jnp.max(scores, axis=0, keepdims=True)
        weights = jnp.exp((scores - maxima) * scale)
        inverse = 1.0 / jnp.sum(weights, axis=0, keepdims=True)
        return weights.astype(jnp.bfloat16), inverse

    for first in range(0, HEADS, GROUP):
        heads = range(first, first + GROUP)
        scores = [wide(head) for head in heads]
        scores = [dot_tn(key, query)[:KEYS] for key, query in scores]
        results = [softmax(one) for one in scores]
        for head, (weights, inverse) in zip(heads, results):
            low = head * HD
            place = model + place_of(head)
            weights_ref[0, head] = weights
            inverse_ref[0, head : head + 1] = inverse
            attended = dot(project_ref[place : place + HD, :KEYS], weights)
            turned_ref[low : low + HD] = (attended * inverse).astype(jnp.bfloat16)
    attended_ref[...] = turned_ref[...].T


def attention_forward(project, tab, ind):
    model = project.shape[0] // 3
    slots = project.shape[1] // TOK
    return pl.pallas_call(
        attention_forward_kernel,
        grid=(slots,),
        in_specs=[
            pl.BlockSpec((3 * model, TOK), lambda i: (0, i)),
            pl.BlockSpec((2 * KEYS, HD), lambda i: (0, 0)),
            pl.BlockSpec((DEPTH - HD, TOK), lambda i: (0, 0)),
        ],
        out_specs=[
            pl.BlockSpec((TOK, model), lambda i: (i, 0)),
            pl.BlockSpec((1, HEADS, KEYS, TOK), lambda i: (i, 0, 0, 0)),
            pl.BlockSpec((1, HEADS, TOK), lambda i: (i, 0, 0)),
        ],
        out_shape=[
            jax.ShapeDtypeStruct((slots * TOK, model), jnp.bfloat16),
            jax.ShapeDtypeStruct((slots, HEADS, KEYS, TOK), jnp.bfloat16),
            jax.ShapeDtypeStruct((slots, HEADS, TOK), jnp.float32),
        ],
        scratch_shapes=[pltpu.VMEM((model, TOK), jnp.bfloat16)],
        compiler_params=pltpu.CompilerParams(vmem_limit_bytes=60 * MIB),
        cost_estimate=pl.CostEstimate(
            flops=slots * 3_500_000_000,
            bytes_accessed=slots * 6 * MIB,
            transcendentals=slots * HEADS * KEYS * TOK,
        ),
    )(project, tab, ind)


def attention_backward_kernel(
    project_ref, weights_ref, inverse_ref, grad_ref, tab_ref, ind_ref, out_ref, dtab_ref, turned_ref
):
    model = turned_ref.shape[0]
    lane = lax.broadcasted_iota(jnp.int32, (SIDE, TOK), 1)
    ind = ind_ref[...]
    tab = tab_ref[...]
    scale = HD**-0.5

    @pl.when(pl.program_id(0) == 0)
    def _():
        dtab_ref[...] = jnp.zeros_like(dtab_ref)

    turned_ref[...] = grad_ref[...].T
    total = jnp.zeros(dtab_ref.shape, jnp.float32)
    def products(head):
        low = head * HD
        value = project_ref[2 * model + low : 2 * model + low + HD]
        grad = (turned_ref[low : low + HD] * inverse_ref[0, head : head + 1]).astype(jnp.bfloat16)
        return grad, dot_tn(value, grad)[:KEYS]

    def score_grads(head, product):
        weights = weights_ref[0, head].astype(jnp.float32)
        terms = weights * product
        inner = jnp.sum(terms, axis=0, keepdims=True) * inverse_ref[0, head : head + 1]
        return (terms - weights * inner).astype(jnp.bfloat16)

    def wide_grads(head, grad, grad_scores):
        low = head * HD
        query = project_ref[low : low + HD]
        key = project_ref[model + low : model + low + HD]
        key = jnp.concatenate([key, ind], axis=0)
        grad_wide = dot(key[:, :KEYS], grad_scores)
        grad_value = dot_nt(grad, weights_ref[0, head])
        grad_key = dot_nt(query, grad_scores) * scale
        out_ref[model + low : model + low + HD, :KEYS] = grad_key.astype(jnp.bfloat16)
        out_ref[2 * model + low : 2 * model + low + HD, :KEYS] = grad_value.astype(jnp.bfloat16)
        return grad_wide

    def offset_grads(head, grad_wide, total):
        low = head * HD
        query = project_ref[low : low + HD]
        rows = grad_wide[HD : HD + SIDE]
        cols = grad_wide[HD + SIDE : HD + 2 * SIDE]
        spread = jnp.concatenate(
            [jnp.where(lane // SIDE == a, rows, 0.0) for a in range(WIN)]
            + [jnp.where(lane % SIDE == b, cols, 0.0) for b in range(WIN)],
            axis=0,
        ).astype(jnp.bfloat16)
        grad_query = grad_wide[:HD] * scale + dot_tn(tab, spread)
        out_ref[low : low + HD] = grad_query.astype(jnp.bfloat16)
        return total + dot_nt(spread, query)

    for first in range(0, HALF, GROUP):
        heads = range(first, first + GROUP)
        pairs = [products(head) for head in heads]
        pairs = [
            (grad, score_grads(head, product)) for head, (grad, product) in zip(heads, pairs)
        ]
        grads = [wide_grads(head, *pair) for head, pair in zip(heads, pairs)]
        for head, grad_wide in zip(heads, grads):
            total = offset_grads(head, grad_wide, total)
    out_ref[model:, KEYS:] = jnp.zeros((2 * model, TOK - KEYS), jnp.bfloat16)
    dtab_ref[...] += total


def attention_backward(project, weights, inverse, grad, tab, ind, half):
    model = project.shape[0] // 6
    slots = project.shape[1] // TOK
    return pl.pallas_call(
        attention_backward_kernel,
        grid=(slots,),
        in_specs=[
            pl.BlockSpec((3 * model, TOK), lambda i: (half, i)),
            pl.BlockSpec((1, HALF, KEYS, TOK), lambda i: (i, half, 0, 0)),
            pl.BlockSpec((1, HALF, TOK), lambda i: (i, half, 0)),
            pl.BlockSpec((TOK, model), lambda i: (i, half)),
            pl.BlockSpec((2 * KEYS, HD), lambda i: (0, 0)),
            pl.BlockSpec((DEPTH - HD, TOK), lambda i: (0, 0)),
        ],
        out_specs=[
            pl.BlockSpec((3 * model, TOK), lambda i: (0, i)),
            pl.BlockSpec((2 * KEYS, HD), lambda i: (0, 0)),
        ],
        out_shape=[
            jax.ShapeDtypeStruct((3 * model, slots * TOK), jnp.bfloat16),
            jax.ShapeDtypeStruct((2 * KEYS, HD), jnp.float32),
        ],
        scratch_shapes=[pltpu.VMEM((model, TOK), jnp.bfloat16)],
        compiler_params=pltpu.CompilerParams(vmem_limit_bytes=60 * MIB),
        cost_estimate=pl.CostEstimate(
            flops=slots * 2_500_000_000, bytes_accessed=slots * 4 * MIB, transcendentals=0
        ),
    )(project, weights, inverse, grad, tab, ind)


def write_placed(table_ref, kept_ref, sent_ref, core_stride, write):
    devices = table_ref.shape[0] - 1
    for core in (0, 1):

        @pl.when(table_ref[devices] == core)
        def _():
            def write_block(block, rows, value):
                place = table_ref[block]
                if block // core_stride % 2 == core:
                    kept_ref[place, rows] = value
                else:
                    sent_ref[place - devices // 2, rows] = value

            write(write_block)


def mlp_kernel(rows, begins, ends, placed, core_stride, *refs):
    if placed:
        table_ref, *refs = refs
    normed_ref, cot_ref, up_ref, down_ref, shift_ref, mixed0_ref, grad0_ref = refs[:7]
    last_ref, mixed_ref, grad_ref, dup_ref, ddown_ref, dshift_ref = refs[7:13]
    active_ref, hidden_ref = refs[13:15]
    sum_ref = refs[15] if ends else mixed_ref
    tokens = normed_ref.shape[0]
    step = pl.program_id(0) * pl.num_programs(1) + pl.program_id(1)

    @pl.when(step == 0)
    def _():
        sum_ref[...] = jnp.zeros_like(sum_ref)
        grad_ref[...] = jnp.zeros_like(grad_ref)

    piece = mixed0_ref.shape[0]

    @pl.when(step < tokens // piece)
    def _():
        place = pl.ds(pl.multiple_of(step * piece, piece), piece)
        sum_ref[place] += mixed0_ref[...]
        if not begins:
            grad_ref[place] += grad0_ref[...]

    up = up_ref[...]
    down = down_ref[...]
    shift = shift_ref[...]
    total = jnp.zeros(shift.shape, jnp.float32)
    for step_rows in range(tokens // rows):
        part = slice(step_rows * rows, (step_rows + 1) * rows)
        hidden = dot(normed_ref[part], up) + shift
        grad_active = dot_nt(cot_ref[part], down)
        half = 0.5 + 0.5 * lax.erf(hidden * 0.5**0.5)
        active = (hidden * half).astype(jnp.bfloat16)
        slope = half + hidden * jnp.exp(hidden * hidden * -0.5) * (2 * np.pi) ** -0.5
        grad_hidden = (grad_active * slope).astype(jnp.bfloat16)
        active_ref[part] = active
        hidden_ref[part] = grad_hidden
        total = total + jnp.sum(grad_hidden.astype(jnp.float32), axis=0, keepdims=True)
        sum_ref[part] += dot(active, down)
        grad_ref[part] += dot_nt(grad_hidden, up)
    dshift_ref[...] = total
    grad_down = dot_tn(active_ref[...], cot_ref[...]).astype(jnp.bfloat16)
    grad_up = dot_tn(normed_ref[...], hidden_ref[...]).astype(jnp.bfloat16)
    if not placed:
        ddown_ref[...] = grad_down
        dup_ref[...] = grad_up
    else:
        devices = table_ref.shape[0] - 1
        share, wide = grad_up.shape[0] // devices, grad_up.shape[1]
        steps = grad_up.shape[0] // wide
        for index in range(steps):

            @pl.when(pl.program_id(1) == index)
            def _():
                def write(write_block):
                    for block in range(devices):
                        part = grad_up[block * share : (block + 1) * share]
                        write_block(block, slice(index * share, (index + 1) * share), part)
                    for block in range(devices // steps):
                        part = grad_down[block * share : (block + 1) * share]
                        for n in range(steps):
                            low = (steps + n) * share
                            piece = part[:, n * wide : (n + 1) * wide]
                            place = index * devices // steps + block
                            write_block(place, slice(low, low + share), piece)

                write_placed(table_ref, ddown_ref, dup_ref, core_stride, write)
    if ends:

        @pl.when(step == pl.num_programs(0) * pl.num_programs(1) - 1)
        def _():
            mixed_ref[...] = (sum_ref[...] + last_ref[...]).astype(jnp.bfloat16)


def mlp(normed, cot, joint, shift, mixed0, grad0, last, first, count, table):
    tokens, model = normed.shape
    devices = table.shape[0] - 1
    share = model // devices
    steps = 2
    block = model // steps
    begins, ends = first == 0, first + count == PARTS
    placed = share % 8 == 0
    if placed:
        shape = (devices // 2, count * 2 * steps * share, block)
        shapes = [jax.ShapeDtypeStruct(shape, jnp.bfloat16)] * 2
        spec = pl.BlockSpec((devices // 2, 2 * steps * share, block), lambda p, i, *_: (0, p, 0))
        specs = [spec, spec]
    else:
        shapes = [
            jax.ShapeDtypeStruct((model, count * model), jnp.bfloat16),
            jax.ShapeDtypeStruct((count * model, model), jnp.bfloat16),
        ]
        specs = [
            pl.BlockSpec((model, block), lambda p, i, *_: (0, p * steps + i)),
            pl.BlockSpec((block, model), lambda p, i, *_: (p * steps + i, 0)),
        ]
    pieces = count * steps
    piece = pl.BlockSpec((tokens // pieces, model), lambda p, i, *_: (p * steps + i, 0))
    once = pl.Buffered(1)
    whole = pl.BlockSpec((tokens, model), lambda p, i, *_: (0, 0), pipeline_mode=once)
    core_stride = lax.axis_size("rows") * lax.axis_size("cols")
    mixed, grad, sent, kept, grad_shift = pl.pallas_call(
        functools.partial(mlp_kernel, tokens // 2, begins, ends, placed, core_stride),
        grid_spec=pltpu.PrefetchScalarGridSpec(
            num_scalar_prefetch=1 if placed else 0,
            grid=(count, steps),
            in_specs=[
                whole,
                whole,
                pl.BlockSpec((model, block), lambda p, i, *_: (0, p * steps + i)),
                pl.BlockSpec((block, model), lambda p, i, *_: (i, count + p)),
                pl.BlockSpec((1, block), lambda p, i, *_: (0, (first + p) * steps + i)),
                piece,
                pl.BlockSpec((8, LANES), lambda p, i, *_: (0, 0)) if begins else piece,
                pl.BlockSpec((1, model), lambda p, i, *_: (0, 0)),
            ],
            out_specs=[
                whole,
                whole,
                specs[0],
                specs[1],
                pl.BlockSpec((1, block), lambda p, i, *_: (0, p * steps + i)),
            ],
            scratch_shapes=[pltpu.VMEM((tokens, block), jnp.bfloat16)] * 2
            + ([pltpu.VMEM((tokens, model), jnp.float32)] if ends else []),
        ),
        out_shape=[
            jax.ShapeDtypeStruct((tokens, model), jnp.bfloat16 if ends else jnp.float32),
            jax.ShapeDtypeStruct((tokens, model), jnp.float32),
            shapes[0],
            shapes[1],
            jax.ShapeDtypeStruct((1, count * model), jnp.float32),
        ],
        compiler_params=pltpu.CompilerParams(vmem_limit_bytes=62 * MIB),
        cost_estimate=pl.CostEstimate(
            flops=16 * tokens * model * model * count,
            bytes_accessed=8 * model * model * count + 24 * tokens * model,
            transcendentals=2 * tokens * model * count,
        ),
    )(*([table] if placed else []), normed, cot, joint, joint, shift, mixed0, grad0, last)
    if placed:
        return mixed, grad, (sent, kept), grad_shift
    down = kept.reshape(count, devices, share, model).transpose(1, 0, 2, 3)
    parts = [sent.reshape(devices, share, -1), down.reshape(devices, -1, model)]
    return mixed, grad, parts, grad_shift


def token_gradient_kernel(grad_ref, weight_ref, out_ref):
    out_ref[...] = dot(weight_ref[...], grad_ref[...]).astype(jnp.bfloat16).T


def token_gradient(grad, weight, half):
    wide, tokens = grad.shape
    model = weight.shape[0]
    return pl.pallas_call(
        token_gradient_kernel,
        grid=(tokens // TOK,),
        in_specs=[
            pl.BlockSpec((wide, TOK), lambda i: (0, i)),
            pl.BlockSpec((model, wide), lambda i: (0, half), pipeline_mode=pl.Buffered(1)),
        ],
        out_specs=pl.BlockSpec((TOK, model), lambda i: (i, 0)),
        out_shape=jax.ShapeDtypeStruct((tokens, model), jnp.bfloat16),
        compiler_params=pltpu.CompilerParams(vmem_limit_bytes=40 * MIB),
        cost_estimate=pl.CostEstimate(
            flops=2 * tokens * model * wide,
            bytes_accessed=2 * (wide * tokens + model * wide + tokens * model),
            transcendentals=0,
        ),
    )(grad, weight)


def window_gradient_kernel(own, core_stride, table_ref, *refs):
    tokens_ref, grad_ref, *ready, sent_ref, kept_ref, sums_ref = refs
    devices = table_ref.shape[0] - 1
    share = tokens_ref.shape[1] // devices
    step = pl.program_id(0)

    def place(value):
        def write(write_block):
            for block in range(devices):
                part = value[block * share : (block + 1) * share]
                write_block(block, slice(0, share), part)

        write_placed(table_ref, kept_ref, sent_ref, core_stride, write)

    @pl.when(step < own)
    def _():
        place(dot(grad_ref[...], tokens_ref[...]).astype(jnp.bfloat16).T)
        total = 0
        for low in range(0, grad_ref.shape[1], LANES):
            total = total + grad_ref[:, low : low + LANES].astype(jnp.float32)
        sums_ref[...] = total

    for ready_ref in ready:

        @pl.when(step >= own)
        def _():
            place(ready_ref[...])


def window_gradient(rows, grad, ready, table):
    tokens, model = rows.shape
    devices = table.shape[0] - 1
    wide = model // 2
    own = grad.shape[0] // wide
    steps = own + sum(one.shape[1] // wide for one in ready)
    shape = jax.ShapeDtypeStruct((devices // 2, model // devices, steps * wide), jnp.bfloat16)
    spec = pl.BlockSpec((devices // 2, model // devices, wide), lambda n, *_: (0, 0, n))
    core_stride = lax.axis_size("rows") * lax.axis_size("cols")
    return pl.pallas_call(
        functools.partial(window_gradient_kernel, own, core_stride),
        grid_spec=pltpu.PrefetchScalarGridSpec(
            num_scalar_prefetch=1,
            grid=(steps,),
            in_specs=[
                pl.BlockSpec((tokens, model), lambda n, *_: (0, 0), pipeline_mode=pl.Buffered(1)),
                pl.BlockSpec((wide, tokens), lambda n, *_: (jnp.minimum(n, own - 1), 0)),
            ]
            + [pl.BlockSpec((model, wide), lambda n, *_: (0, jnp.maximum(n - own, 0)))] * len(ready),
            out_specs=[
                spec,
                spec,
                pl.BlockSpec((wide, LANES), lambda n, *_: (jnp.minimum(n, own - 1), 0)),
            ],
        ),
        out_shape=[shape, shape, jax.ShapeDtypeStruct((own * wide, LANES), jnp.float32)],
        compiler_params=pltpu.CompilerParams(vmem_limit_bytes=56 * MIB),
        cost_estimate=pl.CostEstimate(
            flops=2 * tokens * model * own * wide,
            bytes_accessed=2 * (tokens * model + tokens * own * wide + model * steps * wide),
            transcendentals=0,
        ),
    )(table, rows, grad, *ready)


def hidden_parts(unit):
    return 5 if unit % 160 == 0 else 1


def normalised(values):
    average = jnp.mean(values, axis=-1, keepdims=True)
    centered = values - average
    variance = jnp.mean(centered * centered, axis=-1, keepdims=True)
    inverse = lax.rsqrt(variance + eps)
    return centered * inverse, inverse


def norm_backward(unit, inverse, gain, grad):
    scaled = grad * gain
    return inverse * (
        scaled
        - jnp.mean(scaled, axis=-1, keepdims=True)
        - unit * jnp.mean(scaled * unit, axis=-1, keepdims=True)
    )


def column_sum(value):
    return jnp.sum(value, axis=0, keepdims=True)


def row_block(tokens):
    return tokens // 4


def row_norm_kernel(rows_ref, vectors_ref, out_ref):
    unit, _ = normalised(rows_ref[...].astype(jnp.float32))
    out_ref[...] = (unit * vectors_ref[0:1] + vectors_ref[1:2]).astype(jnp.bfloat16)


def row_norm(rows, vectors):
    tokens, model = rows.shape
    block = pl.BlockSpec((row_block(tokens), model), lambda i: (i, 0))
    return pl.pallas_call(
        row_norm_kernel,
        grid=(4,),
        in_specs=[block, pl.BlockSpec((8, model), lambda i: (0, 0))],
        out_specs=block,
        out_shape=jax.ShapeDtypeStruct((tokens, model), jnp.bfloat16),
        cost_estimate=pl.CostEstimate(
            flops=8 * tokens * model, bytes_accessed=4 * tokens * model, transcendentals=0
        ),
    )(rows, vectors)


def middle_kernel(attended_ref, proj_ref, image_ref, vectors_ref, middle_ref, normed_ref):
    branch = dot(attended_ref[...], proj_ref[...]) + vectors_ref[0:1]
    middle = image_ref[...].astype(jnp.float32) + branch
    unit, _ = normalised(middle)
    normed = (unit * vectors_ref[1:2] + vectors_ref[2:3]).astype(jnp.bfloat16)
    middle_ref[...] = middle
    normed_ref[...] = normed


def middle_forward(attended, proj, image, vectors):
    tokens, model = attended.shape
    rows = row_block(tokens)
    block = pl.BlockSpec((rows, model), lambda i: (i, 0))
    return pl.pallas_call(
        middle_kernel,
        grid=(tokens // rows,),
        in_specs=[
            block,
            pl.BlockSpec((model, model), lambda i: (0, PARTS)),
            block,
            pl.BlockSpec((8, model), lambda i: (0, 0)),
        ],
        out_specs=[block, block],
        out_shape=[
            jax.ShapeDtypeStruct((tokens, model), jnp.float32),
            jax.ShapeDtypeStruct((tokens, model), jnp.bfloat16),
        ],
        compiler_params=pltpu.CompilerParams(vmem_limit_bytes=40 * MIB),
        cost_estimate=pl.CostEstimate(
            flops=2 * tokens * model * model, bytes_accessed=12 * tokens * model, transcendentals=0
        ),
    )(attended, proj, image, vectors)


def middle_backward_kernel(
    grad_ref, middle_ref, cot_ref, attended_ref, proj_ref, vectors_ref,
    grad_middle_ref, grad_attended_ref, dproj_ref, sums_ref, branch_ref,
):
    step = pl.program_id(0)

    @pl.when(step == 0)
    def _():
        sums_ref[...] = jnp.zeros_like(sums_ref)

    rows = middle_ref.shape[0]
    unit, inverse = normalised(middle_ref[...])
    grad = grad_ref[...]
    cot = cot_ref[...].astype(jnp.float32)
    grad_middle = cot + norm_backward(unit, inverse, vectors_ref[1:2], grad)
    branch = grad_middle.astype(jnp.bfloat16)
    grad_middle_ref[...] = grad_middle
    branch_ref[pl.ds(pl.multiple_of(step * rows, rows), rows)] = branch
    grad_attended_ref[...] = dot_nt(branch, proj_ref[...]).astype(jnp.bfloat16)
    sums_ref[0:1] += column_sum(branch.astype(jnp.float32))
    sums_ref[1:2] += column_sum(grad * unit)
    sums_ref[2:3] += column_sum(grad)
    sums_ref[3:4] += column_sum(cot)

    @pl.when(step == pl.num_programs(0) - 1)
    def _():
        dproj_ref[...] = dot_tn(attended_ref[...], branch_ref[...]).astype(jnp.bfloat16)


def middle_backward(grad, middle, cot, attended, proj, vectors):
    tokens, model = attended.shape
    rows = row_block(tokens)
    block = pl.BlockSpec((rows, model), lambda i: (i, 0))
    few = pl.BlockSpec((8, model), lambda i: (0, 0))
    return pl.pallas_call(
        middle_backward_kernel,
        grid=(tokens // rows,),
        in_specs=[
            block, block, block,
            pl.BlockSpec((tokens, model), lambda i: (0, 0), pipeline_mode=pl.Buffered(1)),
            pl.BlockSpec((model, model), lambda i: (0, PARTS), pipeline_mode=pl.Buffered(1)),
            few,
        ],
        out_specs=[block, block, pl.BlockSpec((model, model), lambda i: (0, 0)), few],
        out_shape=[
            jax.ShapeDtypeStruct((tokens, model), jnp.float32),
            jax.ShapeDtypeStruct((tokens, model), jnp.bfloat16),
            jax.ShapeDtypeStruct((model, model), jnp.bfloat16),
            jax.ShapeDtypeStruct((8, model), jnp.float32),
        ],
        scratch_shapes=[pltpu.VMEM((tokens, model), jnp.bfloat16)],
        compiler_params=pltpu.CompilerParams(vmem_limit_bytes=56 * MIB),
        cost_estimate=pl.CostEstimate(
            flops=4 * tokens * model * model, bytes_accessed=24 * tokens * model, transcendentals=0
        ),
    )(grad, middle, cot, attended, proj, vectors)


def image_backward_kernel(
    rows_ref, first_ref, second_ref, grad_middle_ref, vectors_ref, out_ref, sums_ref
):
    @pl.when(pl.program_id(0) == 0)
    def _():
        sums_ref[...] = jnp.zeros_like(sums_ref)

    unit, inverse = normalised(rows_ref[...].astype(jnp.float32))
    grad = first_ref[...].astype(jnp.float32) + second_ref[...].astype(jnp.float32)
    total = grad_middle_ref[...] + norm_backward(unit, inverse, vectors_ref[0:1], grad)
    out_ref[...] = total.astype(jnp.bfloat16)
    sums_ref[0:1] += column_sum(grad * unit)
    sums_ref[1:2] += column_sum(grad)


def image_backward(rows, first, second, grad_middle, vectors):
    tokens, model = rows.shape
    block = pl.BlockSpec((row_block(tokens), model), lambda i: (i, 0))
    few = pl.BlockSpec((8, model), lambda i: (0, 0))
    return pl.pallas_call(
        image_backward_kernel,
        grid=(4,),
        in_specs=[block, block, block, block, few],
        out_specs=[block, few],
        out_shape=[
            jax.ShapeDtypeStruct((tokens, model), jnp.bfloat16),
            jax.ShapeDtypeStruct((8, model), jnp.float32),
        ],
        cost_estimate=pl.CostEstimate(
            flops=12 * tokens * model, bytes_accessed=10 * tokens * model, transcendentals=0
        ),
    )(rows, first, second, grad_middle, vectors)


def main_place(width):
    col = lax.broadcasted_iota(jnp.int32, (width, NWIN * SIDE), 0)
    slot = lax.broadcasted_iota(jnp.int32, (width, NWIN * SIDE), 1)
    inside = slot % SIDE < WIN
    return (inside & (col == slot // SIDE * WIN + slot % SIDE)).astype(jnp.bfloat16)


def end_starts(width, count):
    return [b * WIN for b in range(count - 1)] + [width - END]


def end_place(width):
    count = lax.axis_size("rows")
    row = lax.axis_index("rows")
    start = jnp.array(end_starts(width, count))[row]
    col = start + lax.broadcasted_iota(jnp.int32, (END, 2 * SIDE), 0)
    slot = lax.broadcasted_iota(jnp.int32, (END, 2 * SIDE), 1)
    held = (slot % SIDE < WIN) & ((slot < SIDE) | (row == count - 1))
    window = row + slot // SIDE
    return (held & (col == window * WIN + slot % SIDE)).astype(jnp.bfloat16)


def to_windows_kernel(width, rest, rows_ref, main_ref, end_ref, out_ref):
    out_ref[...] = jnp.zeros_like(out_ref)
    for i in range(WIN):
        part = dot_tn(main_ref[...], rows_ref[i * width : (i + 1) * width]).astype(jnp.bfloat16)
        for b in range(NWIN):
            out_ref[b * TOK + i * SIDE : b * TOK + (i + 1) * SIDE] = part[b * SIDE : (b + 1) * SIDE]
    first = WIN * width
    for i in range(rest):
        part = rows_ref[first + i * END : first + (i + 1) * END]
        part = dot_tn(end_ref[...], part).astype(jnp.bfloat16)
        for b in range(2):
            place = (NWIN + b) * TOK + i * SIDE
            out_ref[place : place + SIDE] = part[b * SIDE : (b + 1) * SIDE]


def to_rows_kernel(width, rest, windows_ref, main_ref, end_ref, out_ref):
    for i in range(WIN):
        part = jnp.concatenate(
            [windows_ref[b * TOK + i * SIDE : b * TOK + (i + 1) * SIDE] for b in range(NWIN)],
            axis=0,
        )
        out_ref[i * width : (i + 1) * width] = dot(main_ref[...], part).astype(jnp.bfloat16)
    first = WIN * width
    for i in range(rest):
        part = jnp.concatenate(
            [
                windows_ref[b * TOK + i * SIDE : b * TOK + (i + 1) * SIDE]
                for b in range(NWIN, NWIN + 2)
            ],
            axis=0,
        )
        part = dot(end_ref[...], part).astype(jnp.bfloat16)
        out_ref[first + i * END : first + (i + 1) * END] = part


def rearranged(kernel, value, width, rest, tokens):
    model = value.shape[1]
    lanes = model // 5
    main, end = main_place(width), end_place(width)
    return pl.pallas_call(
        functools.partial(kernel, width, rest),
        grid=(5,),
        in_specs=[
            pl.BlockSpec((value.shape[0], lanes), lambda i: (0, i)),
            pl.BlockSpec(main.shape, lambda i: (0, 0)),
            pl.BlockSpec(end.shape, lambda i: (0, 0)),
        ],
        out_specs=pl.BlockSpec((tokens, lanes), lambda i: (0, i)),
        out_shape=jax.ShapeDtypeStruct((tokens, model), jnp.bfloat16),
        compiler_params=pltpu.CompilerParams(vmem_limit_bytes=32 * MIB),
        cost_estimate=pl.CostEstimate(
            flops=200 * tokens * model, bytes_accessed=6 * tokens * model, transcendentals=0
        ),
    )(value, main, end)


def axis_bits(axis):
    count = lax.axis_size(axis)
    return [(axis, 1 << bit) for bit in range(count.bit_length() - 1)]


def flipped(value, bit):
    axis, mask = bit
    return lax.ppermute(value, axis, [(i, i ^ mask) for i in range(lax.axis_size(axis))])


def bit_of(bit):
    axis, mask = bit
    return (lax.axis_index(axis) // mask) % 2


def device_bits():
    return [bit for axis in ALL for bit in reversed(axis_bits(axis))]


def after(value, others):
    return lax.optimization_barrier((value, others))[0]


def beside(flights, value, kernel):
    return sync(kernel(launch(value, flights)), flights)


class Flight:

    def __init__(self, steps):
        self.steps = steps
        self.sent = self.arrived = self.value = None
        self.flying = True

    def advance(self):
        try:
            self.sent, self.arrived = self.steps.send(self.arrived)
        except StopIteration as end:
            self.sent, self.arrived, self.flying = [], [], False
            self.value = end.value

    def finish(self):
        while self.flying:
            self.advance()
        return self.value


def launch(value, flights):
    for one in flights:
        if one.flying:
            one.advance()
    return after(value, [one.sent for one in flights])


def sync(value, flights):
    flights = [one for one in flights if one.flying]
    value, arrived = lax.optimization_barrier((value, [one.arrived for one in flights]))
    for one, pieces in zip(flights, arrived):
        one.arrived = pieces
    return value


def index_masks(bits):
    weights = {"cols": 1, "rows": lax.axis_size("cols")}
    weights["dp"] = weights["rows"] * lax.axis_size("rows")
    return [weights[axis] * mask for axis, mask in bits]


def halving_orders():
    dp, rows, cols = axis_bits("dp"), axis_bits("rows"), axis_bits("cols")
    core, chips = dp[:1], dp[1:]
    (core,) = index_masks(core)
    orders = [cols + chips + rows, chips + rows[:1] + cols + rows[1:]]
    return core, [index_masks(order) for order in orders]


def block_tables():
    core, orders = halving_orders()
    me = lax.axis_index(ALL)
    steps = len(orders[0])
    flips = []
    for order in orders:
        place = np.arange(1 << steps)
        flips.append(sum((place >> (steps - 1 - n) & 1) * mask for n, mask in enumerate(order)))
    flips = [jnp.asarray(flip, jnp.int32) for flip in flips]
    first = (me & core) == 0
    there = (me ^ core) ^ jnp.where(first, flips[1], flips[0])
    here = me ^ jnp.where(first, flips[0], flips[1])
    return there, here


def place_table():
    there, here = block_tables()
    blocks = jnp.concatenate([here, there])
    count = blocks.shape[0]
    hit = blocks[:, None] == jnp.arange(count)[None, :]
    places = jnp.sum(jnp.where(hit, jnp.arange(count)[:, None], 0), axis=0)
    core, _ = halving_orders()
    return jnp.concatenate([places, (lax.axis_index(ALL) // core % 2)[None]]).astype(jnp.int32)


def partner_permute(value, step):
    core, orders = halving_orders()
    pairs = []
    for index in range(lax.axis_size(ALL)):
        order = orders[(index & core) // core]
        pairs.append((index, index ^ (core if step == 0 else order[step - 1])))
    return lax.ppermute(value, ALL, pairs)


def packed_shape(parts):
    if len({part.shape[1] for part in parts}) == 1:
        return parts[0].shape[1], sum(part.shape[2] for part in parts)
    wide = 2 * LANES
    return sum(part.shape[1] * part.shape[2] // wide for part in parts), wide


def pack_into(refs, write):
    rows, wide = packed_shape(refs)
    side = rows == refs[0].shape[1]
    place = 0
    for ref in refs:
        height, width = ref.shape[1:]
        if side:
            write(slice(0, rows), slice(place, place + width), ref[0])
            place += width
            continue
        for low in range(0, width, wide):
            write(slice(place, place + height), slice(0, wide), ref[0, :, low : low + wide])
            place += height


def pack_kernel(table_ref, *refs):
    def write(rows, cols, value):
        refs[-1][0, rows, cols] = value

    pack_into(refs[:-1], write)


def pack(parts, table):
    count = table.shape[0]
    rows, wide = packed_shape(parts)
    return pl.pallas_call(
        pack_kernel,
        grid_spec=pltpu.PrefetchScalarGridSpec(
            num_scalar_prefetch=1,
            grid=(count,),
            in_specs=[
                pl.BlockSpec((1,) + part.shape[1:], lambda i, table: (table[i], 0, 0))
                for part in parts
            ],
            out_specs=pl.BlockSpec((1, rows, wide), lambda i, table: (i, 0, 0)),
        ),
        out_shape=jax.ShapeDtypeStruct((count, rows, wide), jnp.bfloat16),
        cost_estimate=pl.CostEstimate(
            flops=0, bytes_accessed=4 * count * rows * wide, transcendentals=0
        ),
    )(table, *parts)


def summed(sent, kept):
    held = [kept]
    size = 2 * kept.shape[0]
    step = 0
    while size > 1:
        if step:
            sent = sum(piece[size // 2 : size].astype(jnp.float32) for piece in held)
            sent = sent.astype(jnp.bfloat16)
        held = yield [sent], [partner_permute(sent, step)] + held
        size //= 2
        step += 1
    return sum(piece[0].astype(jnp.float32) for piece in held)


def summed_packed(parts):
    there, here = block_tables()
    total = yield from summed(pack(parts, there), pack(parts, here))
    shapes = [part.shape[1:] for part in parts]
    rows, wide = packed_shape(parts)
    out = []
    place = 0
    for height, width in shapes:
        if rows == height:
            out.append(total[:, place : place + width])
            place += width
        else:
            pieces = width // wide
            piece = total[place : place + pieces * height].reshape(pieces, height, wide)
            out.append(piece.transpose(1, 0, 2).reshape(height, width))
            place += pieces * height
    return out


def summed_mlp(parts, share):
    total = yield from summed(*parts)
    wide = total.shape[1]
    total = total.reshape(-1, 2, 2, share, wide)
    up = total[:, 0].transpose(2, 0, 1, 3).reshape(share, -1)
    down = total[:, 1].transpose(0, 2, 1, 3).reshape(-1, 2 * wide)
    return [up, down]


def summed_columns(sent, kept, widths):
    total = yield from summed(sent, kept)
    places = np.cumsum([0] + list(widths))
    return [total[:, low : low + width] for low, width in zip(places, widths)]


def all_sum(value):
    for bit in axis_bits("dp") + axis_bits("cols") + axis_bits("rows"):
        (arrived,) = yield [value], [flipped(value, bit)]
        value = value + arrived
    return value


def small_gather(value):
    for bit in reversed(device_bits()):
        arrived = flipped(value, bit)
        value = jnp.where(
            bit_of(bit) == 0,
            jnp.concatenate([value, arrived], axis=0),
            jnp.concatenate([arrived, value], axis=0),
        )
    return value


SWAP = [(0, 1), (1, 0)]


def split_tiles(tiles):
    col = lax.axis_index("cols")
    kept = lax.dynamic_index_in_dim(tiles, col, 0, keepdims=False)
    sent = lax.dynamic_index_in_dim(tiles, 1 - col, 0, keepdims=False)
    return kept, sent, lax.ppermute(sent, "cols", SWAP)


def join_tiles(kept, arrived):
    return jnp.where(
        lax.axis_index("cols") == 0,
        jnp.concatenate([kept, arrived], axis=1),
        jnp.concatenate([arrived, kept], axis=1),
    )


def split_image(image):
    col = lax.axis_index("cols")
    width = image.shape[1] // 2
    kept = lax.dynamic_slice_in_dim(image, col * width, width, 1)
    sent = lax.dynamic_slice_in_dim(image, (1 - col) * width, width, 1)
    return kept, sent, lax.ppermute(sent, "cols", SWAP)


def join_image(kept, arrived):
    return jnp.where(
        lax.axis_index("cols") == 0, jnp.stack([kept, arrived]), jnp.stack([arrived, kept])
    )


def halves_to_image(tiles):
    kept, _, arrived = split_tiles(tiles)
    return join_tiles(kept, arrived)


def image_to_halves(image):
    kept, _, arrived = split_image(image)
    return join_image(kept, arrived)


def column_windows(rows):
    width = rows.shape[1]
    parts = []
    for b in range(NWIN):
        piece = rows[:, b * WIN : min((b + 1) * WIN, width)]
        parts.append(jnp.pad(piece, ((0, 0), (0, SIDE - piece.shape[1]), (0, 0))))
    return jnp.stack(parts)


def column_rows(windows, width):
    parts = [windows[b, :, : min(WIN, width - b * WIN)] for b in range(len(windows))]
    return jnp.concatenate(parts, axis=1)


def pad_rows(value, top, bottom):
    widths = [(0, 0)] * value.ndim
    widths[-3] = (top, bottom)
    return jnp.pad(value, widths)


class Layout:

    def __init__(self, tiles):
        self.tiles = tiles
        _, self.height, tile_w, self.model = tiles
        self.width = 2 * tile_w
        self.count = lax.axis_size("rows")
        self.row = lax.axis_index("rows")
        self.near = self.count == NWIN - 1
        self.step = self.height - WIN
        self.halo = self.step * (self.count - 1)
        self.rest = self.height * self.count - WIN * self.count
        if self.near:
            self.slots = NWIN + 2
            self.tokens = WIN * self.width + self.rest * END
        else:
            self.slots = -(-NWIN * NWIN // self.count)
            self.tokens = 2 * self.height * tile_w

    def enter(self, tiles):
        if not self.near:
            return tiles.reshape(self.tokens, self.model)
        last, rest, halo = self.count - 1, self.rest, self.halo
        top = self.height - rest
        kept_low, sent_low, low = split_tiles(tiles[:, top:])
        (low,) = yield [sent_low], [low]
        lower = join_tiles(kept_low, low)
        kept_up, sent_up, up = split_tiles(after(tiles[:, :top], low))
        starts = end_starts(self.width, self.count)
        sent = [lower[rest - halo :]]
        arrived = [lax.ppermute(sent[0], "rows", [(i, i + 1) for i in range(last)])]
        for target in range(last):
            sent.append(lower[:, starts[target] : starts[target] + SIDE])
            arrived.append(lax.ppermute(sent[-1], "rows", [(last, target)]))
        up, down, *arrived = yield sent + [sent_up], [up] + arrived
        upper = join_tiles(kept_up, up)
        end = lower[:, starts[last] :]
        for target in range(last):
            piece = jnp.pad(arrived[target], ((0, 0), (0, END - SIDE), (0, 0)))
            end = jnp.where(self.row == target, piece, end)
        held = jnp.sum(end_place(self.width), axis=1).astype(jnp.bfloat16)
        end = end * held[None, :, None]
        whole = jnp.concatenate([down, upper, lower], axis=0)
        main = lax.dynamic_slice_in_dim(whole, halo - self.step * self.row, WIN, 0)
        return jnp.concatenate(
            [main.reshape(-1, self.model), end.reshape(-1, self.model)], axis=0
        )

    def leave(self, tokens, early):
        if not self.near:
            return tokens.reshape(self.tiles)
        last, rest, halo = self.count - 1, self.rest, self.halo
        top = self.height - rest
        width, model, step = self.width, self.model, self.step
        end = tokens[WIN * width :].reshape(rest, END, model)
        held = jnp.sum(end_place(width), axis=1).astype(jnp.bfloat16)
        end = end * held[None, :, None]
        up = tokens[: halo * width].reshape(halo, width, model)
        up = lax.ppermute(up, "rows", [(i + 1, i) for i in range(last)])
        piece = end[:, :SIDE]
        pieces = [lax.ppermute(piece, "rows", [(source, last)]) for source in range(last)]
        upper = lax.dynamic_slice_in_dim(tokens, step * self.row * width, top * width, 0)
        upper = upper.reshape(top, width, model)
        if early:
            kept_up, sent_up, arrived_up = split_image(upper)
            up, arrived_up, *pieces = yield [piece, sent_up], [up, arrived_up] + pieces
        else:
            up, *pieces = yield [piece], [up] + pieces
        tail = 0
        for start, piece in zip(end_starts(width, self.count), pieces + [end]):
            rest_wide = width - piece.shape[1] - start
            tail = tail + jnp.pad(piece, ((0, 0), (start, rest_wide), (0, 0)))
        below = jnp.where(self.row == last, tail, pad_rows(up, 0, rest - halo))
        whole = tokens[top * width : WIN * width].reshape(WIN - top, width, model)
        whole = jnp.concatenate([whole, below], axis=0)
        kept_low, sent_low, arrived_low = split_image(
            lax.dynamic_slice_in_dim(whole, step * self.row, rest, 0)
        )
        if early:
            (arrived_low,) = yield [sent_low], [arrived_low]
        else:
            kept_up, sent_up, arrived_up = split_image(upper)
            arrived_up, arrived_low = yield [sent_low, sent_up], [arrived_up, arrived_low]
        upper = join_image(kept_up, arrived_up)
        lower = join_image(kept_low, arrived_low)
        return jnp.concatenate([upper, lower], axis=1)

    def to_windows(self, tokens):
        if self.near:
            total = self.slots * TOK
            return rearranged(to_windows_kernel, tokens, self.width, self.rest, total)
        windows = column_windows(halves_to_image(tokens.reshape(self.tiles)))
        windows = lax.all_gather(windows, "rows", axis=1, tiled=True)
        extra = NWIN * WIN - windows.shape[1]
        windows = jnp.pad(windows, ((0, 0), (0, extra), (0, 0), (0, 0)))
        windows = windows.reshape(NWIN, NWIN, WIN, SIDE, self.model).transpose(1, 0, 2, 3, 4)
        windows = windows.reshape(NWIN * NWIN, WIN, SIDE, self.model)
        extra = self.slots * self.count - NWIN * NWIN
        windows = jnp.pad(windows, ((0, extra), (0, SIDE - WIN), (0, 0), (0, 0)))
        windows = lax.dynamic_slice_in_dim(windows, self.row * self.slots, self.slots, 0)
        return windows.reshape(self.slots * TOK, self.model)

    def to_rows(self, windows):
        if self.near:
            return rearranged(to_rows_kernel, windows, self.width, self.rest, self.tokens)
        windows = windows.reshape(self.slots, SIDE, SIDE, self.model)
        windows = lax.all_gather(windows[:, :WIN], "rows", axis=0, tiled=True)
        windows = windows[: NWIN * NWIN].reshape(NWIN, NWIN, WIN, SIDE, self.model)
        windows = windows.transpose(1, 0, 2, 3, 4).reshape(NWIN, NWIN * WIN, SIDE, self.model)
        windows = lax.dynamic_slice_in_dim(windows, self.row * self.height, self.height, 1)
        return image_to_halves(column_rows(windows, self.width)).reshape(self.tokens, self.model)


def shards(
    image_in,
    ln1_gain,
    ln1_bias,
    w_qkv,
    qv_bias,
    rel_rows,
    rel_cols,
    w_proj,
    proj_bias,
    ln2_gain,
    ln2_bias,
    w_fc1,
    fc1_bias,
    w_fc2,
    fc2_bias,
    cotangent,
):
    devices = lax.axis_size(ALL)
    me = lax.axis_index(ALL)
    model = image_in.shape[3]
    layout = Layout(image_in.shape)
    tokens = layout.tokens
    share = model // devices
    unit = fc1_bias.shape[0]

    rows = Flight(layout.enter(image_in))
    cot = Flight(layout.enter(cotangent))
    rows.advance()

    def gathered(shard):
        return lax.all_gather(shard, ALL, axis=0, tiled=True)

    vectors = [ln1_gain, ln1_bias, qv_bias[:, 0], qv_bias[:, 1], proj_bias, ln2_gain, ln2_bias]
    vectors = small_gather(jnp.concatenate(vectors + [fc2_bias, fc1_bias])[None])
    vectors = launch(sync(vectors, [rows]), [rows])
    w_fc1 = after(w_fc1, rows.sent)
    vectors = vectors.astype(jnp.float32)
    gain1, shift1, query_shift, value_shift, proj_shift, gain2, shift2, down_shift = (
        vectors[:, n * share : (n + 1) * share].reshape(1, model) for n in range(8)
    )
    norm_vectors = jnp.pad(jnp.concatenate([gain1, shift1], axis=0), ((0, 6), (0, 0)))
    middle_vectors = jnp.concatenate([proj_shift, gain2, shift2, down_shift], axis=0)
    middle_vectors = jnp.pad(middle_vectors, ((0, 4), (0, 0)))
    up_shift = vectors[:, 8 * share :].reshape(devices, PARTS, share)
    up_shift = up_shift.transpose(1, 0, 2).reshape(1, devices * unit)
    half = model // 2
    thirds = [w_qkv[:, n * half : (n + 1) * half] for n in (0, 2, 4, 1, 3, 5)]
    qkv_full = gathered(jnp.concatenate(thirds, axis=1))
    up_shard = w_fc1.reshape(share, devices, PARTS, share).transpose(0, 2, 1, 3)
    down_shard = [w_fc2[n * share : (n + 1) * share] for n in range(PARTS)]
    up_shard = up_shard.reshape(share, devices * unit)
    cut = PARTS // 2
    joint = gathered(
        jnp.concatenate([up_shard[:, : cut * model]] + down_shard[:cut] + [w_proj], axis=1)
    )
    joint2 = gathered(jnp.concatenate([up_shard[:, cut * model :]] + down_shard[cut:], axis=1))

    norm_vectors = sync(norm_vectors, [rows])
    rows = rows.finish()
    window_tokens = layout.to_windows(row_norm(rows, norm_vectors))
    nothing = jnp.zeros((1, half), jnp.float32)
    shift_qkv = jnp.concatenate(
        [query_shift[:, :half], nothing, value_shift[:, :half]]
        + [query_shift[:, half:], nothing, value_shift[:, half:]],
        axis=1,
    )
    window_tokens = launch(window_tokens, [cot])
    project = lax.dot_general(
        qkv_full, window_tokens, (((0,), (1,)), ((), ())), preferred_element_type=jnp.float32
    )
    project = (project + shift_qkv.reshape(3 * model, 1)).astype(jnp.bfloat16)
    project = sync(project, [cot])
    project = launch(project, [cot])
    tab = wide_tables(rel_rows, rel_cols)
    ind = key_indicator()
    attended_windows, weights, inverse = attention_forward(project, tab, ind)
    attended = layout.to_rows(attended_windows)
    attended, cot, joint = sync((attended, cot.finish(), joint), [])
    middle, normed2 = middle_forward(attended, joint, rows, middle_vectors)

    mixed = middle
    grad_normed2 = jnp.zeros((8, LANES), jnp.float32)
    table = place_table()
    sums = []
    shifts = []
    for first, count in ((0, 2), (2, 2)):

        def step(normed2):
            return mlp(
                normed2,
                cot,
                joint if first == 0 else joint2,
                up_shift,
                mixed,
                grad_normed2,
                down_shift,
                first,
                count,
                table,
            )

        if first:
            mixed = launch(mixed, sums)
            mixed, joint2 = sync((mixed, joint2), sums)
        mixed, grad_normed2, blocks, grad_shift = beside(sums, normed2, step)
        shifts.append(grad_shift.reshape(count, devices, share))
        if isinstance(blocks, list):
            sums.append(Flight(summed_packed(blocks)))
        else:
            sums.append(Flight(summed_mlp(blocks, share)))

    output = Flight(layout.leave(mixed, False))
    grad_normed2 = launch(grad_normed2, sums)
    grad_middle, grad_attended, grad_proj, middle_sums = sync(
        middle_backward(grad_normed2, middle, cot, attended, joint, middle_vectors), sums
    )

    def rows_of(vector):
        return vector.reshape(devices, -1)

    def attention_step(half):
        return attention_backward(project, weights, inverse, grad_windows, tab, ind, half)

    def project_step(grad_project, half):
        return token_gradient(grad_project, qkv_full, half)

    grad_windows = layout.to_windows(launch(grad_attended, sums + [output]))
    grad_project, grad_tab = sync(attention_step(0), sums[:1])
    grad_project = launch(grad_project, sums[:1])
    sent, kept, sums0 = sync(
        window_gradient(window_tokens, grad_project, [grad_proj], table), sums[1:] + [output]
    )
    sums.append(Flight(summed_columns(sent, kept, [3 * half, model])))
    grad_project = launch(grad_project, sums[1:] + [output])
    first_rows = layout.to_rows(project_step(grad_project, 0))
    first_rows, grad_windows = sync((first_rows, grad_windows), sums[:1] + sums[-1:])
    grad_windows = launch(grad_windows, sums[:1] + sums[-1:])
    grad_project, grad_part = sync(attention_step(1), sums[:-1] + [output])
    grad_project = launch(grad_project, sums[:-1])
    sent, kept, sums1 = sync(window_gradient(window_tokens, grad_project, [], table), sums)
    sums.append(Flight(summed_columns(sent, kept, [3 * half])))
    grad_project = launch(grad_project, sums)
    grad_tokens = sync(project_step(grad_project, 1), sums)
    second_rows = layout.to_rows(launch(grad_tokens, sums))
    grad_rows, norm_sums = sync(
        image_backward(rows, first_rows, second_rows, grad_middle, norm_vectors), sums
    )
    grad_in = Flight(layout.leave(grad_rows, True))
    grad_in.advance()
    norm_sums, *_ = sync([norm_sums] + grad_in.sent, sums)

    grad_sums = [jnp.sum(piece, axis=1) for piece in (sums0, sums1)]
    up_shift_sums = jnp.concatenate(shifts, axis=0).transpose(1, 0, 2).reshape(devices, unit)
    small = jnp.concatenate(
        [
            rows_of(norm_sums[0]),
            rows_of(norm_sums[1]),
            rows_of(jnp.concatenate([piece[:half] for piece in grad_sums])),
            rows_of(jnp.concatenate([piece[2 * half :] for piece in grad_sums])),
        ]
        + [rows_of(middle_sums[n]) for n in range(4)]
        + [up_shift_sums],
        axis=1,
    )
    shape = small.shape
    small = [small.reshape(-1)] + [
        table.reshape(-1) for table in narrow_tables(grad_tab + grad_part)
    ]
    small = Flight(all_sum(jnp.concatenate(small)))
    sums.append(small)

    def formatted(ups, downs):
        ups = [grad.reshape(share, -1, devices, share) for grad in ups]
        ups = jnp.concatenate(ups, axis=1).transpose(0, 2, 1, 3)
        return ups.reshape(share, devices * unit), jnp.concatenate(downs, axis=0)

    launch(grad_rows, sums)
    flat = [one.finish() for one in sums[:-3]]
    flat, output.arrived = sync((flat, output.arrived), sums)
    launch(flat, sums)
    grad_fc1, grad_fc2 = formatted(*zip(*flat))
    done = output.finish()
    grad_fc1, grad_fc2, done = sync((grad_fc1, grad_fc2, done), sums + [grad_in])
    launch(grad_fc1, [grad_in] + sums)
    first_qkv, sum_proj = sums[-3].finish()
    first_qkv, sum_proj = sync((first_qkv, sum_proj), sums + [grad_in])
    launch(first_qkv, [grad_in] + sums)
    (last_qkv,) = sums[-2].finish()
    small = small.finish()
    tables = small[shape[0] * shape[1] :].reshape(2, REL, HD)
    small = small[: shape[0] * shape[1]].reshape(shape)
    small = lax.dynamic_index_in_dim(small, me, 0, keepdims=False)
    thirds = [
        piece[:, n * half : (n + 1) * half] for n in range(3) for piece in (first_qkv, last_qkv)
    ]
    return (
        done,
        grad_in.finish().astype(jnp.float32),
        small[:share],
        small[share : 2 * share],
        jnp.concatenate(thirds, axis=1),
        jnp.stack([small[2 * share : 3 * share], small[3 * share : 4 * share]], axis=1),
        tables[0],
        tables[1],
        sum_proj,
        small[4 * share : 5 * share],
        small[5 * share : 6 * share],
        small[6 * share : 7 * share],
        grad_fc1,
        small[8 * share :],
        grad_fc2,
        small[7 * share : 8 * share],
    )


def solution(mesh):
    tile = P("dp", "rows", "cols", None)
    vector = P(ALL)
    matrix = P(ALL, None)
    in_specs = (
        tile, vector, vector, matrix, matrix, P(), P(), matrix, vector, vector, vector,
        matrix, vector, matrix, vector, tile,
    )
    out_specs = (
        tile, tile, vector, vector, matrix, matrix, P(), P(), matrix, vector, vector, vector,
        matrix, vector, matrix, vector,
    )
    return jax.shard_map(shards, mesh=mesh, in_specs=in_specs, out_specs=out_specs, check_vma=False)
```

```python
import functools

import jax
import jax.numpy as jnp
import numpy as np
from jax import lax
from jax.experimental import pallas as pl
from jax.experimental.pallas import tpu as pltpu
from jax.sharding import PartitionSpec as P

HEADS = 16
HALF = HEADS // 2
GROUP = 8
WIN = 14
NWIN = 5
SIDE = 16
HD = 80
KEYS = WIN * SIDE
TOK = SIDE * SIDE
LANES = 128
DEPTH = 128
REL = 2 * WIN - 1
NEG = -1e30
END = 24
ALL = ("dp", "rows", "cols")
MIB = 1024 * 1024
PARTS = 4

eps = 1e-06


def dot(a, b):
    return jnp.dot(a, b, preferred_element_type=jnp.float32)


def dot_nt(a, b):
    return lax.dot_general(a, b, (((1,), (1,)), ((), ())), preferred_element_type=jnp.float32)


def dot_tn(a, b):
    return lax.dot_general(a, b, (((0,), (0,)), ((), ())), preferred_element_type=jnp.float32)


def offset_onehot(dtype):
    a = jnp.arange(WIN)[:, None]
    i = jnp.arange(SIDE)[None, :]
    offset = jnp.where(i < WIN, a - i + WIN - 1, -1)
    return (offset[:, :, None] == jnp.arange(REL)).astype(dtype).reshape(KEYS, REL)


def wide_tables(rel_rows, rel_cols):
    onehot = offset_onehot(jnp.bfloat16)
    return jnp.concatenate(
        [dot(onehot, table).astype(jnp.bfloat16) for table in (rel_rows, rel_cols)], axis=0
    )


def narrow_tables(grad):
    onehot = offset_onehot(jnp.float32)
    return [
        lax.dot_general(
            onehot,
            grad[n * KEYS : (n + 1) * KEYS],
            (((0,), (0,)), ((), ())),
            precision=lax.Precision.HIGHEST,
        )
        for n in (0, 1)
    ]


def key_indicator():
    row = lax.broadcasted_iota(jnp.int32, (DEPTH - HD, TOK), 0)
    key = lax.broadcasted_iota(jnp.int32, (DEPTH - HD, TOK), 1)
    return ((row == key // SIDE) | (row - SIDE == key % SIDE)).astype(jnp.bfloat16)


def query_offsets(query, tab_ref, lane):
    halves = []
    for half in range(2):
        low = half * 8
        count = min(8, WIN - low)
        part = dot(
            tab_ref[low * SIDE : (low + count) * SIDE], query[:, half * LANES : (half + 1) * LANES]
        )
        rows = part[:SIDE]
        for a in range(1, count):
            rows = jnp.where(
                lane[:, :LANES] // SIDE == a, part[a * SIDE : (a + 1) * SIDE], rows
            )
        halves.append(rows)
    part = dot(tab_ref[KEYS:], query)
    cols = part[:SIDE]
    for b in range(1, WIN):
        cols = jnp.where(lane % SIDE == b, part[b * SIDE : (b + 1) * SIDE], cols)
    return jnp.concatenate(halves, axis=1), cols


def attention_forward_kernel(
    project_ref, tab_ref, ind_ref, attended_ref, weights_ref, inverse_ref, turned_ref
):
    model = turned_ref.shape[0]
    lane = lax.broadcasted_iota(jnp.int32, (SIDE, TOK), 1)
    sub = lax.broadcasted_iota(jnp.int32, (SIDE, TOK), 0)
    ind = ind_ref[...]
    scale = HD**-0.5
    zeros = jnp.zeros((DEPTH - HD - 2 * SIDE, TOK), jnp.bfloat16)

    def wide(head):
        place = head * HD
        query = project_ref[place : place + HD]
        key = project_ref[model + place : model + place + HD]
        rows, cols = query_offsets(query, tab_ref, lane)
        rows = (rows * HD**0.5).astype(jnp.bfloat16)
        cols = jnp.where(sub < WIN, cols * HD**0.5, NEG).astype(jnp.bfloat16)
        query = jnp.concatenate([query, rows, cols, zeros], axis=0)
        return jnp.concatenate([key, ind], axis=0), query

    def softmax(scores):
        maxima = jnp.max(scores, axis=0, keepdims=True)
        weights = jnp.exp((scores - maxima) * scale)
        inverse = 1.0 / jnp.sum(weights, axis=0, keepdims=True)
        return weights.astype(jnp.bfloat16), inverse

    for first in range(0, HEADS, GROUP):
        heads = range(first, first + GROUP)
        scores = [wide(head) for head in heads]
        scores = [dot_tn(key, query)[:KEYS] for key, query in scores]
        results = [softmax(one) for one in scores]
        for head, (weights, inverse) in zip(heads, results):
            low = head * HD
            place = 2 * model + head * HD
            weights_ref[0, head] = weights
            inverse_ref[0, head : head + 1] = inverse
            attended = dot(project_ref[place : place + HD, :KEYS], weights)
            turned_ref[low : low + HD] = (attended * inverse).astype(jnp.bfloat16)
    attended_ref[...] = turned_ref[...].T


def attention_forward(project, tab, ind):
    model = project.shape[0] // 3
    slots = project.shape[1] // TOK
    return pl.pallas_call(
        attention_forward_kernel,
        grid=(slots,),
        in_specs=[
            pl.BlockSpec((3 * model, TOK), lambda i: (0, i)),
            pl.BlockSpec((2 * KEYS, HD), lambda i: (0, 0)),
            pl.BlockSpec((DEPTH - HD, TOK), lambda i: (0, 0)),
        ],
        out_specs=[
            pl.BlockSpec((TOK, model), lambda i: (i, 0)),
            pl.BlockSpec((1, HEADS, KEYS, TOK), lambda i: (i, 0, 0, 0)),
            pl.BlockSpec((1, HEADS, TOK), lambda i: (i, 0, 0)),
        ],
        out_shape=[
            jax.ShapeDtypeStruct((slots * TOK, model), jnp.bfloat16),
            jax.ShapeDtypeStruct((slots, HEADS, KEYS, TOK), jnp.bfloat16),
            jax.ShapeDtypeStruct((slots, HEADS, TOK), jnp.float32),
        ],
        scratch_shapes=[pltpu.VMEM((model, TOK), jnp.bfloat16)],
        compiler_params=pltpu.CompilerParams(vmem_limit_bytes=60 * MIB),
        cost_estimate=pl.CostEstimate(
            flops=slots * 3_500_000_000,
            bytes_accessed=slots * 6 * MIB,
            transcendentals=slots * HEADS * KEYS * TOK,
        ),
    )(project, tab, ind)


def attention_backward_kernel(
    query_ref, key_ref, value_ref, weights_ref, inverse_ref, grad_ref, tab_ref, ind_ref, out_ref, dtab_ref, turned_ref
):
    model = turned_ref.shape[0]
    lane = lax.broadcasted_iota(jnp.int32, (SIDE, TOK), 1)
    ind = ind_ref[...]
    tab = tab_ref[...]
    scale = HD**-0.5

    @pl.when(pl.program_id(0) == 0)
    def _():
        dtab_ref[...] = jnp.zeros_like(dtab_ref)

    turned_ref[...] = grad_ref[...].T
    total = jnp.zeros(dtab_ref.shape, jnp.float32)
    def products(head):
        low = head * HD
        value = value_ref[low : low + HD]
        grad = (turned_ref[low : low + HD] * inverse_ref[0, head : head + 1]).astype(jnp.bfloat16)
        return grad, dot_tn(value, grad)[:KEYS]

    def score_grads(head, product):
        weights = weights_ref[0, head].astype(jnp.float32)
        terms = weights * product
        inner = jnp.sum(terms, axis=0, keepdims=True) * inverse_ref[0, head : head + 1]
        return (terms - weights * inner).astype(jnp.bfloat16)

    def wide_grads(head, grad, grad_scores):
        low = head * HD
        query = query_ref[low : low + HD]
        key = key_ref[low : low + HD]
        key = jnp.concatenate([key, ind], axis=0)
        grad_wide = dot(key[:, :KEYS], grad_scores)
        grad_value = dot_nt(grad, weights_ref[0, head])
        grad_key = dot_nt(query, grad_scores) * scale
        out_ref[model + low : model + low + HD, :KEYS] = grad_key.astype(jnp.bfloat16)
        out_ref[2 * model + low : 2 * model + low + HD, :KEYS] = grad_value.astype(jnp.bfloat16)
        return grad_wide

    def offset_grads(head, grad_wide, total):
        low = head * HD
        query = query_ref[low : low + HD]
        rows = grad_wide[HD : HD + SIDE]
        cols = grad_wide[HD + SIDE : HD + 2 * SIDE]
        spread = jnp.concatenate(
            [jnp.where(lane // SIDE == a, rows, 0.0) for a in range(WIN)]
            + [jnp.where(lane % SIDE == b, cols, 0.0) for b in range(WIN)],
            axis=0,
        ).astype(jnp.bfloat16)
        grad_query = grad_wide[:HD] * scale + dot_tn(tab, spread)
        out_ref[low : low + HD] = grad_query.astype(jnp.bfloat16)
        return total + dot_nt(spread, query)

    for first in range(0, HALF, GROUP):
        heads = range(first, first + GROUP)
        pairs = [products(head) for head in heads]
        pairs = [
            (grad, score_grads(head, product)) for head, (grad, product) in zip(heads, pairs)
        ]
        grads = [wide_grads(head, *pair) for head, pair in zip(heads, pairs)]
        for head, grad_wide in zip(heads, grads):
            total = offset_grads(head, grad_wide, total)
    out_ref[model:, KEYS:] = jnp.zeros((2 * model, TOK - KEYS), jnp.bfloat16)
    dtab_ref[...] += total


def attention_backward(project, weights, inverse, grad, tab, ind, half):
    model = project.shape[0] // 6
    slots = project.shape[1] // TOK
    return pl.pallas_call(
        attention_backward_kernel,
        grid=(slots,),
        in_specs=[
            pl.BlockSpec((model, TOK), lambda i: (half, i)),
            pl.BlockSpec((model, TOK), lambda i: (2 + half, i)),
            pl.BlockSpec((model, TOK), lambda i: (4 + half, i)),
            pl.BlockSpec((1, HALF, KEYS, TOK), lambda i: (i, half, 0, 0)),
            pl.BlockSpec((1, HALF, TOK), lambda i: (i, half, 0)),
            pl.BlockSpec((TOK, model), lambda i: (i, half)),
            pl.BlockSpec((2 * KEYS, HD), lambda i: (0, 0)),
            pl.BlockSpec((DEPTH - HD, TOK), lambda i: (0, 0)),
        ],
        out_specs=[
            pl.BlockSpec((3 * model, TOK), lambda i: (0, i)),
            pl.BlockSpec((2 * KEYS, HD), lambda i: (0, 0)),
        ],
        out_shape=[
            jax.ShapeDtypeStruct((3 * model, slots * TOK), jnp.bfloat16),
            jax.ShapeDtypeStruct((2 * KEYS, HD), jnp.float32),
        ],
        scratch_shapes=[pltpu.VMEM((model, TOK), jnp.bfloat16)],
        compiler_params=pltpu.CompilerParams(vmem_limit_bytes=60 * MIB),
        cost_estimate=pl.CostEstimate(
            flops=slots * 2_500_000_000, bytes_accessed=slots * 4 * MIB, transcendentals=0
        ),
    )(project, project, project, weights, inverse, grad, tab, ind)


def write_placed(table_ref, kept_ref, sent_ref, core_stride, write):
    devices = table_ref.shape[0] - 1
    for core in (0, 1):

        @pl.when(table_ref[devices] == core)
        def _():
            def write_block(block, rows, value):
                place = table_ref[block]
                if block // core_stride % 2 == core:
                    kept_ref[place, rows] = value
                else:
                    sent_ref[place - devices // 2, rows] = value

            write(write_block)


def mlp_kernel(rows, begins, ends, placed, core_stride, *refs):
    if placed:
        table_ref, *refs = refs
    normed_ref, cot_ref, up_ref, down_ref, shift_ref, mixed0_ref, grad0_ref = refs[:7]
    last_ref, mixed_ref, grad_ref, dup_ref, ddown_ref, dshift_ref = refs[7:13]
    active_ref, hidden_ref = refs[13:15]
    sum_ref = refs[15] if ends else mixed_ref
    tokens = normed_ref.shape[0]
    step = pl.program_id(0) * pl.num_programs(1) + pl.program_id(1)

    @pl.when(step == 0)
    def _():
        sum_ref[...] = jnp.zeros_like(sum_ref)
        grad_ref[...] = jnp.zeros_like(grad_ref)

    piece = mixed0_ref.shape[0]

    @pl.when(step < tokens // piece)
    def _():
        place = pl.ds(pl.multiple_of(step * piece, piece), piece)
        sum_ref[place] += mixed0_ref[...]
        if not begins:
            grad_ref[place] += grad0_ref[...]

    up = up_ref[...]
    down = down_ref[...]
    shift = shift_ref[...]
    total = jnp.zeros(shift.shape, jnp.float32)
    for step_rows in range(tokens // rows):
        part = slice(step_rows * rows, (step_rows + 1) * rows)
        hidden = dot(normed_ref[part], up) + shift
        grad_active = dot_nt(cot_ref[part], down)
        half = 0.5 + 0.5 * lax.erf(hidden * 0.5**0.5)
        active = (hidden * half).astype(jnp.bfloat16)
        slope = half + hidden * jnp.exp(hidden * hidden * -0.5) * (2 * np.pi) ** -0.5
        grad_hidden = (grad_active * slope).astype(jnp.bfloat16)
        active_ref[part] = active
        hidden_ref[part] = grad_hidden
        total = total + jnp.sum(grad_hidden.astype(jnp.float32), axis=0, keepdims=True)
        sum_ref[part] += dot(active, down)
        grad_ref[part] += dot_nt(grad_hidden, up)
    dshift_ref[...] = total
    grad_down = dot_tn(active_ref[...], cot_ref[...]).astype(jnp.bfloat16)
    grad_up = dot_tn(normed_ref[...], hidden_ref[...]).astype(jnp.bfloat16)
    if not placed:
        ddown_ref[...] = grad_down
        dup_ref[...] = grad_up
    else:
        devices = table_ref.shape[0] - 1
        share, wide = grad_up.shape[0] // devices, grad_up.shape[1]
        steps = grad_up.shape[0] // wide
        for index in range(steps):

            @pl.when(pl.program_id(1) == index)
            def _():
                def write(write_block):
                    for block in range(devices):
                        part = grad_up[block * share : (block + 1) * share]
                        write_block(block, slice(index * share, (index + 1) * share), part)
                    for block in range(devices // steps):
                        part = grad_down[block * share : (block + 1) * share]
                        for n in range(steps):
                            low = (steps + n) * share
                            piece = part[:, n * wide : (n + 1) * wide]
                            place = index * devices // steps + block
                            write_block(place, slice(low, low + share), piece)

                write_placed(table_ref, ddown_ref, dup_ref, core_stride, write)
    if ends:

        @pl.when(step == pl.num_programs(0) * pl.num_programs(1) - 1)
        def _():
            mixed_ref[...] = (sum_ref[...] + last_ref[...]).astype(jnp.bfloat16)


def mlp(normed, cot, joint, shift, mixed0, grad0, last, first, count, table):
    tokens, model = normed.shape
    devices = table.shape[0] - 1
    share = model // devices
    steps = 2
    block = model // steps
    begins, ends = first == 0, first + count == PARTS
    placed = share % 8 == 0
    if placed:
        shape = (devices // 2, count * 2 * steps * share, block)
        shapes = [jax.ShapeDtypeStruct(shape, jnp.bfloat16)] * 2
        spec = pl.BlockSpec((devices // 2, 2 * steps * share, block), lambda p, i, *_: (0, p, 0))
        specs = [spec, spec]
    else:
        shapes = [
            jax.ShapeDtypeStruct((model, count * model), jnp.bfloat16),
            jax.ShapeDtypeStruct((count * model, model), jnp.bfloat16),
        ]
        specs = [
            pl.BlockSpec((model, block), lambda p, i, *_: (0, p * steps + i)),
            pl.BlockSpec((block, model), lambda p, i, *_: (p * steps + i, 0)),
        ]
    pieces = count * steps
    piece = pl.BlockSpec((tokens // pieces, model), lambda p, i, *_: (p * steps + i, 0))
    once = pl.Buffered(1)
    whole = pl.BlockSpec((tokens, model), lambda p, i, *_: (0, 0), pipeline_mode=once)
    core_stride = lax.axis_size("rows") * lax.axis_size("cols")
    mixed, grad, sent, kept, grad_shift = pl.pallas_call(
        functools.partial(mlp_kernel, tokens // 2, begins, ends, placed, core_stride),
        grid_spec=pltpu.PrefetchScalarGridSpec(
            num_scalar_prefetch=1 if placed else 0,
            grid=(count, steps),
            in_specs=[
                whole,
                whole,
                pl.BlockSpec((model, block), lambda p, i, *_: (0, p * steps + i)),
                pl.BlockSpec((block, model), lambda p, i, *_: (i, count + p)),
                pl.BlockSpec((1, block), lambda p, i, *_: (0, (first + p) * steps + i)),
                piece,
                pl.BlockSpec((8, LANES), lambda p, i, *_: (0, 0)) if begins else piece,
                pl.BlockSpec((1, model), lambda p, i, *_: (0, 0)),
            ],
            out_specs=[
                whole,
                whole,
                specs[0],
                specs[1],
                pl.BlockSpec((1, block), lambda p, i, *_: (0, p * steps + i)),
            ],
            scratch_shapes=[pltpu.VMEM((tokens, block), jnp.bfloat16)] * 2
            + ([pltpu.VMEM((tokens, model), jnp.float32)] if ends else []),
        ),
        out_shape=[
            jax.ShapeDtypeStruct((tokens, model), jnp.bfloat16 if ends else jnp.float32),
            jax.ShapeDtypeStruct((tokens, model), jnp.float32),
            shapes[0],
            shapes[1],
            jax.ShapeDtypeStruct((1, count * model), jnp.float32),
        ],
        compiler_params=pltpu.CompilerParams(vmem_limit_bytes=62 * MIB),
        cost_estimate=pl.CostEstimate(
            flops=16 * tokens * model * model * count,
            bytes_accessed=8 * model * model * count + 24 * tokens * model,
            transcendentals=2 * tokens * model * count,
        ),
    )(*([table] if placed else []), normed, cot, joint, joint, shift, mixed0, grad0, last)
    if placed:
        return mixed, grad, (sent, kept), grad_shift
    down = kept.reshape(count, devices, share, model).transpose(1, 0, 2, 3)
    parts = [sent.reshape(devices, share, -1), down.reshape(devices, -1, model)]
    return mixed, grad, parts, grad_shift


def token_gradient_kernel(grad_ref, *refs):
    *weight_refs, out_ref = refs
    total = 0
    for n, weight_ref in enumerate(weight_refs):
        wide = weight_ref.shape[1]
        total = total + dot(weight_ref[...], grad_ref[n * wide : (n + 1) * wide])
    out_ref[...] = total.astype(jnp.bfloat16).T


def token_gradient(grad, weight, half):
    wide, tokens = grad.shape
    model = weight.shape[0]
    return pl.pallas_call(
        token_gradient_kernel,
        grid=(tokens // TOK,),
        in_specs=[
            pl.BlockSpec((wide, TOK), lambda i: (0, i)),
            *[
                pl.BlockSpec(
                    (model, wide // 3),
                    lambda i, n=n: (0, 2 * n + half),
                    pipeline_mode=pl.Buffered(1),
                )
                for n in range(3)
            ],
        ],
        out_specs=pl.BlockSpec((TOK, model), lambda i: (i, 0)),
        out_shape=jax.ShapeDtypeStruct((tokens, model), jnp.bfloat16),
        compiler_params=pltpu.CompilerParams(vmem_limit_bytes=40 * MIB),
        cost_estimate=pl.CostEstimate(
            flops=2 * tokens * model * wide,
            bytes_accessed=2 * (wide * tokens + model * wide + tokens * model),
            transcendentals=0,
        ),
    )(grad, weight, weight, weight)


def window_gradient_kernel(own, core_stride, table_ref, *refs):
    tokens_ref, grad_ref, *ready, sent_ref, kept_ref, sums_ref = refs
    devices = table_ref.shape[0] - 1
    share = tokens_ref.shape[1] // devices
    step = pl.program_id(0)

    def place(value):
        def write(write_block):
            for block in range(devices):
                part = value[block * share : (block + 1) * share]
                write_block(block, slice(0, share), part)

        write_placed(table_ref, kept_ref, sent_ref, core_stride, write)

    @pl.when(step < own)
    def _():
        place(dot(grad_ref[...], tokens_ref[...]).astype(jnp.bfloat16).T)
        total = 0
        for low in range(0, grad_ref.shape[1], LANES):
            total = total + grad_ref[:, low : low + LANES].astype(jnp.float32)
        sums_ref[...] = total

    for ready_ref in ready:

        @pl.when(step >= own)
        def _():
            place(ready_ref[...])


def window_gradient(rows, grad, ready, table):
    tokens, model = rows.shape
    devices = table.shape[0] - 1
    wide = model // 2
    own = grad.shape[0] // wide
    steps = own + sum(one.shape[1] // wide for one in ready)
    shape = jax.ShapeDtypeStruct((devices // 2, model // devices, steps * wide), jnp.bfloat16)
    spec = pl.BlockSpec((devices // 2, model // devices, wide), lambda n, *_: (0, 0, n))
    core_stride = lax.axis_size("rows") * lax.axis_size("cols")
    return pl.pallas_call(
        functools.partial(window_gradient_kernel, own, core_stride),
        grid_spec=pltpu.PrefetchScalarGridSpec(
            num_scalar_prefetch=1,
            grid=(steps,),
            in_specs=[
                pl.BlockSpec((tokens, model), lambda n, *_: (0, 0), pipeline_mode=pl.Buffered(1)),
                pl.BlockSpec((wide, tokens), lambda n, *_: (jnp.minimum(n, own - 1), 0)),
            ]
            + [pl.BlockSpec((model, wide), lambda n, *_: (0, jnp.maximum(n - own, 0)))] * len(ready),
            out_specs=[
                spec,
                spec,
                pl.BlockSpec((wide, LANES), lambda n, *_: (jnp.minimum(n, own - 1), 0)),
            ],
        ),
        out_shape=[shape, shape, jax.ShapeDtypeStruct((own * wide, LANES), jnp.float32)],
        compiler_params=pltpu.CompilerParams(vmem_limit_bytes=56 * MIB),
        cost_estimate=pl.CostEstimate(
            flops=2 * tokens * model * own * wide,
            bytes_accessed=2 * (tokens * model + tokens * own * wide + model * steps * wide),
            transcendentals=0,
        ),
    )(table, rows, grad, *ready)


def hidden_parts(unit):
    return 5 if unit % 160 == 0 else 1


def normalised(values):
    average = jnp.mean(values, axis=-1, keepdims=True)
    centered = values - average
    variance = jnp.mean(centered * centered, axis=-1, keepdims=True)
    inverse = lax.rsqrt(variance + eps)
    return centered * inverse, inverse


def norm_backward(unit, inverse, gain, grad):
    scaled = grad * gain
    return inverse * (
        scaled
        - jnp.mean(scaled, axis=-1, keepdims=True)
        - unit * jnp.mean(scaled * unit, axis=-1, keepdims=True)
    )


def column_sum(value):
    return jnp.sum(value, axis=0, keepdims=True)


def row_block(tokens):
    return tokens // 4


def row_norm_kernel(rows_ref, vectors_ref, out_ref):
    unit, _ = normalised(rows_ref[...].astype(jnp.float32))
    out_ref[...] = (unit * vectors_ref[0:1] + vectors_ref[1:2]).astype(jnp.bfloat16)


def row_norm(rows, vectors):
    tokens, model = rows.shape
    block = pl.BlockSpec((row_block(tokens), model), lambda i: (i, 0))
    return pl.pallas_call(
        row_norm_kernel,
        grid=(4,),
        in_specs=[block, pl.BlockSpec((8, model), lambda i: (0, 0))],
        out_specs=block,
        out_shape=jax.ShapeDtypeStruct((tokens, model), jnp.bfloat16),
        cost_estimate=pl.CostEstimate(
            flops=8 * tokens * model, bytes_accessed=4 * tokens * model, transcendentals=0
        ),
    )(rows, vectors)


def middle_kernel(attended_ref, proj_ref, image_ref, vectors_ref, middle_ref, normed_ref):
    branch = dot(attended_ref[...], proj_ref[...]) + vectors_ref[0:1]
    middle = image_ref[...].astype(jnp.float32) + branch
    unit, _ = normalised(middle)
    normed = (unit * vectors_ref[1:2] + vectors_ref[2:3]).astype(jnp.bfloat16)
    middle_ref[...] = middle
    normed_ref[...] = normed


def middle_forward(attended, proj, image, vectors):
    tokens, model = attended.shape
    rows = row_block(tokens)
    block = pl.BlockSpec((rows, model), lambda i: (i, 0))
    return pl.pallas_call(
        middle_kernel,
        grid=(tokens // rows,),
        in_specs=[
            block,
            pl.BlockSpec((model, model), lambda i: (0, PARTS)),
            block,
            pl.BlockSpec((8, model), lambda i: (0, 0)),
        ],
        out_specs=[block, block],
        out_shape=[
            jax.ShapeDtypeStruct((tokens, model), jnp.float32),
            jax.ShapeDtypeStruct((tokens, model), jnp.bfloat16),
        ],
        compiler_params=pltpu.CompilerParams(vmem_limit_bytes=40 * MIB),
        cost_estimate=pl.CostEstimate(
            flops=2 * tokens * model * model, bytes_accessed=12 * tokens * model, transcendentals=0
        ),
    )(attended, proj, image, vectors)


def middle_backward_kernel(
    grad_ref, middle_ref, cot_ref, attended_ref, proj_ref, vectors_ref,
    grad_middle_ref, grad_attended_ref, dproj_ref, sums_ref, branch_ref,
):
    step = pl.program_id(0)

    @pl.when(step == 0)
    def _():
        sums_ref[...] = jnp.zeros_like(sums_ref)

    rows = middle_ref.shape[0]
    unit, inverse = normalised(middle_ref[...])
    grad = grad_ref[...]
    cot = cot_ref[...].astype(jnp.float32)
    grad_middle = cot + norm_backward(unit, inverse, vectors_ref[1:2], grad)
    branch = grad_middle.astype(jnp.bfloat16)
    grad_middle_ref[...] = grad_middle
    branch_ref[pl.ds(pl.multiple_of(step * rows, rows), rows)] = branch
    grad_attended_ref[...] = dot_nt(branch, proj_ref[...]).astype(jnp.bfloat16)
    sums_ref[0:1] += column_sum(branch.astype(jnp.float32))
    sums_ref[1:2] += column_sum(grad * unit)
    sums_ref[2:3] += column_sum(grad)
    sums_ref[3:4] += column_sum(cot)

    @pl.when(step == pl.num_programs(0) - 1)
    def _():
        dproj_ref[...] = dot_tn(attended_ref[...], branch_ref[...]).astype(jnp.bfloat16)


def middle_backward(grad, middle, cot, attended, proj, vectors):
    tokens, model = attended.shape
    rows = row_block(tokens)
    block = pl.BlockSpec((rows, model), lambda i: (i, 0))
    few = pl.BlockSpec((8, model), lambda i: (0, 0))
    return pl.pallas_call(
        middle_backward_kernel,
        grid=(tokens // rows,),
        in_specs=[
            block, block, block,
            pl.BlockSpec((tokens, model), lambda i: (0, 0), pipeline_mode=pl.Buffered(1)),
            pl.BlockSpec((model, model), lambda i: (0, PARTS), pipeline_mode=pl.Buffered(1)),
            few,
        ],
        out_specs=[block, block, pl.BlockSpec((model, model), lambda i: (0, 0)), few],
        out_shape=[
            jax.ShapeDtypeStruct((tokens, model), jnp.float32),
            jax.ShapeDtypeStruct((tokens, model), jnp.bfloat16),
            jax.ShapeDtypeStruct((model, model), jnp.bfloat16),
            jax.ShapeDtypeStruct((8, model), jnp.float32),
        ],
        scratch_shapes=[pltpu.VMEM((tokens, model), jnp.bfloat16)],
        compiler_params=pltpu.CompilerParams(vmem_limit_bytes=56 * MIB),
        cost_estimate=pl.CostEstimate(
            flops=4 * tokens * model * model, bytes_accessed=24 * tokens * model, transcendentals=0
        ),
    )(grad, middle, cot, attended, proj, vectors)


def image_backward_kernel(
    rows_ref, first_ref, second_ref, grad_middle_ref, vectors_ref, out_ref, sums_ref
):
    @pl.when(pl.program_id(0) == 0)
    def _():
        sums_ref[...] = jnp.zeros_like(sums_ref)

    unit, inverse = normalised(rows_ref[...].astype(jnp.float32))
    grad = first_ref[...].astype(jnp.float32) + second_ref[...].astype(jnp.float32)
    total = grad_middle_ref[...] + norm_backward(unit, inverse, vectors_ref[0:1], grad)
    out_ref[...] = total.astype(jnp.bfloat16)
    sums_ref[0:1] += column_sum(grad * unit)
    sums_ref[1:2] += column_sum(grad)


def image_backward(rows, first, second, grad_middle, vectors):
    tokens, model = rows.shape
    block = pl.BlockSpec((row_block(tokens), model), lambda i: (i, 0))
    few = pl.BlockSpec((8, model), lambda i: (0, 0))
    return pl.pallas_call(
        image_backward_kernel,
        grid=(4,),
        in_specs=[block, block, block, block, few],
        out_specs=[block, few],
        out_shape=[
            jax.ShapeDtypeStruct((tokens, model), jnp.bfloat16),
            jax.ShapeDtypeStruct((8, model), jnp.float32),
        ],
        cost_estimate=pl.CostEstimate(
            flops=12 * tokens * model, bytes_accessed=10 * tokens * model, transcendentals=0
        ),
    )(rows, first, second, grad_middle, vectors)


def main_place(width):
    col = lax.broadcasted_iota(jnp.int32, (width, NWIN * SIDE), 0)
    slot = lax.broadcasted_iota(jnp.int32, (width, NWIN * SIDE), 1)
    inside = slot % SIDE < WIN
    return (inside & (col == slot // SIDE * WIN + slot % SIDE)).astype(jnp.bfloat16)


def end_starts(width, count):
    return [b * WIN for b in range(count - 1)] + [width - END]


def end_place(width):
    count = lax.axis_size("rows")
    row = lax.axis_index("rows")
    start = jnp.array(end_starts(width, count))[row]
    col = start + lax.broadcasted_iota(jnp.int32, (END, 2 * SIDE), 0)
    slot = lax.broadcasted_iota(jnp.int32, (END, 2 * SIDE), 1)
    held = (slot % SIDE < WIN) & ((slot < SIDE) | (row == count - 1))
    window = row + slot // SIDE
    return (held & (col == window * WIN + slot % SIDE)).astype(jnp.bfloat16)


def to_windows_kernel(width, rest, rows_ref, main_ref, end_ref, out_ref):
    out_ref[...] = jnp.zeros_like(out_ref)
    for i in range(WIN):
        part = dot_tn(main_ref[...], rows_ref[i * width : (i + 1) * width]).astype(jnp.bfloat16)
        for b in range(NWIN):
            out_ref[b * TOK + i * SIDE : b * TOK + (i + 1) * SIDE] = part[b * SIDE : (b + 1) * SIDE]
    first = WIN * width
    for i in range(rest):
        part = rows_ref[first + i * END : first + (i + 1) * END]
        part = dot_tn(end_ref[...], part).astype(jnp.bfloat16)
        for b in range(2):
            place = (NWIN + b) * TOK + i * SIDE
            out_ref[place : place + SIDE] = part[b * SIDE : (b + 1) * SIDE]


def to_rows_kernel(width, rest, windows_ref, main_ref, end_ref, out_ref):
    for i in range(WIN):
        part = jnp.concatenate(
            [windows_ref[b * TOK + i * SIDE : b * TOK + (i + 1) * SIDE] for b in range(NWIN)],
            axis=0,
        )
        out_ref[i * width : (i + 1) * width] = dot(main_ref[...], part).astype(jnp.bfloat16)
    first = WIN * width
    for i in range(rest):
        part = jnp.concatenate(
            [
                windows_ref[b * TOK + i * SIDE : b * TOK + (i + 1) * SIDE]
                for b in range(NWIN, NWIN + 2)
            ],
            axis=0,
        )
        part = dot(end_ref[...], part).astype(jnp.bfloat16)
        out_ref[first + i * END : first + (i + 1) * END] = part


def rearranged(kernel, value, width, rest, tokens):
    model = value.shape[1]
    lanes = model // 5
    main, end = main_place(width), end_place(width)
    return pl.pallas_call(
        functools.partial(kernel, width, rest),
        grid=(5,),
        in_specs=[
            pl.BlockSpec((value.shape[0], lanes), lambda i: (0, i)),
            pl.BlockSpec(main.shape, lambda i: (0, 0)),
            pl.BlockSpec(end.shape, lambda i: (0, 0)),
        ],
        out_specs=pl.BlockSpec((tokens, lanes), lambda i: (0, i)),
        out_shape=jax.ShapeDtypeStruct((tokens, model), jnp.bfloat16),
        compiler_params=pltpu.CompilerParams(vmem_limit_bytes=32 * MIB),
        cost_estimate=pl.CostEstimate(
            flops=200 * tokens * model, bytes_accessed=6 * tokens * model, transcendentals=0
        ),
    )(value, main, end)


def axis_bits(axis):
    count = lax.axis_size(axis)
    return [(axis, 1 << bit) for bit in range(count.bit_length() - 1)]


def flipped(value, bit):
    axis, mask = bit
    return lax.ppermute(value, axis, [(i, i ^ mask) for i in range(lax.axis_size(axis))])


def bit_of(bit):
    axis, mask = bit
    return (lax.axis_index(axis) // mask) % 2


def device_bits():
    return [bit for axis in ALL for bit in reversed(axis_bits(axis))]


def after(value, others):
    return lax.optimization_barrier((value, others))[0]


def beside(flights, value, kernel):
    return sync(kernel(launch(value, flights)), flights)


class Flight:

    def __init__(self, steps):
        self.steps = steps
        self.sent = self.arrived = self.value = None
        self.flying = True

    def advance(self):
        try:
            self.sent, self.arrived = self.steps.send(self.arrived)
        except StopIteration as end:
            self.sent, self.arrived, self.flying = [], [], False
            self.value = end.value

    def finish(self):
        while self.flying:
            self.advance()
        return self.value


def launch(value, flights):
    for one in flights:
        if one.flying:
            one.advance()
    return after(value, [one.sent for one in flights])


def sync(value, flights):
    flights = [one for one in flights if one.flying]
    value, arrived = lax.optimization_barrier((value, [one.arrived for one in flights]))
    for one, pieces in zip(flights, arrived):
        one.arrived = pieces
    return value


def index_masks(bits):
    weights = {"cols": 1, "rows": lax.axis_size("cols")}
    weights["dp"] = weights["rows"] * lax.axis_size("rows")
    return [weights[axis] * mask for axis, mask in bits]


def halving_orders():
    dp, rows, cols = axis_bits("dp"), axis_bits("rows"), axis_bits("cols")
    core, chips = dp[:1], dp[1:]
    (core,) = index_masks(core)
    orders = [cols + chips + rows, chips + rows[:1] + cols + rows[1:]]
    return core, [index_masks(order) for order in orders]


def block_tables():
    core, orders = halving_orders()
    me = lax.axis_index(ALL)
    steps = len(orders[0])
    flips = []
    for order in orders:
        place = np.arange(1 << steps)
        flips.append(sum((place >> (steps - 1 - n) & 1) * mask for n, mask in enumerate(order)))
    flips = [jnp.asarray(flip, jnp.int32) for flip in flips]
    first = (me & core) == 0
    there = (me ^ core) ^ jnp.where(first, flips[1], flips[0])
    here = me ^ jnp.where(first, flips[0], flips[1])
    return there, here


def place_table():
    there, here = block_tables()
    blocks = jnp.concatenate([here, there])
    count = blocks.shape[0]
    hit = blocks[:, None] == jnp.arange(count)[None, :]
    places = jnp.sum(jnp.where(hit, jnp.arange(count)[:, None], 0), axis=0)
    core, _ = halving_orders()
    return jnp.concatenate([places, (lax.axis_index(ALL) // core % 2)[None]]).astype(jnp.int32)


def partner_permute(value, step):
    core, orders = halving_orders()
    pairs = []
    for index in range(lax.axis_size(ALL)):
        order = orders[(index & core) // core]
        pairs.append((index, index ^ (core if step == 0 else order[step - 1])))
    return lax.ppermute(value, ALL, pairs)


def packed_shape(parts):
    if len({part.shape[1] for part in parts}) == 1:
        return parts[0].shape[1], sum(part.shape[2] for part in parts)
    wide = 2 * LANES
    return sum(part.shape[1] * part.shape[2] // wide for part in parts), wide


def pack_into(refs, write):
    rows, wide = packed_shape(refs)
    side = rows == refs[0].shape[1]
    place = 0
    for ref in refs:
        height, width = ref.shape[1:]
        if side:
            write(slice(0, rows), slice(place, place + width), ref[0])
            place += width
            continue
        for low in range(0, width, wide):
            write(slice(place, place + height), slice(0, wide), ref[0, :, low : low + wide])
            place += height


def pack_kernel(table_ref, *refs):
    def write(rows, cols, value):
        refs[-1][0, rows, cols] = value

    pack_into(refs[:-1], write)


def pack(parts, table):
    count = table.shape[0]
    rows, wide = packed_shape(parts)
    return pl.pallas_call(
        pack_kernel,
        grid_spec=pltpu.PrefetchScalarGridSpec(
            num_scalar_prefetch=1,
            grid=(count,),
            in_specs=[
                pl.BlockSpec((1,) + part.shape[1:], lambda i, table: (table[i], 0, 0))
                for part in parts
            ],
            out_specs=pl.BlockSpec((1, rows, wide), lambda i, table: (i, 0, 0)),
        ),
        out_shape=jax.ShapeDtypeStruct((count, rows, wide), jnp.bfloat16),
        cost_estimate=pl.CostEstimate(
            flops=0, bytes_accessed=4 * count * rows * wide, transcendentals=0
        ),
    )(table, *parts)


def summed(sent, kept):
    held = [kept]
    size = 2 * kept.shape[0]
    step = 0
    while size > 1:
        if step:
            sent = sum(piece[size // 2 : size].astype(jnp.float32) for piece in held)
            sent = sent.astype(jnp.bfloat16)
        held = yield [sent], [partner_permute(sent, step)] + held
        size //= 2
        step += 1
    return sum(piece[0].astype(jnp.float32) for piece in held)


def summed_packed(parts):
    there, here = block_tables()
    total = yield from summed(pack(parts, there), pack(parts, here))
    shapes = [part.shape[1:] for part in parts]
    rows, wide = packed_shape(parts)
    out = []
    place = 0
    for height, width in shapes:
        if rows == height:
            out.append(total[:, place : place + width])
            place += width
        else:
            pieces = width // wide
            piece = total[place : place + pieces * height].reshape(pieces, height, wide)
            out.append(piece.transpose(1, 0, 2).reshape(height, width))
            place += pieces * height
    return out


def summed_mlp(parts, share):
    total = yield from summed(*parts)
    wide = total.shape[1]
    total = total.reshape(-1, 2, 2, share, wide)
    up = total[:, 0].transpose(2, 0, 1, 3).reshape(share, -1)
    down = total[:, 1].transpose(0, 2, 1, 3).reshape(-1, 2 * wide)
    return [up, down]


def summed_columns(sent, kept, widths):
    total = yield from summed(sent, kept)
    places = np.cumsum([0] + list(widths))
    return [total[:, low : low + width] for low, width in zip(places, widths)]


def all_sum(value):
    for bit in axis_bits("dp") + axis_bits("cols") + axis_bits("rows"):
        (arrived,) = yield [value], [flipped(value, bit)]
        value = value + arrived
    return value


def small_gather(value):
    for bit in reversed(device_bits()):
        arrived = flipped(value, bit)
        value = jnp.where(
            bit_of(bit) == 0,
            jnp.concatenate([value, arrived], axis=0),
            jnp.concatenate([arrived, value], axis=0),
        )
    return value


SWAP = [(0, 1), (1, 0)]


def split_tiles(tiles):
    col = lax.axis_index("cols")
    kept = lax.dynamic_index_in_dim(tiles, col, 0, keepdims=False)
    sent = lax.dynamic_index_in_dim(tiles, 1 - col, 0, keepdims=False)
    return kept, sent, lax.ppermute(sent, "cols", SWAP)


def join_tiles(kept, arrived):
    return jnp.where(
        lax.axis_index("cols") == 0,
        jnp.concatenate([kept, arrived], axis=1),
        jnp.concatenate([arrived, kept], axis=1),
    )


def split_image(image):
    col = lax.axis_index("cols")
    width = image.shape[1] // 2
    kept = lax.dynamic_slice_in_dim(image, col * width, width, 1)
    sent = lax.dynamic_slice_in_dim(image, (1 - col) * width, width, 1)
    return kept, sent, lax.ppermute(sent, "cols", SWAP)


def join_image(kept, arrived):
    return jnp.where(
        lax.axis_index("cols") == 0, jnp.stack([kept, arrived]), jnp.stack([arrived, kept])
    )


def halves_to_image(tiles):
    kept, _, arrived = split_tiles(tiles)
    return join_tiles(kept, arrived)


def image_to_halves(image):
    kept, _, arrived = split_image(image)
    return join_image(kept, arrived)


def column_windows(rows):
    width = rows.shape[1]
    parts = []
    for b in range(NWIN):
        piece = rows[:, b * WIN : min((b + 1) * WIN, width)]
        parts.append(jnp.pad(piece, ((0, 0), (0, SIDE - piece.shape[1]), (0, 0))))
    return jnp.stack(parts)


def column_rows(windows, width):
    parts = [windows[b, :, : min(WIN, width - b * WIN)] for b in range(len(windows))]
    return jnp.concatenate(parts, axis=1)


def pad_rows(value, top, bottom):
    widths = [(0, 0)] * value.ndim
    widths[-3] = (top, bottom)
    return jnp.pad(value, widths)


class Layout:

    def __init__(self, tiles):
        self.tiles = tiles
        _, self.height, tile_w, self.model = tiles
        self.width = 2 * tile_w
        self.count = lax.axis_size("rows")
        self.row = lax.axis_index("rows")
        self.near = self.count == NWIN - 1
        self.step = self.height - WIN
        self.halo = self.step * (self.count - 1)
        self.rest = self.height * self.count - WIN * self.count
        if self.near:
            self.slots = NWIN + 2
            self.tokens = WIN * self.width + self.rest * END
        else:
            self.slots = -(-NWIN * NWIN // self.count)
            self.tokens = 2 * self.height * tile_w

    def enter(self, tiles):
        if not self.near:
            return tiles.reshape(self.tokens, self.model)
        last, rest, halo = self.count - 1, self.rest, self.halo
        top = self.height - rest
        kept_low, sent_low, low = split_tiles(tiles[:, top:])
        (low,) = yield [sent_low], [low]
        lower = join_tiles(kept_low, low)
        kept_up, sent_up, up = split_tiles(after(tiles[:, :top], low))
        starts = end_starts(self.width, self.count)
        sent = [lower[rest - halo :]]
        arrived = [lax.ppermute(sent[0], "rows", [(i, i + 1) for i in range(last)])]
        for target in range(last):
            sent.append(lower[:, starts[target] : starts[target] + SIDE])
            arrived.append(lax.ppermute(sent[-1], "rows", [(last, target)]))
        up, down, *arrived = yield sent + [sent_up], [up] + arrived
        upper = join_tiles(kept_up, up)
        end = lower[:, starts[last] :]
        for target in range(last):
            piece = jnp.pad(arrived[target], ((0, 0), (0, END - SIDE), (0, 0)))
            end = jnp.where(self.row == target, piece, end)
        held = jnp.sum(end_place(self.width), axis=1).astype(jnp.bfloat16)
        end = end * held[None, :, None]
        whole = jnp.concatenate([down, upper, lower], axis=0)
        main = lax.dynamic_slice_in_dim(whole, halo - self.step * self.row, WIN, 0)
        return jnp.concatenate(
            [main.reshape(-1, self.model), end.reshape(-1, self.model)], axis=0
        )

    def leave(self, tokens, early):
        if not self.near:
            return tokens.reshape(self.tiles)
        last, rest, halo = self.count - 1, self.rest, self.halo
        top = self.height - rest
        width, model, step = self.width, self.model, self.step
        end = tokens[WIN * width :].reshape(rest, END, model)
        held = jnp.sum(end_place(width), axis=1).astype(jnp.bfloat16)
        end = end * held[None, :, None]
        up = tokens[: halo * width].reshape(halo, width, model)
        up = lax.ppermute(up, "rows", [(i + 1, i) for i in range(last)])
        piece = end[:, :SIDE]
        pieces = [lax.ppermute(piece, "rows", [(source, last)]) for source in range(last)]
        upper = lax.dynamic_slice_in_dim(tokens, step * self.row * width, top * width, 0)
        upper = upper.reshape(top, width, model)
        if early:
            kept_up, sent_up, arrived_up = split_image(upper)
            up, arrived_up, *pieces = yield [piece, sent_up], [up, arrived_up] + pieces
        else:
            up, *pieces = yield [piece], [up] + pieces
        tail = 0
        for start, piece in zip(end_starts(width, self.count), pieces + [end]):
            rest_wide = width - piece.shape[1] - start
            tail = tail + jnp.pad(piece, ((0, 0), (start, rest_wide), (0, 0)))
        below = jnp.where(self.row == last, tail, pad_rows(up, 0, rest - halo))
        whole = tokens[top * width : WIN * width].reshape(WIN - top, width, model)
        whole = jnp.concatenate([whole, below], axis=0)
        kept_low, sent_low, arrived_low = split_image(
            lax.dynamic_slice_in_dim(whole, step * self.row, rest, 0)
        )
        if early:
            (arrived_low,) = yield [sent_low], [arrived_low]
        else:
            kept_up, sent_up, arrived_up = split_image(upper)
            arrived_up, arrived_low = yield [sent_low, sent_up], [arrived_up, arrived_low]
        upper = join_image(kept_up, arrived_up)
        lower = join_image(kept_low, arrived_low)
        return jnp.concatenate([upper, lower], axis=1)

    def to_windows(self, tokens):
        if self.near:
            total = self.slots * TOK
            return rearranged(to_windows_kernel, tokens, self.width, self.rest, total)
        windows = column_windows(halves_to_image(tokens.reshape(self.tiles)))
        windows = lax.all_gather(windows, "rows", axis=1, tiled=True)
        extra = NWIN * WIN - windows.shape[1]
        windows = jnp.pad(windows, ((0, 0), (0, extra), (0, 0), (0, 0)))
        windows = windows.reshape(NWIN, NWIN, WIN, SIDE, self.model).transpose(1, 0, 2, 3, 4)
        windows = windows.reshape(NWIN * NWIN, WIN, SIDE, self.model)
        extra = self.slots * self.count - NWIN * NWIN
        windows = jnp.pad(windows, ((0, extra), (0, SIDE - WIN), (0, 0), (0, 0)))
        windows = lax.dynamic_slice_in_dim(windows, self.row * self.slots, self.slots, 0)
        return windows.reshape(self.slots * TOK, self.model)

    def to_rows(self, windows):
        if self.near:
            return rearranged(to_rows_kernel, windows, self.width, self.rest, self.tokens)
        windows = windows.reshape(self.slots, SIDE, SIDE, self.model)
        windows = lax.all_gather(windows[:, :WIN], "rows", axis=0, tiled=True)
        windows = windows[: NWIN * NWIN].reshape(NWIN, NWIN, WIN, SIDE, self.model)
        windows = windows.transpose(1, 0, 2, 3, 4).reshape(NWIN, NWIN * WIN, SIDE, self.model)
        windows = lax.dynamic_slice_in_dim(windows, self.row * self.height, self.height, 1)
        return image_to_halves(column_rows(windows, self.width)).reshape(self.tokens, self.model)


def shards(
    image_in,
    ln1_gain,
    ln1_bias,
    w_qkv,
    qv_bias,
    rel_rows,
    rel_cols,
    w_proj,
    proj_bias,
    ln2_gain,
    ln2_bias,
    w_fc1,
    fc1_bias,
    w_fc2,
    fc2_bias,
    cotangent,
):
    devices = lax.axis_size(ALL)
    me = lax.axis_index(ALL)
    model = image_in.shape[3]
    layout = Layout(image_in.shape)
    tokens = layout.tokens
    share = model // devices
    unit = fc1_bias.shape[0]

    rows = Flight(layout.enter(image_in))
    cot = Flight(layout.enter(cotangent))
    rows.advance()

    def gathered(shard):
        return lax.all_gather(shard, ALL, axis=0, tiled=True)

    vectors = [ln1_gain, ln1_bias, qv_bias[:, 0], qv_bias[:, 1], proj_bias, ln2_gain, ln2_bias]
    vectors = small_gather(jnp.concatenate(vectors + [fc2_bias, fc1_bias])[None])
    vectors = launch(sync(vectors, [rows]), [rows])
    w_fc1 = after(w_fc1, rows.sent)
    vectors = vectors.astype(jnp.float32)
    gain1, shift1, query_shift, value_shift, proj_shift, gain2, shift2, down_shift = (
        vectors[:, n * share : (n + 1) * share].reshape(1, model) for n in range(8)
    )
    norm_vectors = jnp.pad(jnp.concatenate([gain1, shift1], axis=0), ((0, 6), (0, 0)))
    middle_vectors = jnp.concatenate([proj_shift, gain2, shift2, down_shift], axis=0)
    middle_vectors = jnp.pad(middle_vectors, ((0, 4), (0, 0)))
    up_shift = vectors[:, 8 * share :].reshape(devices, PARTS, share)
    up_shift = up_shift.transpose(1, 0, 2).reshape(1, devices * unit)
    half = model // 2
    qkv_full = gathered(w_qkv)
    up_shard = w_fc1.reshape(share, devices, PARTS, share).transpose(0, 2, 1, 3)
    down_shard = [w_fc2[n * share : (n + 1) * share] for n in range(PARTS)]
    up_shard = up_shard.reshape(share, devices * unit)
    cut = PARTS // 2
    joint = gathered(
        jnp.concatenate([up_shard[:, : cut * model]] + down_shard[:cut] + [w_proj], axis=1)
    )
    joint2 = gathered(jnp.concatenate([up_shard[:, cut * model :]] + down_shard[cut:], axis=1))

    norm_vectors = sync(norm_vectors, [rows])
    rows = rows.finish()
    window_tokens = layout.to_windows(row_norm(rows, norm_vectors))
    shift_qkv = jnp.concatenate([query_shift, jnp.zeros((1, model), jnp.float32), value_shift], 1)
    window_tokens = launch(window_tokens, [cot])
    project = lax.dot_general(
        qkv_full, window_tokens, (((0,), (1,)), ((), ())), preferred_element_type=jnp.float32
    )
    project = (project + shift_qkv.reshape(3 * model, 1)).astype(jnp.bfloat16)
    project = sync(project, [cot])
    project = launch(project, [cot])
    tab = wide_tables(rel_rows, rel_cols)
    ind = key_indicator()
    attended_windows, weights, inverse = attention_forward(project, tab, ind)
    attended = layout.to_rows(attended_windows)
    attended, cot, joint = sync((attended, cot.finish(), joint), [])
    middle, normed2 = middle_forward(attended, joint, rows, middle_vectors)

    mixed = middle
    grad_normed2 = jnp.zeros((8, LANES), jnp.float32)
    table = place_table()
    sums = []
    shifts = []
    for first, count in ((0, 2), (2, 2)):

        def step(normed2):
            return mlp(
                normed2,
                cot,
                joint if first == 0 else joint2,
                up_shift,
                mixed,
                grad_normed2,
                down_shift,
                first,
                count,
                table,
            )

        if first:
            mixed = launch(mixed, sums)
            mixed, joint2 = sync((mixed, joint2), sums)
        mixed, grad_normed2, blocks, grad_shift = beside(sums, normed2, step)
        shifts.append(grad_shift.reshape(count, devices, share))
        if isinstance(blocks, list):
            sums.append(Flight(summed_packed(blocks)))
        else:
            sums.append(Flight(summed_mlp(blocks, share)))

    output = Flight(layout.leave(mixed, False))
    grad_normed2 = launch(grad_normed2, sums)
    grad_middle, grad_attended, grad_proj, middle_sums = sync(
        middle_backward(grad_normed2, middle, cot, attended, joint, middle_vectors), sums
    )

    def rows_of(vector):
        return vector.reshape(devices, -1)

    def attention_step(half):
        return attention_backward(project, weights, inverse, grad_windows, tab, ind, half)

    def project_step(grad_project, half):
        return token_gradient(grad_project, qkv_full, half)

    grad_windows = layout.to_windows(launch(grad_attended, sums + [output]))
    grad_project, grad_tab = sync(attention_step(0), sums[:1])
    grad_project = launch(grad_project, sums[:1])
    sent, kept, sums0 = sync(
        window_gradient(window_tokens, grad_project, [grad_proj], table), sums[1:] + [output]
    )
    sums.append(Flight(summed_columns(sent, kept, [3 * half, model])))
    grad_project = launch(grad_project, sums[1:] + [output])
    first_rows = layout.to_rows(project_step(grad_project, 0))
    first_rows, grad_windows = sync((first_rows, grad_windows), sums[:1] + sums[-1:])
    grad_windows = launch(grad_windows, sums[:1] + sums[-1:])
    grad_project, grad_part = sync(attention_step(1), sums[:-1] + [output])
    grad_project = launch(grad_project, sums[:-1])
    sent, kept, sums1 = sync(window_gradient(window_tokens, grad_project, [], table), sums)
    sums.append(Flight(summed_columns(sent, kept, [3 * half])))
    grad_project = launch(grad_project, sums)
    grad_tokens = sync(project_step(grad_project, 1), sums)
    second_rows = layout.to_rows(launch(grad_tokens, sums))
    grad_rows, norm_sums = sync(
        image_backward(rows, first_rows, second_rows, grad_middle, norm_vectors), sums
    )
    grad_in = Flight(layout.leave(grad_rows, True))
    grad_in.advance()
    norm_sums, *_ = sync([norm_sums] + grad_in.sent, sums)

    grad_sums = [jnp.sum(piece, axis=1) for piece in (sums0, sums1)]
    up_shift_sums = jnp.concatenate(shifts, axis=0).transpose(1, 0, 2).reshape(devices, unit)
    small = jnp.concatenate(
        [
            rows_of(norm_sums[0]),
            rows_of(norm_sums[1]),
            rows_of(jnp.concatenate([piece[:half] for piece in grad_sums])),
            rows_of(jnp.concatenate([piece[2 * half :] for piece in grad_sums])),
        ]
        + [rows_of(middle_sums[n]) for n in range(4)]
        + [up_shift_sums],
        axis=1,
    )
    shape = small.shape
    small = [small.reshape(-1)] + [
        table.reshape(-1) for table in narrow_tables(grad_tab + grad_part)
    ]
    small = Flight(all_sum(jnp.concatenate(small)))
    sums.append(small)

    def formatted(ups, downs):
        ups = [grad.reshape(share, -1, devices, share) for grad in ups]
        ups = jnp.concatenate(ups, axis=1).transpose(0, 2, 1, 3)
        return ups.reshape(share, devices * unit), jnp.concatenate(downs, axis=0)

    launch(grad_rows, sums)
    flat = [one.finish() for one in sums[:-3]]
    flat, output.arrived = sync((flat, output.arrived), sums)
    launch(flat, sums)
    norm_sums = sync(norm_sums, [small])
    launch(norm_sums, [small])
    grad_fc1, grad_fc2 = formatted(*zip(*flat))
    done = output.finish()
    grad_fc1, grad_fc2, done = sync((grad_fc1, grad_fc2, done), sums + [grad_in])
    launch(grad_fc1, [grad_in] + sums)
    norm_sums = sync(norm_sums, [small])
    launch(norm_sums, [small])
    first_qkv, sum_proj = sums[-3].finish()
    first_qkv, sum_proj = sync((first_qkv, sum_proj), sums + [grad_in])
    launch(first_qkv, [grad_in] + sums)
    (last_qkv,) = sums[-2].finish()
    small = small.finish()
    tables = small[shape[0] * shape[1] :].reshape(2, REL, HD)
    small = small[: shape[0] * shape[1]].reshape(shape)
    small = lax.dynamic_index_in_dim(small, me, 0, keepdims=False)
    thirds = [
        piece[:, n * half : (n + 1) * half] for n in range(3) for piece in (first_qkv, last_qkv)
    ]
    return (
        done,
        grad_in.finish().astype(jnp.float32),
        small[:share],
        small[share : 2 * share],
        jnp.concatenate(thirds, axis=1),
        jnp.stack([small[2 * share : 3 * share], small[3 * share : 4 * share]], axis=1),
        tables[0],
        tables[1],
        sum_proj,
        small[4 * share : 5 * share],
        small[5 * share : 6 * share],
        small[6 * share : 7 * share],
        grad_fc1,
        small[8 * share :],
        grad_fc2,
        small[7 * share : 8 * share],
    )


def solution(mesh):
    tile = P("dp", "rows", "cols", None)
    vector = P(ALL)
    matrix = P(ALL, None)
    in_specs = (
        tile, vector, vector, matrix, matrix, P(), P(), matrix, vector, vector, vector,
        matrix, vector, matrix, vector, tile,
    )
    out_specs = (
        tile, tile, vector, vector, matrix, matrix, P(), P(), matrix, vector, vector, vector,
        matrix, vector, matrix, vector,
    )
    return jax.shard_map(shards, mesh=mesh, in_specs=in_specs, out_specs=out_specs, check_vma=False)
```
